32 devices in a mesh: fsdp: 2 (over y), ep: 8 (over z, x), tp: 2 (over core).
Axes of the slice: x: 2, y: 2, z: 4, core: 2. Of those that a mesh axis runs over, the one named last changes fastest.
Arguments:
- tokens: bfloat16 [2048, 2048], P(('fsdp', 'ep')), may hold values from -6 to 6
- routes: int32 [2048, 8], P(('fsdp', 'ep')), may hold values from 0 to 23, all different within a row; in each aligned block of 128 rows (0 to 127, 128 to 255, ...) at most 85 rows name the same one
- places: int32 [2048], replicated, may hold values from 0 to 2047, as said below
- piece_starts: int32 [2, 2], replicated, may hold values from 0 to 768, as said below
- attn_gain: float32 [2048], replicated, may hold values from 0.5 to 1.5
- query_proj: bfloat16 [2048, 4096], P('fsdp', 'tp'), may hold values from -0.125 to 0.125
- key_matrix: bfloat16 [2048, 512], P('fsdp', 'tp'), may hold values from -0.125 to 0.125
- value_matrix: bfloat16 [2048, 512], P('fsdp', 'tp'), may hold values from -0.125 to 0.125
- out_proj: bfloat16 [2048, 4096], P('fsdp', 'tp'), may hold values from -4 to 4
- query_gain: float32 [128], replicated, may hold values from 0.1 to 1.9
- key_gain: float32 [128], replicated, may hold values from 0.1 to 1.9
- ffn_gain: float32 [2048], replicated, may hold values from 0.5 to 1.5
- router: bfloat16 [2048, 24], P('fsdp'), may hold values from -0.0625 to 0.0625
- gate_proj: bfloat16 [24, 2048, 768], P('ep', None, 'tp'), may hold values from -0.125 to 0.125
- up_proj: bfloat16 [24, 2048, 768], P('ep', None, 'tp'), may hold values from -0.125 to 0.125
- down_proj: bfloat16 [24, 768, 2048], P('ep', 'tp'), may hold values from -0.875 to 0.875
- out_grad: bfloat16 [2048, 2048], P(('fsdp', 'ep')), may hold values from -6 to 6
Outputs:
- layer_out: bfloat16 [2048, 2048], P(('fsdp', 'ep'))
- tokens_grad: float32 [2048, 2048], P(('fsdp', 'ep'))
- attn_gain_grad: float32 [2048], replicated
- query_proj_grad: float32 [2048, 4096], P('fsdp', 'tp')
- key_proj_grad: float32 [2048, 512], P('fsdp', 'tp')
- value_proj_grad: float32 [2048, 512], P('fsdp', 'tp')
- out_proj_grad: float32 [2048, 4096], P('fsdp', 'tp')
- query_gain_grad: float32 [128], replicated
- key_gain_grad: float32 [128], replicated
- ffn_gain_grad: float32 [2048], replicated
- router_grad: float32 [2048, 24], P('fsdp')
- gate_proj_grad: float32 [24, 2048, 768], P('ep', None, 'tp')
- up_proj_grad: float32 [24, 2048, 768], P('ep', None, 'tp')
- down_proj_grad: float32 [24, 768, 2048], P('ep', 'tp')
The draws below stay inside these ranges and needn't reach their ends.
Inputs may be any that keep to these rules, and one draw needn't show every extreme that they name: Rows r * 1024 to (r + 1) * 1024 - 1 hold sequence r, each of its positions once: places[t] // 1024 = t // 1024. `routes`: the rows of one device name each expert at most 85 times; some expert is named exactly 85 times by some device's rows. `piece_starts`: piece k of a sequence lies within positions k * (512) to (k + 1) * 512 - 1.
All inputs are finite; a program needn't handle non-finite values.
Results may differ from the reference program's by a relative error of at most 0.018.
Values may be sent and summed in bfloat16 or wider, within the bound.
No kernel may reach another device: no remote copies, remote signals or barrier semaphores. Data moves between devices by JAX's collectives and lax.ppermute only.
A program may use at most 320 MiB of HBM per device.

```python
import math
import jax
import jax.numpy as jnp
import numpy as np
from jax import lax

MODEL_DIM = 2048
QUERY_HEADS = 32
KEY_VALUE_HEADS = 4
HEAD_SIZE = 128
FFE = 768
TOP = 8
PIECE = 256
PIECES = 2
TOK_DEV = 128
EXPERTS = 24
SEQUENCE_LENGTH = 1024
SEQUENCE_COUNT = 2
TOKEN_TOTAL = 2048
CAP = 85
N_TP = 2


def draw_places(key, part):
    keys = jax.random.split(jax.random.fold_in(key, 7), SEQUENCE_COUNT)
    inner = jax.vmap(lambda one_key: jax.random.permutation(one_key, SEQUENCE_LENGTH))(keys).astype(jnp.int32)
    base = (jnp.arange(SEQUENCE_COUNT, dtype=jnp.int32) * SEQUENCE_LENGTH)[:, None]
    return (inner + base).reshape(TOKEN_TOTAL).astype(jnp.int32)


def draw_piece_starts(key, part):
    stretch = SEQUENCE_LENGTH // PIECES
    room = stretch - PIECE + 1
    offsets = jax.random.randint(key, (SEQUENCE_COUNT, PIECES), 0, room, dtype=jnp.int32)
    seq_rows = jnp.arange(SEQUENCE_COUNT, dtype=jnp.int32)[:, None]
    piece_cols = jnp.arange(PIECES, dtype=jnp.int32)[None, :]
    offsets = jnp.where((seq_rows == 0) & (piece_cols == 0), 0, offsets)
    offsets = jnp.where((seq_rows == 0) & (piece_cols == PIECES - 1), room - 1, offsets)
    return (piece_cols * stretch + offsets).astype(jnp.int32)


def shard_levels(stream_key, extent, shards, least, top_value):
    def one(dim, parts):
        draws = jax.random.uniform(jax.random.fold_in(jax.random.fold_in(stream_key, 6), dim), (parts,), jnp.float32, least / len(shards), top_value / len(shards))
        return jnp.repeat(jnp.exp(draws), extent[dim] // parts).reshape((-1,) + (1,) * (len(extent) - dim - 1))

    loudness = one(*shards[0])
    for cut in shards[1:]:
        loudness = loudness * one(*cut)
    return loudness


def routed_block(own_key, own, number, rows, count, top, bound, lean):
    sequence = jax.random.permutation(own_key, count)
    crowded, ordinary = portions_of(count, rows * top, bound, lean, True), portions_of(count, rows * top, bound, lean, False)
    places = jnp.arange(count)

    def named(lengths, rotation):
        used = int((lengths > 0).sum())
        fixed = max(1, used // 4)
        moved = fixed + (places - fixed + rotation * (used - fixed)) % max(1, count - fixed)
        return jnp.zeros((count,), jnp.int32).at[sequence[jnp.where(places < fixed, places, moved)]].set(jnp.asarray(lengths, jnp.int32))

    lengths = jnp.where(number % 4 == 0, named(crowded, number // 4), named(ordinary, number - number // 4 - 1))
    mixed = jax.random.permutation(jax.random.fold_in(own, 3), count)
    giver, sink = mixed[0:count // 2 * 2:2], mixed[1:count // 2 * 2:2]
    slack = jnp.minimum(lengths[giver] - 1, bound - lengths[sink]) // 2
    slack = jnp.where((giver == sequence[0]) | (sink == sequence[0]) | (lengths[sink] == 0), 0, jnp.maximum(slack, 0))
    moved = jax.random.randint(jax.random.fold_in(own, 4), (count // 2,), 0, 1 << 20) % (slack + 1)
    lengths = lengths.at[giver].add(-moved).at[sink].add(moved)
    items = jnp.searchsorted(jnp.cumsum(lengths), jnp.arange(rows * top), side="right").astype(jnp.int32)
    grid = items.reshape(top, rows).T
    grid = grid[jax.random.permutation(jax.random.fold_in(own, 1), rows)]
    rotation = jax.random.randint(jax.random.fold_in(own, 2), (rows, 1), 0, top)
    return jnp.take_along_axis(grid, (jnp.arange(top)[None, :] + rotation) % top, axis=1)


def portions_of(amount, total, reach, skew, full):
    portions = [(1 << 20) // math.isqrt(grade ** skew) + 1 for grade in range(1, amount + 1)]
    largest = reach if full else min(reach, max(-(-total // amount), total * portions[0] // sum(portions)))
    least = 1 if total - largest >= amount - 1 else 0
    holding, rest = [largest] + [least] * (amount - 1), total - largest - least * (amount - 1)
    while rest > 0:
        movable = [i for i in range(1, amount) if holding[i] < largest] or [i for i in range(1, amount) if holding[i] < reach]
        mass, left = sum([portions[i] for i in movable]), rest
        for i in movable:
            more = min(reach - holding[i], max(1, left * portions[i] // mass), rest)
            holding[i] = holding[i] + more
            rest = rest - more
    return np.array(holding)


def bell_draw(stream_key, extent, spread, limit, cuts=(), kind=jnp.bfloat16):
    array = spread * jax.random.normal(stream_key, extent, jnp.float32)
    if cuts:
        array = array * shard_levels(stream_key, extent, cuts, -0.22, 0.18)
    return jnp.clip(array, -limit, limit).astype(kind)


def setup_inputs(seed: int = 0) -> dict:
    arg_keys = jax.random.split(jax.random.key(seed), 18)
    tokens = bell_draw(arg_keys[0], (TOKEN_TOTAL, MODEL_DIM), 1.0, 6.0, ((0, 16),))
    routes_keys = jax.random.split(jax.random.fold_in(arg_keys[1], 1), TOKEN_TOTAL // TOK_DEV)
    routes_turns = jax.random.permutation(jax.random.fold_in(arg_keys[1], 3), TOKEN_TOTAL // TOK_DEV)
    routes = jax.vmap(lambda own, number: routed_block(jax.random.fold_in(arg_keys[1], 2), own, number, TOK_DEV, EXPERTS, TOP, CAP, 2))(routes_keys, routes_turns).reshape((TOKEN_TOTAL, TOP))
    places = draw_places(jax.random.fold_in(arg_keys[17], 71), 0)
    piece_starts = draw_piece_starts(jax.random.fold_in(arg_keys[17], 71), 0)
    attn_gain = jnp.clip(1.0 + 0.1 * jax.random.normal(arg_keys[4], (MODEL_DIM,), jnp.float32), 0.5, 1.5)
    query_proj = bell_draw(arg_keys[5], (MODEL_DIM, QUERY_HEADS * HEAD_SIZE), MODEL_DIM ** -0.5, 0.125, ((0, 2), (1, 2)))
    key_matrix = bell_draw(arg_keys[6], (MODEL_DIM, KEY_VALUE_HEADS * HEAD_SIZE), MODEL_DIM ** -0.5, 0.125, ((0, 2), (1, 2)))
    value_matrix = bell_draw(arg_keys[7], (MODEL_DIM, KEY_VALUE_HEADS * HEAD_SIZE), MODEL_DIM ** -0.5, 0.125, ((0, 2), (1, 2)))
    out_proj = bell_draw(arg_keys[8], (MODEL_DIM, QUERY_HEADS * HEAD_SIZE), 2 ** -0.5, 4.0, ((0, 2), (1, 2)))
    query_gain = jnp.clip(1.0 + 0.18 * jax.random.normal(arg_keys[9], (HEAD_SIZE,), jnp.float32), 0.1, 1.9)
    key_gain = jnp.clip(1.0 + 0.18 * jax.random.normal(arg_keys[10], (HEAD_SIZE,), jnp.float32), 0.1, 1.9)
    ffn_gain = jnp.clip(1.0 + 0.1 * jax.random.normal(arg_keys[11], (MODEL_DIM,), jnp.float32), 0.5, 1.5)
    router = bell_draw(arg_keys[12], (MODEL_DIM, EXPERTS), (4 * MODEL_DIM) ** -0.5, 0.0625, ((0, 2),))
    gate_proj = bell_draw(arg_keys[13], (EXPERTS, MODEL_DIM, FFE), MODEL_DIM ** -0.5, 0.125, ((0, 8), (2, 2)))
    up_proj = bell_draw(arg_keys[14], (EXPERTS, MODEL_DIM, FFE), MODEL_DIM ** -0.5, 0.125, ((0, 8), (2, 2)))
    down_proj = bell_draw(arg_keys[15], (EXPERTS, FFE, MODEL_DIM), (FFE // 16) ** -0.5, 0.875, ((0, 8), (1, 2)))
    out_grad = bell_draw(arg_keys[16], (TOKEN_TOTAL, MODEL_DIM), 1.0, 6.0, ((0, 16),))
    return {"tokens": tokens, "routes": routes, "places": places, "piece_starts": piece_starts, "attn_gain": attn_gain, "query_proj": query_proj, "key_matrix": key_matrix, "value_matrix": value_matrix, "out_proj": out_proj, "query_gain": query_gain, "key_gain": key_gain, "ffn_gain": ffn_gain, "router": router, "gate_proj": gate_proj, "up_proj": up_proj, "down_proj": down_proj, "out_grad": out_grad}


EPSILON = 1e-06
LOG_THETA = math.log(1000000.0)
MASKED_SCORE = -1e+30
EXACT_MODE = lax.Precision.HIGHEST

@jax.custom_vjp
def reduced_precision(v):
    return lax.optimization_barrier(v.astype(jnp.bfloat16)).astype(jnp.float32)

@jax.custom_vjp
def reduced_backward(v):
    return v

def low_keep(v):
    return (reduced_precision(v), None)

def low_pass(kept, grad):
    return (grad,)

def back_keep(v):
    return (v, None)

def back_low(kept, grad):
    return (reduced_precision(grad),)
reduced_precision.defvjp(low_keep, low_pass)
reduced_backward.defvjp(back_keep, back_low)

def inverse_norm(values):
    return lax.rsqrt(lax.optimization_barrier(jnp.mean(values * values, axis=-1, keepdims=True)) + EPSILON)

def rotate(vectors, angles):
    half_dim = vectors.shape[-1] // 2
    cosine = jnp.cos(angles)[:, None, :]
    sine = jnp.sin(angles)[:, None, :]
    leading = vectors[..., :half_dim]
    trailing = vectors[..., half_dim:]
    return jnp.concatenate([leading * cosine - trailing * sine, trailing * cosine + leading * sine], axis=-1)

def rotary_angles(place_ids, seq_len, head_dim):
    half_dim = head_dim // 2
    freqs = jnp.exp(jnp.arange(half_dim, dtype=jnp.float32) * (-2.0 * LOG_THETA / head_dim))
    return (place_ids % seq_len).astype(jnp.float32)[:, None] * freqs[None, :]

def piece_numbers(place_ids, piece_starts, seq_len, piece_len):
    seq_index = place_ids // seq_len
    position = place_ids % seq_len
    seq_total, piece_total = piece_starts.shape
    matches = seq_index[:, None] == jnp.arange(seq_total, dtype=jnp.int32)[None, :]
    begins = piece_starts[None, :, :]
    inside = matches[:, :, None] & (begins <= position[:, None, None]) & (position[:, None, None] < begins + piece_len)
    numbers = jnp.arange(1, piece_total + 1, dtype=jnp.int32)
    return lax.optimization_barrier(jnp.sum(jnp.where(inside, numbers[None, None, :], 0), axis=(1, 2))).astype(jnp.int32)

def forward(tokens, attn_gain, query_proj, key_matrix, value_matrix, out_proj, query_gain, key_gain, ffn_gain, router, gate_proj, up_proj, down_proj, routes, places, piece_starts):
    queries_each_key_head = QUERY_HEADS // KEY_VALUE_HEADS
    query_block_rows = min(512, SEQUENCE_LENGTH)
    blocks_each_sequence = SEQUENCE_LENGTH // query_block_rows
    normed = tokens * inverse_norm(tokens)
    attention_input = reduced_precision(normed * attn_gain)
    q_raw = reduced_backward(jnp.dot(attention_input, query_proj, precision=EXACT_MODE)).reshape(TOKEN_TOTAL, QUERY_HEADS, HEAD_SIZE)
    key_unrotated = reduced_backward(jnp.dot(attention_input, key_matrix, precision=EXACT_MODE)).reshape(TOKEN_TOTAL, KEY_VALUE_HEADS, HEAD_SIZE)
    value_reduced = reduced_precision(reduced_backward(jnp.dot(attention_input, value_matrix, precision=EXACT_MODE))).reshape(TOKEN_TOTAL, KEY_VALUE_HEADS, HEAD_SIZE)
    angles = rotary_angles(places, SEQUENCE_LENGTH, HEAD_SIZE)
    query_rotated = reduced_precision(rotate(q_raw * inverse_norm(q_raw) * query_gain, angles))
    key_rotated = reduced_precision(rotate(key_unrotated * inverse_norm(key_unrotated) * key_gain, angles))
    ordered_by_place = jnp.zeros((TOKEN_TOTAL,), jnp.int32).at[places].set(jnp.arange(TOKEN_TOTAL, dtype=jnp.int32))
    query_sequence = query_rotated[ordered_by_place].reshape(SEQUENCE_COUNT * blocks_each_sequence, query_block_rows, KEY_VALUE_HEADS, queries_each_key_head, HEAD_SIZE)
    key_sequence = key_rotated[ordered_by_place].reshape(SEQUENCE_COUNT, SEQUENCE_LENGTH, KEY_VALUE_HEADS, HEAD_SIZE)
    value_sequence = value_reduced[ordered_by_place].reshape(SEQUENCE_COUNT, SEQUENCE_LENGTH, KEY_VALUE_HEADS, HEAD_SIZE)
    piece_ids = piece_numbers(jnp.arange(TOKEN_TOTAL, dtype=jnp.int32), piece_starts, SEQUENCE_LENGTH, PIECE).reshape(SEQUENCE_COUNT, SEQUENCE_LENGTH)

    def attend(pieces_in):
        q_blk, block_index = pieces_in
        seq_index = block_index // blocks_each_sequence
        begin_pos = block_index % blocks_each_sequence * query_block_rows
        keys_here = lax.dynamic_index_in_dim(key_sequence, seq_index, 0, keepdims=False)
        values_here = lax.dynamic_index_in_dim(value_sequence, seq_index, 0, keepdims=False)
        pieces_here = lax.dynamic_index_in_dim(piece_ids, seq_index, 0, keepdims=False)
        query_pos = begin_pos + jnp.arange(query_block_rows, dtype=jnp.int32)
        key_pos = jnp.arange(SEQUENCE_LENGTH, dtype=jnp.int32)
        query_piece = lax.dynamic_slice_in_dim(pieces_here, begin_pos, query_block_rows)
        allowed = (key_pos[None, :] <= query_pos[:, None]) | (query_piece[:, None] == pieces_here[None, :]) & (query_piece[:, None] > 0)
        allowed = allowed[None, None]
        scores = reduced_backward(jnp.einsum('thgd,khd->hgtk', q_blk, keys_here, precision=EXACT_MODE) * HEAD_SIZE ** (-0.5))
        row_max = lax.optimization_barrier(jnp.max(jnp.where(allowed, scores, MASKED_SCORE), axis=-1, keepdims=True))
        weights = jnp.exp(jnp.where(allowed, scores - row_max, MASKED_SCORE))
        probabilities = reduced_precision(weights / lax.optimization_barrier(jnp.sum(weights, axis=-1, keepdims=True)))
        return jnp.einsum('hgtk,khd->thgd', probabilities, values_here, precision=EXACT_MODE)
    attn_seq = lax.map(jax.checkpoint(attend), (query_sequence, jnp.arange(SEQUENCE_COUNT * blocks_each_sequence, dtype=jnp.int32)))
    attn_low = reduced_precision(reduced_backward(attn_seq.reshape(TOKEN_TOTAL, QUERY_HEADS * HEAD_SIZE)[places]))
    residual = tokens + reduced_backward(jnp.dot(attn_low, out_proj.T, precision=EXACT_MODE))
    mid_normed = residual * inverse_norm(residual)
    ffn_in = reduced_precision(mid_normed * ffn_gain)
    logits = reduced_backward(jnp.dot(ffn_in, router, precision=EXACT_MODE))
    chosen = routes[:, :, None] == jnp.arange(EXPERTS, dtype=jnp.int32)[None, None, :]
    picked = lax.optimization_barrier(jnp.sum(jnp.where(chosen, logits[:, None, :], 0.0), axis=-1))
    gates = jax.nn.softmax(picked, axis=-1)
    weight_cols = lax.optimization_barrier(jnp.sum(jnp.where(chosen, gates[:, :, None], 0.0), axis=1))
    hidden_half = FFE // N_TP

    def expert_step(running, pieces_in):
        gate_w, up_w, down_w, weight_col = pieces_in
        gate_val = reduced_backward(jnp.dot(ffn_in, gate_w, precision=EXACT_MODE))
        up_val = reduced_backward(jnp.dot(ffn_in, up_w, precision=EXACT_MODE))
        act_low = reduced_precision(jax.nn.silu(gate_val) * up_val)
        partials = jnp.einsum('tnf,nfd->tnd', act_low.reshape(TOKEN_TOTAL, N_TP, hidden_half), down_w.reshape(N_TP, hidden_half, MODEL_DIM), precision=EXACT_MODE)
        expert_rows = reduced_backward(lax.optimization_barrier(jnp.sum(reduced_precision(partials), axis=1)))
        return (running + weight_col[:, None] * expert_rows, None)
    ffn_out, _ = lax.scan(jax.checkpoint(expert_step), jnp.zeros((TOKEN_TOTAL, MODEL_DIM), jnp.float32), (gate_proj, up_proj, down_proj, weight_cols.T))
    return residual + ffn_out

def reference(tokens, routes, places, piece_starts, attn_gain, query_proj, key_matrix, value_matrix, out_proj, query_gain, key_gain, ffn_gain, router, gate_proj, up_proj, down_proj, out_grad):
    floats = tuple((member.astype(jnp.float32) for member in (tokens, attn_gain, query_proj, key_matrix, value_matrix, out_proj, query_gain, key_gain, ffn_gain, router, gate_proj, up_proj, down_proj)))

    def layer_fn(*members):
        return forward(*members, routes, places, piece_starts)
    layer_val, pullback = jax.vjp(layer_fn, *floats)
    gradients = pullback(out_grad.astype(jnp.float32))
    return (layer_val.astype(jnp.bfloat16), gradients[0], gradients[1], gradients[2], gradients[3], gradients[4], gradients[5], gradients[6], gradients[7], gradients[8], gradients[9], gradients[10], gradients[11], gradients[12])
```

```python
import math

import jax
import jax.numpy as jnp
import numpy as np
from jax import lax
from jax.sharding import PartitionSpec as P

PIECE = 256


EPSILON = 1e-06
LOG_THETA = math.log(1000000.0)
MASKED_SCORE = -1e30
LANES = 128
BF16 = jnp.bfloat16
F32 = jnp.float32


def inverse_norm(values):
    return lax.rsqrt(jnp.mean(values * values, axis=-1, keepdims=True) + EPSILON)


def rotate(vectors, cosine, sine):
    half_dim = vectors.shape[-1] // 2
    leading = vectors[..., :half_dim]
    trailing = vectors[..., half_dim:]
    return jnp.concatenate(
        [leading * cosine - trailing * sine, trailing * cosine + leading * sine], axis=-1
    )


def norm_backward(grad_rot, unit, inverse, gain, cosine, sine):
    grad_normed = rotate(grad_rot, cosine, -sine)
    gain_part = jnp.sum(grad_normed * unit, axis=(0, 1))
    unit_grad = grad_normed * gain
    raw_grad = inverse * (unit_grad - unit * jnp.mean(unit_grad * unit, axis=-1, keepdims=True))
    return (raw_grad, gain_part)


def dot(left, right):
    return jnp.dot(left, right, preferred_element_type=F32)


def contract_rows(left, right):
    return lax.dot_general(left, right, (((0,), (0,)), ((), ())), preferred_element_type=F32)


def contract_cols(left, right):
    return lax.dot_general(left, right, (((1,), (1,)), ((), ())), preferred_element_type=F32)


class Ring:
    def __init__(self):
        self.owners = lax.axis_size("ep")
        self.groups = lax.axis_size("fsdp")
        self.index = lax.axis_index("ep")
        self.group = lax.axis_index("fsdp")
        self.half = lax.axis_index("tp")
        n = self.owners
        if n == 8:
            order = [0, 2, 4, 6, 7, 5, 3, 1] if self.groups == 2 else [0, 1, 2, 3, 7, 6, 5, 4]
        else:
            order = list(range(n))
        self.forward = [(order[i], order[(i + 1) % n]) for i in range(n)]
        self.backward = [(dst, src) for src, dst in self.forward]
        self.ahead = n // 2
        self.behind = (n - 1) // 2
        offsets = [0]
        for step in range(1, self.ahead + 1):
            offsets.append(-step)
            if step <= self.behind:
                offsets.append(step)
        self.slot = {offset: place for place, offset in enumerate(offsets)}
        self.slot[self.ahead] = self.slot[-self.ahead] if n % 2 == 0 else self.slot[self.ahead]
        table = np.zeros((n, n), np.int32)
        for position, owner in enumerate(order):
            for place, offset in enumerate(offsets):
                table[owner, place] = order[(position + offset) % n]
        self.owners_by_slot = jnp.asarray(table)[self.index]

    def send(self, values, pairs, axis="ep"):
        return lax.ppermute(values, axis, pairs)

    def swap_halves(self, values):
        return self.send(values, [(0, 1), (1, 0)], "tp")

    def swap_groups(self, values):
        return self.send(values, [(0, 1), (1, 0)], "fsdp")

    def blocks(self, own):
        ahead, behind = own, own
        found = [own]
        for step in range(1, self.ahead + 1):
            ahead = self.send(ahead, self.forward)
            found.append(ahead)
            if step <= self.behind:
                behind = self.send(behind, self.backward)
                found.append(behind)
        return found

    def gather(self, own):
        mine = jnp.concatenate(self.blocks(own), axis=0)
        return mine, jnp.concatenate([mine, self.swap_halves(mine)], axis=0)

    def scatter(self, partial):
        rows, width = partial.shape
        mine = partial[: rows // 2].astype(F32) + self.swap_halves(partial[rows // 2 :]).astype(F32)
        mine = mine.astype(BF16).reshape(self.owners, rows // 2 // self.owners, width)

        def block(offset):
            return mine[self.slot[offset]].astype(F32)

        total = block(0)
        ahead = block(self.ahead)
        for offset in range(self.ahead - 1, -1, -1):
            ahead = self.send(ahead.astype(BF16), self.forward).astype(F32)
            if offset:
                ahead = ahead + block(offset)
        if self.behind:
            behind = block(-self.behind)
            for offset in range(self.behind - 1, -1, -1):
                behind = self.send(behind.astype(BF16), self.backward).astype(F32)
                if offset:
                    behind = behind + block(-offset)
            total = total + behind
        return total + ahead

    def own_rows(self, values):
        rows = values.shape[0] // 2
        return lax.dynamic_slice_in_dim(values, self.half * rows, rows)

    def join_halves(self, own):
        other = self.swap_halves(own)
        first = self.half == 0
        return jnp.concatenate([jnp.where(first, own, other), jnp.where(first, other, own)], axis=0)

    def whole_rows(self, own):
        if self.groups == 2:
            other = self.swap_groups(own)
            first = self.group == 0
            return jnp.concatenate(
                [jnp.where(first, own, other), jnp.where(first, other, own)], axis=0
            )
        return lax.all_gather(own, "fsdp", axis=0, tiled=True)

    def share_rows(self, left, right, kind):
        share = left.shape[1] // self.groups
        if self.groups == 2:
            theirs = lax.dynamic_slice_in_dim(left, (1 - self.group) * share, share, 1)
            ours = lax.dynamic_slice_in_dim(left, self.group * share, share, 1)
            arrived = self.swap_groups(contract_rows(theirs, right).astype(kind))
            return contract_rows(ours, right) + arrived.astype(F32)
        return lax.psum_scatter(
            contract_rows(left, right), "fsdp", scatter_dimension=0, tiled=True
        )

    def other_group(self, mine):
        theirs = self.swap_groups(mine)
        return jnp.concatenate([theirs, self.swap_halves(theirs)], axis=0)

    def all_groups(self, mine):
        theirs = lax.all_gather(mine, "fsdp", axis=0)
        return jnp.concatenate([theirs, self.swap_halves(theirs)], axis=1)

    def sum_all(self, values):
        for axis in ("ep", "fsdp", "tp"):
            step = 1
            while step < lax.axis_size(axis):
                pairs = [(i, i ^ step) for i in range(lax.axis_size(axis))]
                values = values + self.send(values, pairs, axis)
                step *= 2
        return values


def pad_lanes(values):
    return jnp.pad(values, ((0, 0), (0, LANES - values.shape[1])))


def expert_terms(rows, grads, weights, gate_up, down):
    tokens_here, experts_here = weights.shape
    hidden = down.shape[0]
    each = hidden // experts_here
    both = dot(rows, gate_up)
    gate_val, up_val = both[:, :hidden], both[:, hidden:]
    back = contract_cols(grads, down)
    spread = jnp.concatenate(
        [jnp.broadcast_to(weights[:, i : i + 1], (tokens_here, each)) for i in range(experts_here)],
        axis=1,
    )
    sigmoid_val = jax.nn.sigmoid(gate_val)
    silu_val = gate_val * sigmoid_val
    act = silu_val * up_val
    act_grad = spread * back
    weighted = (spread * act).astype(BF16)
    gate_low = (act_grad * up_val * sigmoid_val * (1.0 + gate_val * (1.0 - sigmoid_val))).astype(BF16)
    up_low = (act_grad * silu_val).astype(BF16)
    products = act * back
    row_grads = [
        jnp.sum(products[:, i * each : (i + 1) * each], axis=1, keepdims=True)
        for i in range(experts_here)
    ]
    return weighted, jnp.concatenate([gate_low, up_low], axis=1), row_grads


def body(
    tokens,
    routes,
    places,
    piece_starts,
    attn_gain,
    query_proj,
    key_matrix,
    value_matrix,
    out_proj,
    query_gain,
    key_gain,
    ffn_gain,
    router,
    gate_proj,
    up_proj,
    down_proj,
    out_grad,
):
    ring = Ring()
    local_rows, width = tokens.shape
    head_dim = query_gain.shape[0]
    owners, groups = ring.owners, ring.groups
    heads_tp = query_proj.shape[1] // head_dim
    kv_tp = key_matrix.shape[1] // head_dim
    heads_here = heads_tp // owners
    heads_each_key = heads_tp // kv_tp
    sharers = heads_each_key // heads_here
    experts_here, _, each = gate_proj.shape
    expert_count = experts_here * owners
    picks = routes.shape[1]
    seq_len = local_rows * owners
    half_rows = local_rows // 2
    scale = head_dim ** (-0.5)
    e, f, t = ring.index, ring.group, ring.half
    key_head = (e * heads_here) // heads_each_key
    shared_index = e % sharers

    q_cols = heads_here * head_dim
    attn_weights = ring.whole_rows(
        jnp.concatenate(
            [
                lax.dynamic_slice_in_dim(query_proj, e * q_cols, q_cols, 1),
                lax.dynamic_slice_in_dim(key_matrix, key_head * head_dim, head_dim, 1),
                lax.dynamic_slice_in_dim(value_matrix, key_head * head_dim, head_dim, 1),
            ],
            axis=1,
        )
    )
    out_weights = ring.whole_rows(lax.dynamic_slice_in_dim(out_proj, e * q_cols, q_cols, 1))
    whole_router = ring.whole_rows(router)
    gate_up = jnp.concatenate(
        [gate_proj[i] for i in range(experts_here)] + [up_proj[i] for i in range(experts_here)],
        axis=1,
    )
    down = down_proj.reshape(experts_here * each, width)

    group_places = lax.dynamic_slice_in_dim(places, f * seq_len, seq_len)
    by_slot = jnp.take(group_places.reshape(owners, 2, half_rows), ring.owners_by_slot, axis=0)
    order_places = jnp.concatenate(
        [
            lax.dynamic_index_in_dim(by_slot, t, 1, keepdims=False).reshape(-1),
            lax.dynamic_index_in_dim(by_slot, 1 - t, 1, keepdims=False).reshape(-1),
        ]
    )
    position = order_places % seq_len
    begins = lax.dynamic_slice_in_dim(piece_starts, f, 1)
    inside = (begins <= position[:, None]) & (position[:, None] < begins + PIECE)
    numbers = jnp.arange(1, piece_starts.shape[1] + 1, dtype=jnp.int32)
    pieces = jnp.sum(jnp.where(inside, numbers[None, :], 0), axis=1)
    half_dim = head_dim // 2
    freqs = jnp.exp(jnp.arange(half_dim, dtype=F32) * (-2.0 * LOG_THETA / head_dim))
    angles = position.astype(F32)[:, None] * freqs[None, :]
    cosine, sine = jnp.cos(angles)[:, None, :], jnp.sin(angles)[:, None, :]

    stream = ring.own_rows(tokens).astype(F32)
    first_inverse = inverse_norm(stream)
    normed = stream * first_inverse
    _, attn_in = ring.gather((normed * attn_gain).astype(BF16))
    raw = dot(attn_in, attn_weights)
    q_raw = raw[:, :q_cols].reshape(seq_len, heads_here, head_dim)
    k_raw = raw[:, q_cols : q_cols + head_dim].reshape(seq_len, 1, head_dim)
    value_low = raw[:, q_cols + head_dim :].astype(BF16)
    q_inverse = inverse_norm(q_raw)
    q_unit = q_raw * q_inverse
    k_inverse = inverse_norm(k_raw)
    k_unit = k_raw * k_inverse
    query_low = rotate(q_unit * query_gain, cosine, sine).astype(BF16)
    key_low = rotate(k_unit * key_gain, cosine, sine).astype(BF16).reshape(seq_len, head_dim)
    allowed = (position[None, :] <= position[:, None]) | (
        (pieces[:, None] == pieces[None, :]) & (pieces[:, None] > 0)
    )
    scores = jnp.einsum("thd,kd->htk", query_low, key_low, preferred_element_type=F32) * scale
    scores = jnp.where(allowed[None], scores, MASKED_SCORE)
    weights = jnp.exp(scores - jnp.max(scores, axis=-1, keepdims=True))
    probs = weights / jnp.sum(weights, axis=-1, keepdims=True)
    probs_low = probs.astype(BF16)
    attn_low = (
        jnp.einsum("htk,kd->thd", probs_low, value_low, preferred_element_type=F32)
        .astype(BF16)
        .reshape(seq_len, q_cols)
    )
    residual = stream + ring.scatter(contract_cols(attn_low, out_weights).astype(BF16))

    routes_low = pad_lanes(ring.own_rows(routes).astype(BF16))
    grads_own = ring.own_rows(out_grad)
    grads_mine, grads_all = ring.gather(jnp.concatenate([grads_own, routes_low], axis=1))

    second_inverse = inverse_norm(residual)
    mid_normed = residual * second_inverse
    ffn_own = (mid_normed * ffn_gain).astype(BF16)
    ffn_mine, ffn_in = ring.gather(ffn_own)

    def gates_of(rows, routed):
        logits = dot(rows, whole_router)
        names = routed[:, width : width + picks].astype(jnp.int32)
        chosen = jnp.any(
            names[:, :, None] == jnp.arange(expert_count, dtype=jnp.int32)[None, None, :], axis=1
        )
        logits = jnp.where(chosen, logits, MASKED_SCORE)
        powers = jnp.where(chosen, jnp.exp(logits - jnp.max(logits, axis=1, keepdims=True)), 0.0)
        gates = powers / jnp.sum(powers, axis=1, keepdims=True)
        return gates, lax.dynamic_slice_in_dim(gates, e * experts_here, experts_here, 1)

    gates, gates_here = gates_of(ffn_in, grads_all)
    weighted, hidden_grads, row_grads = expert_terms(
        ffn_in, grads_all[:, :width], gates_here, gate_up, down
    )
    input_part = contract_cols(hidden_grads, gate_up).astype(BF16)
    column = lax.broadcasted_iota(jnp.int32, (1, LANES), 1)
    side = jnp.zeros((seq_len, LANES), F32)
    for i in range(experts_here):
        high = row_grads[i].astype(BF16).astype(F32)
        place = t * expert_count + e * experts_here + i
        side = side + jnp.where(column == place, high, 0.0)
        side = side + jnp.where(column == place + 2 * expert_count, row_grads[i] - high, 0.0)
    back_sum = ring.scatter(jnp.concatenate([input_part, side.astype(BF16)], axis=1))
    layer_val = residual + ring.scatter(dot(weighted, down).astype(BF16))
    layer_out = ring.join_halves(layer_val.astype(BF16))

    gate_grad_rows = sum(
        back_sum[:, width + i * expert_count : width + (i + 1) * expert_count] for i in range(4)
    )
    own_gates = gates[:half_rows]
    picked_grad = own_gates * (
        gate_grad_rows - jnp.sum(own_gates * gate_grad_rows, axis=-1, keepdims=True)
    )
    logit_grad = picked_grad.astype(BF16)
    ffn_in_grad = back_sum[:, :width] + contract_cols(logit_grad, whole_router)
    ffn_gain_part = jnp.sum(ffn_in_grad * mid_normed, axis=0)
    second_normed_grad = ffn_in_grad * ffn_gain
    mid_grad = grads_own.astype(F32) + second_inverse * (
        second_normed_grad
        - mid_normed * jnp.mean(second_normed_grad * mid_normed, axis=-1, keepdims=True)
    )
    _, branch_all = ring.gather(
        jnp.concatenate([mid_grad.astype(BF16), pad_lanes(logit_grad)], axis=1)
    )
    branch_grad = branch_all[:, :width]

    value_grad_in = dot(branch_grad, out_weights).astype(BF16).reshape(seq_len, heads_here, head_dim)
    prob_grad = jnp.einsum("thd,kd->htk", value_grad_in, value_low, preferred_element_type=F32)
    delta = jnp.sum(probs * prob_grad, axis=-1, keepdims=True)
    score_grad = (probs * (prob_grad - delta)).astype(BF16)
    q_grad = jnp.einsum("htk,kd->thd", score_grad, key_low, preferred_element_type=F32) * scale
    k_grad = jnp.einsum("htk,thd->kd", score_grad, query_low, preferred_element_type=F32) * scale
    v_grad = jnp.einsum("htk,thd->kd", probs_low, value_grad_in, preferred_element_type=F32)
    q_raw_grad, query_gain_part = norm_backward(
        q_grad, q_unit, q_inverse, query_gain, cosine, sine
    )
    k_raw_grad, key_gain_part = norm_backward(
        k_grad[:, None, :], k_unit, k_inverse, key_gain, cosine, sine
    )
    q_low = q_raw_grad.reshape(seq_len, q_cols).astype(BF16)
    kv_low = jnp.concatenate([k_raw_grad.reshape(seq_len, head_dim), v_grad], axis=1).astype(BF16)
    raw_grads = jnp.concatenate([q_low, kv_low], axis=1)
    attn_in_grad = ring.scatter(contract_cols(raw_grads, attn_weights).astype(BF16))
    first_normed_grad = attn_in_grad * attn_gain
    tokens_grad = mid_grad + first_inverse * (
        first_normed_grad - normed * jnp.mean(first_normed_grad * normed, axis=-1, keepdims=True)
    )
    tokens_grad = ring.join_halves(tokens_grad)
    attn_gain_part = jnp.sum(attn_in_grad * normed, axis=0)
    gains = ring.sum_all(
        jnp.concatenate([attn_gain_part, ffn_gain_part, query_gain_part, key_gain_part])
    )

    def columns(share):
        found = ring.blocks(share.astype(BF16))
        cols = share.shape[1]
        whole = jnp.zeros((share.shape[0], cols * owners), F32)
        for place, part in enumerate(found):
            whole = lax.dynamic_update_slice_in_dim(
                whole, part.astype(F32), ring.owners_by_slot[place] * cols, 1
            )
        return whole

    out_grad_w = columns(ring.share_rows(branch_grad, attn_low, BF16))
    query_grad_w = columns(ring.share_rows(attn_in, q_low, BF16))
    kv_share = ring.share_rows(attn_in, kv_low, BF16)
    step = sharers // 2
    while step:
        cols = kv_share.shape[1] // 2
        bit = (shared_index // step) % 2
        pairs = [(i, i ^ step) for i in range(owners)]
        sent = lax.dynamic_slice_in_dim(kv_share, (1 - bit) * cols, cols, 1)
        kept = lax.dynamic_slice_in_dim(kv_share, bit * cols, cols, 1)
        kv_share = kept + ring.send(sent.astype(BF16), pairs).astype(F32)
        step //= 2
    kv_all = columns(kv_share).reshape(-1, kv_tp, 2, head_dim)
    key_grad_w = kv_all[:, :, 0].reshape(-1, kv_tp * head_dim)
    value_grad_w = kv_all[:, :, 1].reshape(-1, kv_tp * head_dim)
    router_grad = ring.share_rows(ffn_in, branch_all[:, width : width + expert_count], F32)

    def weight_terms(rows, routed):
        _, here = gates_of(rows, routed)
        weighted, hidden_grads, _ = expert_terms(rows, routed[:, :width], here, gate_up, down)
        return contract_rows(weighted, routed[:, :width]), contract_rows(rows, hidden_grads)

    if groups == 2:
        totals = weight_terms(ring.other_group(ffn_mine), ring.other_group(grads_mine))
        down_total = totals[0] + contract_rows(weighted, grads_all[:, :width])
        gate_up_total = totals[1] + contract_rows(ffn_in, hidden_grads)
    else:
        rows_by_group, routed_by_group = ring.all_groups(ffn_mine), ring.all_groups(grads_mine)

        def add_group(i, totals):
            more = weight_terms(rows_by_group[i], routed_by_group[i])
            return totals[0] + more[0], totals[1] + more[1]

        down_total, gate_up_total = lax.fori_loop(
            0, groups, add_group, (jnp.zeros(down.shape, F32), jnp.zeros(gate_up.shape, F32))
        )
    hidden = experts_here * each
    gate_total = jnp.stack([gate_up_total[:, i * each : (i + 1) * each] for i in range(experts_here)])
    up_total = jnp.stack(
        [gate_up_total[:, hidden + i * each : hidden + (i + 1) * each] for i in range(experts_here)]
    )
    return (
        layer_out,
        tokens_grad,
        gains[:width],
        query_grad_w,
        key_grad_w,
        value_grad_w,
        out_grad_w,
        gains[2 * width : 2 * width + head_dim],
        gains[2 * width + head_dim :],
        gains[width : 2 * width],
        router_grad,
        gate_total,
        up_total,
        down_total.reshape(experts_here, each, width),
    )


def solution(mesh):
    return jax.shard_map(
        body,
        mesh=mesh,
        in_specs=(
            P(("fsdp", "ep"), None),
            P(("fsdp", "ep"), None),
            P(),
            P(),
            P(),
            P("fsdp", "tp"),
            P("fsdp", "tp"),
            P("fsdp", "tp"),
            P("fsdp", "tp"),
            P(),
            P(),
            P(),
            P("fsdp", None),
            P("ep", None, "tp"),
            P("ep", None, "tp"),
            P("ep", "tp", None),
            P(("fsdp", "ep"), None),
        ),
        out_specs=(
            P(("fsdp", "ep"), None),
            P(("fsdp", "ep"), None),
            P(),
            P("fsdp", "tp"),
            P("fsdp", "tp"),
            P("fsdp", "tp"),
            P("fsdp", "tp"),
            P(),
            P(),
            P(),
            P("fsdp", None),
            P("ep", None, "tp"),
            P("ep", None, "tp"),
            P("ep", "tp", None),
        ),
        check_vma=False,
    )
```

```python
import functools
import math

import jax
import jax.numpy as jnp
import numpy as np
from jax import lax
from jax.experimental import pallas as pl
from jax.experimental.pallas import tpu as pltpu
from jax.sharding import PartitionSpec as P

PIECE = 256


EPSILON = 1e-06
LOG_THETA = math.log(1000000.0)
MASKED_SCORE = -1e30
LANES = 128
BF16 = jnp.bfloat16
F32 = jnp.float32


def inverse_norm(values):
    return lax.rsqrt(jnp.mean(values * values, axis=-1, keepdims=True) + EPSILON)


def dot(left, right):
    return jnp.dot(left, right, preferred_element_type=F32)


def contract_rows(left, right):
    return lax.dot_general(left, right, (((0,), (0,)), ((), ())), preferred_element_type=F32)


def contract_cols(left, right):
    return lax.dot_general(left, right, (((1,), (1,)), ((), ())), preferred_element_type=F32)


class Ring:
    def __init__(self):
        self.owners = lax.axis_size("ep")
        self.groups = lax.axis_size("fsdp")
        self.index = lax.axis_index("ep")
        self.group = lax.axis_index("fsdp")
        self.half = lax.axis_index("tp")
        n = self.owners
        if n == 8:
            order = [0, 2, 4, 6, 7, 5, 3, 1] if self.groups == 2 else [0, 1, 2, 3, 7, 6, 5, 4]
        else:
            order = list(range(n))
        self.forward = [(order[i], order[(i + 1) % n]) for i in range(n)]
        self.backward = [(dst, src) for src, dst in self.forward]
        self.ahead = n // 2
        self.behind = (n - 1) // 2
        offsets = [0]
        for step in range(1, self.ahead + 1):
            offsets.append(-step)
            if step <= self.behind:
                offsets.append(step)
        self.slot = {offset: place for place, offset in enumerate(offsets)}
        self.slot[self.ahead] = self.slot[-self.ahead] if n % 2 == 0 else self.slot[self.ahead]
        table = np.zeros((n, n), np.int32)
        for position, owner in enumerate(order):
            for place, offset in enumerate(offsets):
                table[owner, place] = order[(position + offset) % n]
        self.owners_by_slot = jnp.asarray(table)[self.index]

    def send(self, values, pairs, axis="ep"):
        return lax.ppermute(values, axis, pairs)

    def swap_halves(self, values):
        return self.send(values, [(0, 1), (1, 0)], "tp")

    def swap_groups(self, values):
        return self.send(values, [(0, 1), (1, 0)], "fsdp")

    def walk(self, own, even=False):
        return Walk(self, own, even)

    def blocks(self, own, hook=None, even=False):
        walk = Walk(self, own, even)
        for step in range(self.ahead):
            done = None if hook is None else hook(step, walk)
            walk.step()
            walk.hold(done)
        return walk.found

    def gather(self, own, hook=None):
        found = self.blocks(own, hook)
        mine = jnp.concatenate(found, axis=0)
        return (mine, self.swap_halves(mine)), found

    def scatter(self, mine, other, hook=None):
        mine = mine.astype(F32) + self.swap_halves(other).astype(F32)
        mine = mine.astype(BF16).reshape(self.owners, -1, mine.shape[-1])

        def block(offset):
            return mine[self.slot[offset]].astype(F32)

        total = block(0)
        ahead = mine[self.slot[self.ahead]]
        behind = mine[self.slot[-self.behind]] if self.behind else None
        for step in range(self.ahead):
            done = None if hook is None else hook(step, ahead)
            offset = self.ahead - 1 - step
            ahead = self.send(ahead, self.forward)
            if done is not None:
                ahead = after(ahead, done)
            if offset:
                ahead = (ahead.astype(F32) + block(offset)).astype(BF16)
            offset = self.behind - 1 - step
            if offset >= 0:
                behind = self.send(behind, self.backward)
                if done is not None:
                    behind = after(behind, done)
                if offset:
                    behind = (behind.astype(F32) + block(-offset)).astype(BF16)
        if self.behind:
            total = total + behind.astype(F32)
        return total + ahead.astype(F32)

    def own_rows(self, values):
        rows = values.shape[0] // 2
        return lax.dynamic_slice_in_dim(values, self.half * rows, rows)

    def join_halves(self, own):
        other = self.swap_halves(own)
        first = self.half == 0
        return jnp.concatenate([jnp.where(first, own, other), jnp.where(first, other, own)], axis=0)

    def whole_rows(self, own):
        if self.groups == 2:
            other = self.swap_groups(own)
            first = self.group == 0
            return jnp.concatenate(
                [jnp.where(first, own, other), jnp.where(first, other, own)], axis=0
            )
        return lax.all_gather(own, "fsdp", axis=0, tiled=True)

    def send_share(self, lefts, rights, width, kind, cols=None, block=0):
        if self.groups != 2:
            return None, None
        theirs = transposed_product(lefts, rights, width // 2, 1 - self.group, kind, cols, block)
        return theirs, self.swap_groups(theirs)

    def add_share(self, arrived, lefts, rights, width, cols=None, block=0):
        if self.groups == 2:
            ours = transposed_product(lefts, rights, width // 2, self.group, F32, cols, block)
            return ours + arrived.astype(F32)
        cols = cols or rights[0].shape[1]
        whole = contract_rows(
            jnp.concatenate(lefts, axis=0)[:, :width],
            jnp.concatenate(rights, axis=0)[:, block * cols : (block + 1) * cols],
        )
        return lax.psum_scatter(whole, "fsdp", scatter_dimension=0, tiled=True)

    def all_groups(self, mine):
        theirs = lax.all_gather(mine, "fsdp", axis=0)
        return theirs, self.swap_halves(theirs)

    def sum_all(self, values):
        for axis in ("ep", "fsdp", "tp"):
            step = 1
            while step < lax.axis_size(axis):
                pairs = [(i, i ^ step) for i in range(lax.axis_size(axis))]
                values = values + self.send(values, pairs, axis)
                step *= 2
        return values


def after(values, signal):
    return lax.optimization_barrier((values, signal))[0]


class Walk:
    def __init__(self, ring, own, even):
        self.ring, self.ahead, self.behind, self.even = ring, own, own, even
        self.found, self.count = [own], 0

    def hold(self, done):
        if done is not None:
            self.ahead, self.behind, self.found[-1] = after(
                (self.ahead, self.behind, self.found[-1]), done
            )

    def step(self, signal=None):
        ring = self.ring
        self.count += 1
        if signal is not None:
            self.ahead, self.behind = after((self.ahead, self.behind), signal)
        if self.count > ring.behind and self.even and ring.behind:
            cut = self.ahead.shape[0] // 2
            self.found.append(
                (
                    ring.send(self.ahead[:cut], ring.forward),
                    ring.send(self.behind[cut:], ring.backward),
                )
            )
            return
        self.ahead = ring.send(self.ahead, ring.forward)
        self.found.append(self.ahead)
        if self.count <= ring.behind:
            self.behind = ring.send(self.behind, ring.backward)
            self.found.append(self.behind)


def pad_lanes(values):
    return jnp.pad(values, ((0, 0), (0, LANES - values.shape[1])))


VMEM = pltpu.VMEM
SMEM = pltpu.SMEM
ROW_BLOCK = 256


def call(kernel, micros, **kwargs):
    return pl.pallas_call(
        kernel,
        compiler_params=pltpu.CompilerParams(vmem_limit_bytes=56 * 1024 * 1024),
        cost_estimate=pl.CostEstimate(
            flops=int(micros * 1.15e9), bytes_accessed=0, transcendentals=0
        ),
        **kwargs,
    )


def whole_spec():
    return pl.BlockSpec(memory_space=VMEM)


def turned(values):
    return pltpu.roll(values, values.shape[-1] // 2, 1)


def row_blocks(mine, other, step=ROW_BLOCK):
    half = mine.shape[0]
    for place, ref in enumerate((mine, other)):
        for start in range(0, half, step):
            yield ref, start, place * half + start


def cut_kernel(e_ref, q_ref, k_ref, v_ref, o_ref, out_ref):
    cols, dim = q_ref.shape[1], k_ref.shape[1]
    out_ref[:, :cols] = q_ref[...]
    out_ref[:, cols : cols + dim] = k_ref[...]
    out_ref[:, cols + dim : cols + 2 * dim] = v_ref[...]
    out_ref[:, cols + 2 * dim :] = o_ref[...]


def cut_weights(device, key_head, query_proj, key_matrix, value_matrix, out_proj, cols, dim):
    rows = query_proj.shape[0]
    heads = pl.BlockSpec((rows, cols), lambda i, e: (0, e[0]))
    key = pl.BlockSpec((rows, dim), lambda i, e: (0, e[1]))
    return call(
        cut_kernel,
        3,
        grid_spec=pltpu.PrefetchScalarGridSpec(
            num_scalar_prefetch=1,
            grid=(1,),
            in_specs=[heads, key, key, heads],
            out_specs=pl.BlockSpec((rows, 2 * cols + 2 * dim), lambda i, e: (0, 0)),
        ),
        out_shape=jax.ShapeDtypeStruct((rows, 2 * cols + 2 * dim), BF16),
    )(jnp.stack([device, key_head]).astype(jnp.int32), query_proj, key_matrix, value_matrix, out_proj)


def spots(at_ref, w_refs):
    rows = w_refs[0].shape[0]
    return [(pl.ds(pl.multiple_of(at_ref[i] * rows, rows), rows), ref) for i, ref in enumerate(w_refs)]


def project_kernel(
    heads, parts, at_ref, xm_ref, xo_ref, cos_ref, sin_ref, qg_ref, kg_ref, *refs
):
    w_refs, (raw_ref, ql_ref, kl_ref, vl_ref) = refs[:parts], refs[parts:]
    dim = qg_ref.shape[1]
    cols = heads * dim
    for ref, start, row in row_blocks(xm_ref, xo_ref):
        rows = slice(row, row + ROW_BLOCK)
        raw = sum(
            dot(ref[start : start + ROW_BLOCK, spot], w_ref[:, : cols + 2 * dim])
            for spot, w_ref in spots(at_ref, w_refs)
        )
        raw_ref[rows, :] = raw[:, : cols + dim]
        cosine, sine = cos_ref[rows, :], sin_ref[rows, :]
        for head in range(heads + 1):
            part = raw[:, head * dim : (head + 1) * dim]
            gain = qg_ref[...] if head < heads else kg_ref[...]
            part = part * inverse_norm(part) * gain
            part = (part * cosine + turned(part) * sine).astype(BF16)
            if head < heads:
                ql_ref[rows, head * dim : (head + 1) * dim] = part
            else:
                kl_ref[rows, :] = part
        vl_ref[rows, :] = raw[:, cols + dim :].astype(BF16)


def smem_spec():
    return pl.BlockSpec(memory_space=SMEM)


def project(at, x, weights, heads, cosine, sine, q_gain, k_gain):
    rows, dim = 2 * x[0].shape[0], q_gain.shape[1]
    cols = heads * dim
    return call(
        functools.partial(project_kernel, heads, len(weights)),
        7,
        in_specs=[smem_spec()] + [whole_spec()] * (6 + len(weights)),
        out_specs=[whole_spec()] * 4,
        out_shape=[
            jax.ShapeDtypeStruct((rows, cols + dim), F32),
            jax.ShapeDtypeStruct((rows, cols), BF16),
            jax.ShapeDtypeStruct((rows, dim), BF16),
            jax.ShapeDtypeStruct((rows, dim), BF16),
        ],
    )(at, *x, cosine, sine, q_gain, k_gain, *weights)


def attend_kernel(heads, base, parts, at_ref, pos_ref, lim_ref, ql_ref, kl_ref, vl_ref, *refs):
    w_refs, (out_ref, lse_ref, part_ref) = refs[:parts], refs[parts:]
    dim = kl_ref.shape[1]
    cols = heads * dim
    scale = dim ** (-0.5)
    for row in range(0, out_ref.shape[0], ROW_BLOCK):
        rows, among = slice(row, row + ROW_BLOCK), slice(base + row, base + row + ROW_BLOCK)
        allowed = pos_ref[...] <= lim_ref[among, :]
        for head in range(heads):
            cut = slice(head * dim, (head + 1) * dim)
            scores = contract_cols(ql_ref[among, cut], kl_ref[...]) * scale
            scores = jnp.where(allowed, scores, MASKED_SCORE)
            top = jnp.max(scores, axis=1, keepdims=True)
            powers = jnp.exp(scores - top)
            total = jnp.sum(powers, axis=1, keepdims=True)
            lse_ref[head, rows, :] = top + jnp.log(total)
            probs = (powers * (1.0 / total)).astype(BF16)
            out_ref[rows, cut] = dot(probs, vl_ref[...]).astype(BF16)
        for spot, w_ref in spots(at_ref, w_refs):
            part_ref[rows, spot] = contract_cols(
                out_ref[rows, :], w_ref[:, cols + 2 * dim :]
            ).astype(BF16)


def attend(at, place, weights, position, limit, query, key, value):
    rows, dim = key.shape
    cols = query.shape[1]
    half, width = rows // 2, sum(w.shape[0] for w in weights)
    heads = cols // dim
    return call(
        functools.partial(attend_kernel, heads, place * half, len(weights)),
        6.5,
        in_specs=[smem_spec()] + [whole_spec()] * (5 + len(weights)),
        out_specs=[whole_spec()] * 3,
        out_shape=[
            jax.ShapeDtypeStruct((half, cols), BF16),
            jax.ShapeDtypeStruct((heads, half, 1), F32),
            jax.ShapeDtypeStruct((half, width), BF16),
        ],
    )(at, position, limit, query, key, value, *weights)


def attend_back_kernel(
    heads,
    parts,
    at_ref,
    bm_ref,
    bo_ref,
    cos_ref,
    sin_ref,
    qg_ref,
    kg_ref,
    pos_ref,
    lim_ref,
    raw_ref,
    ql_ref,
    kl_ref,
    vl_ref,
    lm_ref,
    lo_ref,
    *refs,
):
    w_refs, refs = refs[:parts], refs[parts:]
    layer_refs, (rm_ref, ro_ref, gains_ref, pm_ref, po_ref, dk_ref, dv_ref) = refs[:-7], refs[-7:]
    dim = qg_ref.shape[1]
    cols = heads * dim
    scale = dim ** (-0.5)
    q_part = jnp.zeros((1, dim), F32)
    k_part = jnp.zeros((1, dim), F32)

    def norm_back(grad, rows, raw, gain):
        inverse = inverse_norm(raw)
        unit = raw * inverse
        grad = grad * cos_ref[rows, :] - turned(grad) * sin_ref[rows, :]
        part = jnp.sum(grad * unit, axis=0, keepdims=True)
        grad = grad * gain
        return inverse * (grad - unit * jnp.mean(grad * unit, axis=1, keepdims=True)), part

    first = True
    for (ref, start, row), lse_ref, rg_ref in zip(
        row_blocks(bm_ref, bo_ref), (lm_ref, lm_ref, lo_ref, lo_ref), (rm_ref, rm_ref, ro_ref, ro_ref)
    ):
        rows, here = slice(row, row + ROW_BLOCK), slice(start, start + ROW_BLOCK)
        grads = sum(
            dot(ref[here, spot], w_ref[:, cols + 2 * dim :]) for spot, w_ref in spots(at_ref, w_refs)
        ).astype(BF16)
        allowed = pos_ref[...] <= lim_ref[rows, :]
        for head in range(heads):
            cut = slice(head * dim, (head + 1) * dim)
            query, value_grad = ql_ref[rows, cut], grads[:, cut]
            scores = contract_cols(query, kl_ref[...]) * scale
            probs = jnp.exp(jnp.where(allowed, scores - lse_ref[head, here, :], MASKED_SCORE))
            prob_grad = contract_cols(value_grad, vl_ref[...])
            weighed = probs * prob_grad
            delta = jnp.sum(weighed, axis=1, keepdims=True)
            score_grad = (weighed - probs * delta).astype(BF16)
            q_grad = dot(score_grad, kl_ref[...]) * scale
            k_more = contract_rows(query, score_grad)
            v_more = contract_rows(value_grad, probs.astype(BF16))
            if first:
                dk_ref[...] = k_more
                dv_ref[...] = v_more
                first = False
            else:
                dk_ref[...] += k_more
                dv_ref[...] += v_more
            q_raw_grad, part = norm_back(q_grad, rows, raw_ref[rows, cut], qg_ref[...])
            q_part = q_part + part
            rg_ref[here, cut] = q_raw_grad.astype(BF16)
    own = pm_ref.shape[1] // 2
    for out_ref, part_refs in (
        (pm_ref, layer_refs[: len(layer_refs) // 2]),
        (po_ref, layer_refs[len(layer_refs) // 2 :]),
    ):
        block = 0
        for part_ref in part_refs:
            for start in range(0, part_ref.shape[0], own):
                out_ref[block, own:, :] = part_ref[start : start + own, :]
                block += 1
    for (_, start, row), rg_ref, ref in zip(
        row_blocks(bm_ref, bo_ref),
        (rm_ref, rm_ref, ro_ref, ro_ref),
        (pm_ref, pm_ref, po_ref, po_ref),
    ):
        rows, here = slice(row, row + ROW_BLOCK), slice(start, start + ROW_BLOCK)
        k_grad = dk_ref[:, rows].T * scale
        k_raw_grad, part = norm_back(k_grad, rows, raw_ref[rows, cols : cols + dim], kg_ref[...])
        k_part = k_part + part
        rg_ref[here, cols : cols + dim] = k_raw_grad.astype(BF16)
        rg_ref[here, cols + dim :] = dv_ref[:, rows].T.astype(BF16)
        for spot, w_ref in spots(at_ref, w_refs):
            part = contract_cols(rg_ref[here, :], w_ref[:, : cols + 2 * dim]).astype(BF16)
            for i in range(ROW_BLOCK // own):
                ref[start // own + i, :own, spot] = part[i * own : (i + 1) * own, :]
    gains_ref[0:1, :] = q_part
    gains_ref[1:2, :] = k_part


def attend_back(
    at, branch, weights, layer, own, cosine, sine, q_gain, k_gain, position, limit, saved
):
    half = branch[0].shape[0]
    dim = q_gain.shape[1]
    width = sum(w.shape[0] for w in weights)
    cols = saved[1].shape[1]
    raw_half = jax.ShapeDtypeStruct((half, cols + 2 * dim), BF16)
    return call(
        functools.partial(attend_back_kernel, cols // dim, len(weights)),
        18.5,
        in_specs=[smem_spec()] + [whole_spec()] * (14 + len(weights) + len(layer)),
        out_specs=[whole_spec()] * 5,
        out_shape=[
            raw_half,
            raw_half,
            jax.ShapeDtypeStruct((2, dim), F32),
            jax.ShapeDtypeStruct((half // own, 2 * own, width), BF16),
            jax.ShapeDtypeStruct((half // own, 2 * own, width), BF16),
        ],
        scratch_shapes=[VMEM((dim, 2 * half), F32), VMEM((dim, 2 * half), F32)],
    )(at, *branch, cosine, sine, q_gain, k_gain, position, limit, *saved, *weights, *layer)


def routed_gates(x_ref, g_ref, router_ref, picks):
    lane = lax.broadcasted_iota(jnp.int32, (1, LANES), 1).astype(F32)
    logits = dot(x_ref[...], router_ref[...])
    names = g_ref[:, x_ref.shape[1] :].astype(F32)
    chosen = jnp.zeros(logits.shape, F32)
    for k in range(picks):
        chosen = jnp.where(names[:, k : k + 1] == lane, 1.0, chosen)
    logits = jnp.where(chosen > 0.0, logits, MASKED_SCORE)
    powers = chosen * jnp.exp(logits - jnp.max(logits, axis=1, keepdims=True))
    return powers / jnp.sum(powers, axis=1, keepdims=True)


def expert_values(x, g, gates, name, gate_up, down):
    each = down.shape[0]
    lane = lax.broadcasted_iota(jnp.int32, (1, LANES), 1)
    both = dot(x, gate_up)
    gate_val, up_val = both[:, :each], both[:, each:]
    grad = contract_cols(g, down)
    gate = jnp.sum(jnp.where(lane == name, gates, 0.0), axis=1, keepdims=True)
    sigmoid_val = 0.5 * jnp.tanh(0.5 * gate_val) + 0.5
    silu_val = gate_val * sigmoid_val
    act = silu_val * up_val
    act_grad = gate * grad
    gate_low = (act_grad * up_val * (sigmoid_val + silu_val * (1.0 - sigmoid_val))).astype(BF16)
    up_low = (act_grad * silu_val).astype(BF16)
    return (gate * act).astype(BF16), gate_low, up_low, act * grad


def experts_kernel(
    picks,
    expert_count,
    first_ref,
    xm_ref,
    xo_ref,
    gm_ref,
    go_ref,
    wg_ref,
    wu_ref,
    wd_ref,
    router_ref,
    weighted_ref,
    hidden_ref,
    gates_ref,
    pm_ref,
    po_ref,
    both_ref,
    side_ref,
):
    expert = pl.program_id(0)
    wide, width = xm_ref.shape
    each = wg_ref.shape[2]
    lane = lax.broadcasted_iota(jnp.int32, (1, LANES), 1)
    halves = ((xm_ref, gm_ref, pm_ref, 0), (xo_ref, go_ref, po_ref, wide))

    @pl.when(expert == 0)
    def _():
        for x_ref, g_ref, _, row in halves:
            gates_ref[row : row + wide, :] = routed_gates(x_ref, g_ref, router_ref, picks)

    name = first_ref[0] + expert
    place = first_ref[1] + name
    at = pl.multiple_of(expert * 2 * each, 2 * each)
    both_ref[:, pl.ds(at, each)] = wg_ref[0]
    both_ref[:, pl.ds(at + each, each)] = wu_ref[0]
    for x_ref, g_ref, _, row in halves:
        rows = slice(row, row + wide)
        weighted, gate_low, up_low, products = expert_values(
            x_ref[...],
            g_ref[:, :width],
            gates_ref[rows, :],
            name,
            both_ref[:, pl.ds(at, 2 * each)],
            wd_ref[0],
        )
        weighted_ref[rows, :] = weighted
        hidden_ref[rows, pl.ds(at, each)] = gate_low
        hidden_ref[rows, pl.ds(at + each, each)] = up_low
        row_grad = jnp.sum(products, axis=1, keepdims=True)
        high = row_grad.astype(BF16).astype(F32)
        side = jnp.where(lane == place, high, 0.0)
        side = side + jnp.where(lane == place + 2 * expert_count, row_grad - high, 0.0)
        side_ref[rows, :] = jnp.where(expert == 0, side, side_ref[rows, :] + side)

    @pl.when(expert == pl.num_programs(0) - 1)
    def _():
        for _, _, ref, row in halves:
            rows = slice(row, row + wide)
            ref[:, :width] = contract_cols(hidden_ref[rows, :], both_ref[...]).astype(BF16)
            ref[:, width:] = side_ref[rows, :].astype(BF16)


def experts(first, x, g, gate_proj, up_proj, down_proj, router, picks, expert_count):
    half, width = x[0].shape
    rows = 2 * half
    count, _, each = gate_proj.shape
    resident = lambda shape: pl.BlockSpec(
        shape, lambda i, first: (0,) * len(shape), pipeline_mode=pl.Buffered(1)
    )
    payload = (half, width + LANES)
    return call(
        functools.partial(experts_kernel, picks, expert_count),
        41,
        grid_spec=pltpu.PrefetchScalarGridSpec(
            num_scalar_prefetch=1,
            grid=(count,),
            in_specs=[resident((half, width))] * 2
            + [resident(payload)] * 2
            + [pl.BlockSpec((1, width, each), lambda i, first: (i, 0, 0))] * 2
            + [
                pl.BlockSpec((1, each, width), lambda i, first: (i, 0, 0)),
                resident((width, LANES)),
            ],
            out_specs=[
                pl.BlockSpec((rows, each), lambda i, first: (0, i)),
                resident((rows, 2 * count * each)),
                resident((rows, LANES)),
                resident(payload),
                resident(payload),
            ],
            scratch_shapes=[VMEM((width, 2 * count * each), BF16), VMEM((rows, LANES), F32)],
        ),
        out_shape=[
            jax.ShapeDtypeStruct((rows, count * each), BF16),
            jax.ShapeDtypeStruct((rows, 2 * count * each), BF16),
            jax.ShapeDtypeStruct((rows, LANES), F32),
            jax.ShapeDtypeStruct(payload, BF16),
            jax.ShapeDtypeStruct(payload, BF16),
        ],
    )(first, x[0], x[1], g[0], g[1], gate_proj, up_proj, down_proj, router)


def transposed_product_kernel(side_ref, am_ref, ao_ref, bm_ref, bo_ref, out_ref):
    total = contract_rows(am_ref[...], bm_ref[...]) + contract_rows(ao_ref[...], bo_ref[...])
    out_ref[...] = total.astype(out_ref.dtype)


def transposed_product(lefts, rights, share, side, kind, cols=None, block=0):
    half = rights[0].shape[0]
    cols = cols or rights[0].shape[1]
    left = pl.BlockSpec((half, share), lambda i, side: (0, side[0]))
    return call(
        transposed_product_kernel,
        4,
        grid_spec=pltpu.PrefetchScalarGridSpec(
            num_scalar_prefetch=1,
            grid=(1,),
            in_specs=[left, left] + [pl.BlockSpec((half, cols), lambda i, side: (0, block))] * 2,
            out_specs=pl.BlockSpec((share, cols), lambda i, side: (0, 0)),
        ),
        out_shape=jax.ShapeDtypeStruct((share, cols), kind),
    )(side.reshape(1).astype(jnp.int32), *lefts, *rights)


def layer_kernel(w_ref, d_ref, out_ref):
    out_ref[...] = dot(w_ref[...], d_ref[...]).astype(BF16)


def layer_part(part, parts, weighted, down):
    rows, hidden = weighted.shape
    width = down.shape[1]
    return call(
        layer_kernel,
        4,
        grid=(1,),
        in_specs=[
            pl.BlockSpec((rows // parts, hidden), lambda i: (part, 0)),
            pl.BlockSpec((hidden, width), lambda i: (0, 0)),
        ],
        out_specs=pl.BlockSpec((rows // parts, width), lambda i: (0, 0)),
        out_shape=jax.ShapeDtypeStruct((rows // parts, width), BF16),
    )(weighted, down)


def other_experts_kernel(
    picks, first_ref, x_ref, g_ref, wg_ref, wu_ref, wd_ref, router_ref, w_ref, h_ref, gates_ref
):
    expert = pl.program_id(0)
    width = x_ref.shape[1]
    each = wg_ref.shape[2]

    @pl.when(expert == 0)
    def _():
        gates_ref[...] = routed_gates(x_ref, g_ref, router_ref, picks)

    w_ref[...], h_ref[:, :each], h_ref[:, each:], _ = expert_values(
        x_ref[...],
        g_ref[:, :width],
        gates_ref[...],
        first_ref[0] + expert,
        jnp.concatenate([wg_ref[0], wu_ref[0]], axis=1),
        wd_ref[0],
    )


def other_experts(first, x, g, gate_proj, up_proj, down_proj, router, picks):
    rows, width = x.shape
    count, _, each = gate_proj.shape
    resident = lambda shape: pl.BlockSpec(
        shape, lambda i, first: (0,) * len(shape), pipeline_mode=pl.Buffered(1)
    )
    return call(
        functools.partial(other_experts_kernel, picks),
        14,
        grid_spec=pltpu.PrefetchScalarGridSpec(
            num_scalar_prefetch=1,
            grid=(count,),
            in_specs=[resident(x.shape), resident(g.shape)]
            + [pl.BlockSpec((1, width, each), lambda i, first: (i, 0, 0))] * 2
            + [
                pl.BlockSpec((1, each, width), lambda i, first: (i, 0, 0)),
                resident(router.shape),
            ],
            out_specs=[
                pl.BlockSpec((rows, each), lambda i, first: (0, i)),
                pl.BlockSpec((rows, 2 * each), lambda i, first: (0, i)),
            ],
            scratch_shapes=[VMEM((rows, LANES), F32)],
        ),
        out_shape=[
            jax.ShapeDtypeStruct((rows, count * each), BF16),
            jax.ShapeDtypeStruct((rows, 2 * count * each), BF16),
        ],
    )(first, x, g, gate_proj, up_proj, down_proj, router)


def in_halves(values, block, index):
    if isinstance(values, (tuple, list)):
        places = (0, 0)
    else:
        values, places = (values, values), (0, 1)
    specs = [
        pl.BlockSpec(block, lambda i, place=place: (place, index), pipeline_mode=pl.Buffered(1))
        for place in places
    ]
    return list(values), specs


def sign(token_ref):
    token_ref[...] = jnp.zeros(token_ref.shape, token_ref.dtype)


TOKEN = (8, LANES)


def gate_up_grad_kernel(x0, x1, x2, x3, d0, d1, d2, d3, *refs):
    gate_ref, up_ref, token_ref = refs[-3:]
    each = gate_ref.shape[2]
    total = (contract_rows(x0[...], d0[...]) + contract_rows(x1[...], d1[...])) + (
        contract_rows(x2[...], d2[...]) + contract_rows(x3[...], d3[...])
    )
    gate_ref[0] = total[:, :each]
    up_ref[0] = total[:, each:]
    sign(token_ref)


def gate_up_grad(expert, count, totals, own, other, own_hidden, other_hidden):
    half, width = own[0].shape
    each = own_hidden.shape[1] // 2 // count
    wide = 2 * ROW_BLOCK
    left = pl.BlockSpec((half, wide), lambda i: (0, i))
    part = pl.BlockSpec((1, wide, each), lambda i: (expert, i, 0))
    rights, specs = in_halves(own_hidden, (half, 2 * each), expert)
    more, more_specs = in_halves(other_hidden, (half, 2 * each), expert)
    return call(
        gate_up_grad_kernel,
        11.7,
        grid=(width // wide,),
        in_specs=[left] * 4
        + specs
        + more_specs
        + [pl.BlockSpec(memory_space=pl.ANY)] * len(totals),
        out_specs=[part] * 2 + [pl.BlockSpec(TOKEN, lambda i: (0, 0))],
        out_shape=[jax.ShapeDtypeStruct((count, width, each), F32)] * 2
        + [jax.ShapeDtypeStruct(TOKEN, F32)],
        input_output_aliases={8: 0, 9: 1} if totals else {},
    )(*own, *other, *rights, *more, *totals)


def down_grad_kernel(count, w0, w1, w2, w3, g0, g1, g2, g3, *refs):
    out_ref, token_ref = refs[-2:]
    each = out_ref.shape[1]
    total = (contract_rows(w0[...], g0[...]) + contract_rows(w1[...], g1[...])) + (
        contract_rows(w2[...], g2[...]) + contract_rows(w3[...], g3[...])
    )
    for i in range(count):
        out_ref[i] = total[i * each : (i + 1) * each, :]
    sign(token_ref)


def down_grad(part, parts, count, totals, own_weighted, other_weighted, own, other):
    half, width = own[0].shape[0], own[0].shape[1] - LANES
    hidden = own_weighted.shape[1]
    each = hidden // count
    wide = 2 * ROW_BLOCK
    steps = width // wide // parts
    right = pl.BlockSpec((half, wide), lambda i: (0, part * steps + i))
    place = pl.BlockSpec((count, each, wide), lambda i: (0, 0, part * steps + i))
    lefts, specs = in_halves(own_weighted, (half, hidden), 0)
    more, more_specs = in_halves(other_weighted, (half, hidden), 0)
    return call(
        functools.partial(down_grad_kernel, count),
        9.7,
        grid=(steps,),
        in_specs=specs
        + more_specs
        + [right] * 4
        + [pl.BlockSpec(memory_space=pl.ANY)] * len(totals),
        out_specs=[place, pl.BlockSpec(TOKEN, lambda i: (0, 0))],
        out_shape=[
            jax.ShapeDtypeStruct((count, each, width), F32),
            jax.ShapeDtypeStruct(TOKEN, F32),
        ],
        input_output_aliases={8: 0} if totals else {},
    )(*lefts, *more, *own, *other, *totals)


def join_kernel(*refs):
    out_ref = refs[-1]
    own = refs[0].shape[0]
    for i, ref in enumerate(refs[:-1]):
        out_ref[i * own : (i + 1) * own, :] = ref[...]


def join_rows(blocks):
    own, width = blocks[0].shape
    return call(
        join_kernel,
        2,
        in_specs=[whole_spec()] * len(blocks),
        out_specs=whole_spec(),
        out_shape=jax.ShapeDtypeStruct((own * len(blocks), width), blocks[0].dtype),
    )(*blocks)


def place_wide_kernel(owners_ref, *refs):
    blocks, out_ref = refs[:-1], refs[-1]
    cols = blocks[0].shape[1]
    start = 0
    slot = 0
    for ref in blocks:
        rows = ref.shape[0]
        at = pl.multiple_of(owners_ref[slot] * cols, cols)
        out_ref[start : start + rows, pl.ds(at, cols)] = ref[...].astype(F32)
        start += rows
        if start == out_ref.shape[0]:
            start, slot = 0, slot + 1


def place_wide(owners_by_slot, blocks, width):
    share = blocks[0].shape[0]
    return call(
        place_wide_kernel,
        6,
        in_specs=[smem_spec()] + [whole_spec()] * len(blocks),
        out_specs=whole_spec(),
        out_shape=jax.ShapeDtypeStruct((share, width), F32),
    )(owners_by_slot, *blocks)


def place_kernel(sharers, owners_ref, *refs):
    blocks, (q_ref, k_ref, v_ref) = refs[:-3], refs[-3:]
    share = q_ref.shape[0]
    cols = blocks[0].shape[1]
    dim = cols // 2
    rows = blocks[0].shape[0] - share
    for i, ref in enumerate(blocks):
        owner = owners_ref[i]
        at = pl.multiple_of(owner * cols, cols)
        q_ref[:, pl.ds(at, cols)] = ref[:share, :].astype(F32)
        down = pl.multiple_of(owner % sharers * rows, rows)
        right = pl.multiple_of(owner // sharers * dim, dim)
        k_ref[pl.ds(down, rows), pl.ds(right, dim)] = ref[share:, :dim].astype(F32)
        v_ref[pl.ds(down, rows), pl.ds(right, dim)] = ref[share:, dim:].astype(F32)


def place_blocks(owners_by_slot, blocks, shapes, sharers):
    return call(
        functools.partial(place_kernel, sharers),
        7,
        in_specs=[pl.BlockSpec(memory_space=SMEM)] + [whole_spec()] * len(blocks),
        out_specs=[whole_spec()] * 3,
        out_shape=[jax.ShapeDtypeStruct(shape, F32) for shape in shapes],
    )(owners_by_slot, *blocks)


def place_last_kernel(share, owner_ref, top_in, low_in, q_any, k_any, v_any, q_ref, k_ref, v_ref):
    dim = k_ref.shape[1]
    cut = top_in.shape[0]
    q_ref[:cut, :] = top_in[...].astype(F32)
    q_ref[cut:, :] = low_in[: share - cut, :].astype(F32)
    k_ref[...] = low_in[share - cut :, :dim].astype(F32)
    v_ref[...] = low_in[share - cut :, dim:].astype(F32)


def place_last(owner, halves, totals, sharers):
    share = totals[0].shape[0]
    top, low = halves
    cols = top.shape[1]
    rows = top.shape[0] + low.shape[0] - share
    spots = pl.BlockSpec((rows, cols // 2), lambda i, o: (o[0] % sharers, o[0] // sharers))
    return call(
        functools.partial(place_last_kernel, share),
        3,
        grid_spec=pltpu.PrefetchScalarGridSpec(
            num_scalar_prefetch=1,
            grid=(1,),
            in_specs=[
                pl.BlockSpec(top.shape, lambda i, o: (0, 0)),
                pl.BlockSpec(low.shape, lambda i, o: (0, 0)),
            ]
            + [pl.BlockSpec(memory_space=pl.ANY)] * 3,
            out_specs=[pl.BlockSpec((share, cols), lambda i, o: (0, o[0])), spots, spots],
        ),
        out_shape=[jax.ShapeDtypeStruct(total.shape, F32) for total in totals],
        input_output_aliases={3: 0, 4: 1, 5: 2},
    )(owner.reshape(1), top, low, *totals)


def body(
    tokens,
    routes,
    places,
    piece_starts,
    attn_gain,
    query_proj,
    key_matrix,
    value_matrix,
    out_proj,
    query_gain,
    key_gain,
    ffn_gain,
    router,
    gate_proj,
    up_proj,
    down_proj,
    out_grad,
):
    ring = Ring()
    local_rows, width = tokens.shape
    head_dim = query_gain.shape[0]
    owners, groups = ring.owners, ring.groups
    heads_tp = query_proj.shape[1] // head_dim
    kv_tp = key_matrix.shape[1] // head_dim
    heads_here = heads_tp // owners
    heads_each_key = heads_tp // kv_tp
    sharers = heads_each_key // heads_here
    experts_here, _, each = gate_proj.shape
    expert_count = experts_here * owners
    picks = routes.shape[1]
    seq_len = local_rows * owners
    half_rows = local_rows // 2
    scale = head_dim ** (-0.5)
    e, f, t = ring.index, ring.group, ring.half
    key_head = (e * heads_here) // heads_each_key
    shared_index = e % sharers

    pair = groups == 2
    q_cols = heads_here * head_dim
    down = down_proj.reshape(experts_here * each, width)
    first = jnp.stack([e * experts_here, t * expert_count]).astype(jnp.int32)

    def attention_tables(places, piece_starts):
        group_places = lax.dynamic_slice_in_dim(places, f * seq_len, seq_len)
        by_slot = jnp.take(group_places.reshape(owners, 2, half_rows), ring.owners_by_slot, axis=0)
        order_places = jnp.concatenate(
            [
                lax.dynamic_index_in_dim(by_slot, t, 1, keepdims=False).reshape(-1),
                lax.dynamic_index_in_dim(by_slot, 1 - t, 1, keepdims=False).reshape(-1),
            ]
        )
        position = order_places % seq_len
        begins = lax.dynamic_slice_in_dim(piece_starts, f, 1)
        inside = (begins <= position[:, None]) & (position[:, None] < begins + PIECE)
        limit = jnp.maximum(
            position, jnp.max(jnp.where(inside, begins + (PIECE - 1), 0), axis=1)
        )
        half_dim = head_dim // 2
        freqs = jnp.exp(jnp.arange(half_dim, dtype=F32) * (-2.0 * LOG_THETA / head_dim))
        angles = position.astype(F32)[:, None] * freqs[None, :]
        cosine, sine = jnp.cos(angles), jnp.sin(angles)
        return (
            jnp.concatenate([cosine, cosine], axis=1),
            jnp.concatenate([-sine, sine], axis=1),
            query_gain[None, :],
            key_gain[None, :],
            position[None, :],
            limit[:, None],
        )

    grads_own = ring.own_rows(out_grad)
    payload = jnp.concatenate([grads_own, pad_lanes(ring.own_rows(routes).astype(BF16))], axis=1)
    stream = ring.own_rows(tokens).astype(F32)
    first_inverse = inverse_norm(stream)
    normed = stream * first_inverse
    made = {}

    def first_hook(step, walk):
        done = []
        if step == 0:
            made["cut"] = cut_weights(
                e, key_head, query_proj, key_matrix, value_matrix, out_proj, q_cols, head_dim
            )
            made["chunks"] = []
            if not pair:
                made["weights"] = (lax.all_gather(made["cut"], "fsdp", axis=0, tiled=True),)
        if pair:
            rows = made["cut"].shape[0] // ring.ahead
            chunk = made["cut"][step * rows : (step + 1) * rows]
            if step:
                chunk = after(chunk, walk.ahead)
            made["chunks"].append(ring.swap_groups(chunk))
            done.append(made["chunks"][-1])
        grads_walk.step(walk.ahead if step else None)
        done.append(grads_walk.ahead)
        if step == 1:
            made["tables"] = attention_tables(*after((places, piece_starts), walk.ahead))
            done += made["tables"][:4]
        if step == 2:
            done += made["tables"][4:]
        return tuple(done)

    grads_walk = ring.walk(payload)
    attn_in, _ = ring.gather((normed * attn_gain).astype(BF16), first_hook)
    if pair:
        made["weights"] = (made["cut"], jnp.concatenate(made["chunks"], axis=0))
    tables, weights = made["tables"], made["weights"]
    at = jnp.stack([f, 1 - f] if pair else [jnp.zeros_like(f)]).astype(jnp.int32)
    raw, query_low, key_low, value_low = project(at, attn_in, weights, heads_here, *tables[:4])
    low = (query_low, key_low, value_low)
    attn_other, lse_other, part_other = attend(at, 1, weights, *tables[4:], *low)
    attn_mine, lse_mine, part_mine = attend(at, 0, weights, *tables[4:], *low)
    grads_found = grads_walk.found
    grads_mine = jnp.concatenate(grads_found, axis=0)
    grads = (grads_mine, ring.swap_halves(grads_mine))
    their_rows = []

    def across(signal):
        if not pair:
            return []
        rows = ffn_in[0].shape[0] // ring.ahead
        start = len(their_rows) * rows
        their_rows.append(ring.swap_groups(after(ffn_in[0], signal)[start : start + rows]))
        return their_rows[-1:]

    def branch_hook(step, signal):
        if step != 1:
            return None
        made["router"] = ring.whole_rows(after(router, signal))
        made["lanes"] = pad_lanes(made["router"])
        return made["lanes"]

    residual = stream + ring.scatter(part_mine, part_other, branch_hook)
    whole_router, router_lanes = made["router"], made["lanes"]

    second_inverse = inverse_norm(residual)
    mid_normed = residual * second_inverse
    ffn_in, _ = ring.gather((mid_normed * ffn_gain).astype(BF16))
    if pair:
        their_grads = ring.swap_groups(grads_mine)
    weighted, hidden, gates, back_mine, back_other = experts(
        first, ffn_in, grads, gate_proj, up_proj, down_proj, router_lanes, picks, expert_count
    )

    if pair:
        made["grads"], back_mine = after((their_grads, back_mine), their_grads)
    back_sum = ring.scatter(back_mine, back_other)

    gate_grad_rows = sum(
        back_sum[:, width + i * expert_count : width + (i + 1) * expert_count] for i in range(4)
    )
    own_gates = gates[:half_rows, :expert_count]
    picked_grad = own_gates * (
        gate_grad_rows - jnp.sum(own_gates * gate_grad_rows, axis=-1, keepdims=True)
    )
    logit_grad = picked_grad.astype(BF16)
    ffn_in_grad = back_sum[:, :width] + contract_cols(logit_grad, whole_router)
    ffn_gain_part = jnp.sum(ffn_in_grad * mid_normed, axis=0)
    second_normed_grad = ffn_in_grad * ffn_gain
    mid_grad = grads_own.astype(F32) + second_inverse * (
        second_normed_grad
        - mid_normed * jnp.mean(second_normed_grad * mid_normed, axis=-1, keepdims=True)
    )
    layer_parts = []

    def layer_hook(step, walk):
        layer_parts.append(layer_part(step, ring.ahead, after(weighted, walk.ahead), down))
        return tuple([layer_parts[-1]] + across(walk.ahead))

    branch, _ = ring.gather(
        jnp.concatenate([mid_grad.astype(BF16), pad_lanes(logit_grad)], axis=1), layer_hook
    )
    middle = len(layer_parts) // 2

    attn_halves = (attn_mine, attn_other)
    out_theirs, out_arrived = ring.send_share(branch, attn_halves, width, BF16)
    raw_mine, raw_other, head_gains, both_mine, both_other = attend_back(
        at,
        branch if out_theirs is None else after(branch, out_theirs),
        weights,
        layer_parts,
        half_rows,
        *tables,
        (raw, query_low, key_low, value_low, lse_mine, lse_other),
    )
    raw_halves = (raw_mine, raw_other)
    qkv_theirs, qkv_arrived = ring.send_share(attn_in, raw_halves, width, BF16)


    made["other"] = []

    def other_piece(half, signal):
        x, g = after([part[half] for part in made["theirs"]], signal)
        made["other"].append(
            other_experts(first, x, g, gate_proj, up_proj, down_proj, router_lanes, picks)
        )
        return made["other"][-1]

    totals = {"gate_up": [], "down": []}

    def last_piece(n, signal):
        x, g = made["theirs"]
        if n < experts_here:
            *totals["gate_up"], token = gate_up_grad(
                n,
                experts_here,
                totals["gate_up"],
                after(ffn_in, signal),
                x,
                hidden,
                [part[1] for part in made["other"]],
            )
        else:
            *totals["down"], token = down_grad(
                n - experts_here,
                2,
                experts_here,
                totals["down"],
                after(weighted, signal),
                [part[0] for part in made["other"]],
                grads,
                g,
            )
        return [token]

    def in_hook(step, signal):
        done = []
        if step == 0:
            share = ring.add_share(out_arrived, after(branch, signal), attn_halves, width)
            made["out_walk"] = ring.walk(share.astype(BF16), True)
            if pair:
                theirs = [join_rows(after(their_rows, signal)), after(made["grads"], signal)]
                made["theirs"] = [(part, ring.swap_halves(part)) for part in theirs]
                done += made["theirs"]
        else:
            made["out_walk"].step(signal)
        done.append(made["out_walk"].found[-1])
        if step == 1:
            made["qkv"] = ring.add_share(qkv_arrived, after(attn_in, signal), raw_halves, width)
            done.append(made["qkv"])
        if step in (1, 2) and pair:
            done += other_piece(step - 1, signal)
        if step == 3 and pair:
            done += last_piece(0, signal)
        return tuple(done)

    if qkv_theirs is not None:
        both_mine = after(both_mine, qkv_theirs)
    both_sum = ring.scatter(both_mine, both_other, in_hook)
    attn_in_grad = both_sum[:half_rows]
    layer_out = ring.join_halves((residual + both_sum[half_rows:]).astype(BF16))
    qkv_share = made["qkv"]
    first_normed_grad = attn_in_grad * attn_gain
    tokens_grad = mid_grad + first_inverse * (
        first_normed_grad - normed * jnp.mean(first_normed_grad * normed, axis=-1, keepdims=True)
    )
    tokens_grad = ring.join_halves(tokens_grad)
    attn_gain_part = jnp.sum(attn_in_grad * normed, axis=0)
    gains = ring.sum_all(
        jnp.concatenate([attn_gain_part, ffn_gain_part, head_gains[0], head_gains[1]])
    )

    kv_share = qkv_share[:, q_cols:]
    step = sharers // 2
    while step:
        rows = kv_share.shape[0] // 2
        bit = (shared_index // step) % 2
        pairs = [(i, i ^ step) for i in range(owners)]
        sent = lax.dynamic_slice_in_dim(kv_share, (1 - bit) * rows, rows)
        kept = lax.dynamic_slice_in_dim(kv_share, bit * rows, rows)
        kv_share = kept + ring.send(sent.astype(BF16), pairs).astype(F32)
        step //= 2
    own_share = jnp.concatenate([qkv_share[:, :q_cols], kv_share], axis=0).astype(BF16)

    last = ring.ahead - 1
    lanes_at = width // LANES

    share_rows = qkv_share.shape[0]
    shapes = [(share_rows, heads_tp * head_dim)] + [(share_rows, kv_tp * head_dim)] * 2

    def weight_hook(step, walk):
        signal = walk.ahead
        done = []
        if step == 0:
            made["out_walk"].step(signal)
            done += made["out_walk"].found[-1]
        if pair:
            done += last_piece(step + 1, signal)
        if step == 1:
            _, arrived = ring.send_share(after(ffn_in, signal), branch, width, F32, LANES, lanes_at)
            made["router_arrived"] = arrived
            done += [] if arrived is None else [arrived]
        if step == 2:
            made["router_grad"] = ring.add_share(
                made["router_arrived"], after(ffn_in, signal), branch, width, LANES, lanes_at
            )
            done.append(made["router_grad"])
        if step == last:
            found = made["out_walk"].found
            made["out_grad"] = place_wide(
                ring.owners_by_slot,
                [after(found[0], signal)] + found[1:-1] + list(found[-1]),
                heads_tp * head_dim,
            )
            done.append(made["out_grad"])
        if step == last:
            found = walk.found
            made["placed"] = place_blocks(
                ring.owners_by_slot, [after(found[0], signal)] + found[1:], shapes, sharers
            )
            done += made["placed"]
        return tuple(done)

    found = ring.blocks(own_share, weight_hook, True)
    out_grad_w = made["out_grad"]
    query_grad_w, key_grad_w, value_grad_w = place_last(
        ring.owners_by_slot[owners - 1], found[-1], made["placed"], sharers
    )
    router_grad = made["router_grad"][:, :expert_count]

    if pair:
        gate_total, up_total = totals["gate_up"]
        (down_total,) = totals["down"]
    else:
        all_rows, all_grads = ring.all_groups(ffn_in[0]), ring.all_groups(grads[0])

        def add_group(n, sums):
            gate_up, low = 0.0, 0.0
            for x, g in zip(all_rows, all_grads, strict=True):
                w, h = other_experts(
                    first, x[n], g[n], gate_proj, up_proj, down_proj, router_lanes, picks
                )
                gate_up = gate_up + contract_rows(x[n], h)
                low = low + contract_rows(w, g[n])[:, :width]
            gate_up = gate_up.reshape(width, experts_here, 2, each)
            return (
                sums[0] + jnp.swapaxes(gate_up[:, :, 0], 0, 1),
                sums[1] + jnp.swapaxes(gate_up[:, :, 1], 0, 1),
                sums[2] + low.reshape(experts_here, each, width),
            )

        gate_total, up_total, down_total = lax.fori_loop(
            0,
            groups,
            add_group,
            tuple(jnp.zeros(w.shape, F32) for w in (gate_proj, up_proj, down_proj)),
        )
    return (
        layer_out,
        tokens_grad,
        gains[:width],
        query_grad_w,
        key_grad_w,
        value_grad_w,
        out_grad_w,
        gains[2 * width : 2 * width + head_dim],
        gains[2 * width + head_dim :],
        gains[width : 2 * width],
        router_grad,
        gate_total,
        up_total,
        down_total,
    )


def solution(mesh):
    return jax.shard_map(
        body,
        mesh=mesh,
        in_specs=(
            P(("fsdp", "ep"), None),
            P(("fsdp", "ep"), None),
            P(),
            P(),
            P(),
            P("fsdp", "tp"),
            P("fsdp", "tp"),
            P("fsdp", "tp"),
            P("fsdp", "tp"),
            P(),
            P(),
            P(),
            P("fsdp", None),
            P("ep", None, "tp"),
            P("ep", None, "tp"),
            P("ep", "tp", None),
            P(("fsdp", "ep"), None),
        ),
        out_specs=(
            P(("fsdp", "ep"), None),
            P(("fsdp", "ep"), None),
            P(),
            P("fsdp", "tp"),
            P("fsdp", "tp"),
            P("fsdp", "tp"),
            P("fsdp", "tp"),
            P(),
            P(),
            P(),
            P("fsdp", None),
            P("ep", None, "tp"),
            P("ep", None, "tp"),
            P("ep", "tp", None),
        ),
        check_vma=False,
    )
```

```python
import functools
import math

import jax
import jax.numpy as jnp
import numpy as np
from jax import lax
from jax.experimental import pallas as pl
from jax.experimental.pallas import tpu as pltpu
from jax.sharding import PartitionSpec as P

PIECE = 256


EPSILON = 1e-06
LOG_THETA = math.log(1000000.0)
MASKED_SCORE = -1e30
LANES = 128
BF16 = jnp.bfloat16
F32 = jnp.float32


def inverse_norm(values):
    return lax.rsqrt(jnp.mean(values * values, axis=-1, keepdims=True) + EPSILON)


def dot(left, right):
    return jnp.dot(left, right, preferred_element_type=F32)


def contract_rows(left, right):
    return lax.dot_general(left, right, (((0,), (0,)), ((), ())), preferred_element_type=F32)


def contract_cols(left, right):
    return lax.dot_general(left, right, (((1,), (1,)), ((), ())), preferred_element_type=F32)


class Ring:
    def __init__(self):
        self.owners = lax.axis_size("ep")
        self.groups = lax.axis_size("fsdp")
        self.index = lax.axis_index("ep")
        self.group = lax.axis_index("fsdp")
        self.half = lax.axis_index("tp")
        n = self.owners
        if n == 8:
            order = [0, 2, 4, 6, 7, 5, 3, 1] if self.groups == 2 else [0, 1, 2, 3, 7, 6, 5, 4]
        else:
            order = list(range(n))
        self.forward = [(order[i], order[(i + 1) % n]) for i in range(n)]
        self.backward = [(dst, src) for src, dst in self.forward]
        self.ahead = n // 2
        self.behind = (n - 1) // 2
        offsets = [0]
        for step in range(1, self.ahead + 1):
            offsets.append(-step)
            if step <= self.behind:
                offsets.append(step)
        self.slot = {offset: place for place, offset in enumerate(offsets)}
        self.slot[self.ahead] = self.slot[-self.ahead] if n % 2 == 0 else self.slot[self.ahead]
        table = np.zeros((n, n), np.int32)
        for position, owner in enumerate(order):
            for place, offset in enumerate(offsets):
                table[owner, place] = order[(position + offset) % n]
        self.owners_by_slot = jnp.asarray(table)[self.index]

    def send(self, values, pairs, axis="ep"):
        return lax.ppermute(values, axis, pairs)

    def swap_halves(self, values):
        return self.send(values, [(0, 1), (1, 0)], "tp")

    def swap_groups(self, values):
        return self.send(values, [(0, 1), (1, 0)], "fsdp")

    def walk(self, own, even=False):
        return Walk(self, own, even)

    def blocks(self, own, hook=None, even=False):
        walk = Walk(self, own, even)
        for step in range(self.ahead):
            done = None if hook is None else hook(step, walk)
            walk.step()
            walk.hold(done)
        return walk.found

    def gather(self, own, hook=None):
        found = self.blocks(own, hook)
        mine = jnp.concatenate(found, axis=0)
        return (mine, self.swap_halves(mine)), found

    def scatter(self, mine, other, hook=None):
        fold = Fold(self, mine, other)
        for step in range(self.ahead):
            done = None if hook is None else hook(step, fold.ahead)
            fold.step(None, done)
        return fold.result()

    def own_rows(self, values):
        rows = values.shape[0] // 2
        return lax.dynamic_slice_in_dim(values, self.half * rows, rows)

    def join_halves(self, own):
        other = self.swap_halves(own)
        first = self.half == 0
        return jnp.concatenate([jnp.where(first, own, other), jnp.where(first, other, own)], axis=0)

    def whole_rows(self, own):
        if self.groups == 2:
            other = self.swap_groups(own)
            first = self.group == 0
            return jnp.concatenate(
                [jnp.where(first, own, other), jnp.where(first, other, own)], axis=0
            )
        return lax.all_gather(own, "fsdp", axis=0, tiled=True)

    def send_share(self, lefts, rights, width, kind, cols=None, block=0):
        if self.groups != 2:
            return None, None
        theirs = transposed_product(lefts, rights, width // 2, 1 - self.group, kind, cols, block)
        return theirs, self.swap_groups(theirs)

    def add_share(self, arrived, lefts, rights, width, cols=None, block=0):
        if self.groups == 2:
            ours = transposed_product(lefts, rights, width // 2, self.group, F32, cols, block)
            return ours + arrived.astype(F32)
        cols = cols or rights[0].shape[1]
        whole = contract_rows(
            jnp.concatenate(lefts, axis=0)[:, :width],
            jnp.concatenate(rights, axis=0)[:, block * cols : (block + 1) * cols],
        )
        return lax.psum_scatter(whole, "fsdp", scatter_dimension=0, tiled=True)

    def all_groups(self, mine):
        theirs = lax.all_gather(mine, "fsdp", axis=0)
        return theirs, self.swap_halves(theirs)

    def sum_all(self, values):
        for axis in ("ep", "fsdp", "tp"):
            step = 1
            while step < lax.axis_size(axis):
                pairs = [(i, i ^ step) for i in range(lax.axis_size(axis))]
                values = values + self.send(values, pairs, axis)
                step *= 2
        return values


def after(values, signal):
    return lax.optimization_barrier((values, signal))[0]


class Walk:
    def __init__(self, ring, own, even):
        self.ring, self.ahead, self.behind, self.even = ring, own, own, even
        self.found, self.count = [own], 0

    def hold(self, done):
        if done is not None:
            self.ahead, self.behind, self.found[-1] = after(
                (self.ahead, self.behind, self.found[-1]), done
            )

    def step(self, signal=None):
        ring = self.ring
        self.count += 1
        if signal is not None:
            self.ahead, self.behind = after((self.ahead, self.behind), signal)
        if self.count > ring.behind and self.even and ring.behind:
            cut = self.ahead.shape[0] // 2
            self.found.append(
                (
                    ring.send(self.ahead[:cut], ring.forward),
                    ring.send(self.behind[cut:], ring.backward),
                )
            )
            return
        self.ahead = ring.send(self.ahead, ring.forward)
        self.found.append(self.ahead)
        if self.count <= ring.behind:
            self.behind = ring.send(self.behind, ring.backward)
            self.found.append(self.behind)


class Fold:
    def __init__(self, ring, mine, other):
        mine = mine.astype(F32) + ring.swap_halves(other).astype(F32)
        self.ring = ring
        self.mine = mine.astype(BF16).reshape(ring.owners, -1, mine.shape[-1])
        self.ahead = self.mine[ring.slot[ring.ahead]]
        self.behind = self.mine[ring.slot[-ring.behind]] if ring.behind else None
        self.count = 0

    def block(self, offset):
        return self.mine[self.ring.slot[offset]].astype(F32)

    def step(self, signal=None, done=None):
        ring = self.ring
        self.count += 1
        if signal is not None:
            self.ahead = after(self.ahead, signal)
        offset = ring.ahead - self.count
        self.ahead = ring.send(self.ahead, ring.forward)
        if done is not None:
            self.ahead = after(self.ahead, done)
        if offset:
            self.ahead = (self.ahead.astype(F32) + self.block(offset)).astype(BF16)
        offset = ring.behind - self.count
        if offset >= 0:
            if signal is not None:
                self.behind = after(self.behind, signal)
            self.behind = ring.send(self.behind, ring.backward)
            if done is not None:
                self.behind = after(self.behind, done)
            if offset:
                self.behind = (self.behind.astype(F32) + self.block(-offset)).astype(BF16)

    def result(self):
        total = self.block(0) + self.ahead.astype(F32)
        return total if self.behind is None else total + self.behind.astype(F32)


def pad_lanes(values):
    return jnp.pad(values, ((0, 0), (0, LANES - values.shape[1])))


VMEM = pltpu.VMEM
SMEM = pltpu.SMEM
ROW_BLOCK = 256


def call(kernel, micros, **kwargs):
    return pl.pallas_call(
        kernel,
        compiler_params=pltpu.CompilerParams(vmem_limit_bytes=56 * 1024 * 1024),
        cost_estimate=pl.CostEstimate(
            flops=int(micros * 1.15e9), bytes_accessed=0, transcendentals=0
        ),
        **kwargs,
    )


def whole_spec():
    return pl.BlockSpec(memory_space=VMEM)


def turned(values):
    return pltpu.roll(values, values.shape[-1] // 2, 1)


def row_blocks(mine, other, step=ROW_BLOCK):
    half = mine.shape[0]
    for place, ref in enumerate((mine, other)):
        for start in range(0, half, step):
            yield ref, start, place * half + start


def cut_kernel(e_ref, q_ref, k_ref, v_ref, o_ref, out_ref):
    cols, dim = q_ref.shape[1], k_ref.shape[1]
    out_ref[:, :cols] = q_ref[...]
    out_ref[:, cols : cols + dim] = k_ref[...]
    out_ref[:, cols + dim : cols + 2 * dim] = v_ref[...]
    out_ref[:, cols + 2 * dim :] = o_ref[...]


def cut_weights(device, key_head, query_proj, key_matrix, value_matrix, out_proj, cols, dim):
    rows = query_proj.shape[0]
    heads = pl.BlockSpec((rows, cols), lambda i, e: (0, e[0]))
    key = pl.BlockSpec((rows, dim), lambda i, e: (0, e[1]))
    return call(
        cut_kernel,
        3,
        grid_spec=pltpu.PrefetchScalarGridSpec(
            num_scalar_prefetch=1,
            grid=(1,),
            in_specs=[heads, key, key, heads],
            out_specs=pl.BlockSpec((rows, 2 * cols + 2 * dim), lambda i, e: (0, 0)),
        ),
        out_shape=jax.ShapeDtypeStruct((rows, 2 * cols + 2 * dim), BF16),
    )(jnp.stack([device, key_head]).astype(jnp.int32), query_proj, key_matrix, value_matrix, out_proj)


def spots(at_ref, w_refs):
    rows = w_refs[0].shape[0]
    return [(pl.ds(pl.multiple_of(at_ref[i] * rows, rows), rows), ref) for i, ref in enumerate(w_refs)]


def project_kernel(
    heads, parts, at_ref, xm_ref, xo_ref, cos_ref, sin_ref, qg_ref, kg_ref, *refs
):
    w_refs, (raw_ref, ql_ref, kl_ref, vl_ref) = refs[:parts], refs[parts:]
    dim = qg_ref.shape[1]
    cols = heads * dim
    for ref, start, row in row_blocks(xm_ref, xo_ref):
        rows = slice(row, row + ROW_BLOCK)
        raw = sum(
            dot(ref[start : start + ROW_BLOCK, spot], w_ref[:, : cols + 2 * dim])
            for spot, w_ref in spots(at_ref, w_refs)
        )
        raw_ref[rows, :] = raw[:, : cols + dim]
        cosine, sine = cos_ref[rows, :], sin_ref[rows, :]
        for head in range(heads + 1):
            part = raw[:, head * dim : (head + 1) * dim]
            gain = qg_ref[...] if head < heads else kg_ref[...]
            part = part * inverse_norm(part) * gain
            part = (part * cosine + turned(part) * sine).astype(BF16)
            if head < heads:
                ql_ref[rows, head * dim : (head + 1) * dim] = part
            else:
                kl_ref[rows, :] = part
        vl_ref[rows, :] = raw[:, cols + dim :].astype(BF16)


def smem_spec():
    return pl.BlockSpec(memory_space=SMEM)


def project(at, x, weights, heads, cosine, sine, q_gain, k_gain):
    rows, dim = 2 * x[0].shape[0], q_gain.shape[1]
    cols = heads * dim
    return call(
        functools.partial(project_kernel, heads, len(weights)),
        7,
        in_specs=[smem_spec()] + [whole_spec()] * (6 + len(weights)),
        out_specs=[whole_spec()] * 4,
        out_shape=[
            jax.ShapeDtypeStruct((rows, cols + dim), F32),
            jax.ShapeDtypeStruct((rows, cols), BF16),
            jax.ShapeDtypeStruct((rows, dim), BF16),
            jax.ShapeDtypeStruct((rows, dim), BF16),
        ],
    )(at, *x, cosine, sine, q_gain, k_gain, *weights)


def attend_kernel(heads, base, parts, at_ref, pos_ref, lim_ref, ql_ref, kl_ref, vl_ref, *refs):
    w_refs, (out_ref, lse_ref, part_ref) = refs[:parts], refs[parts:]
    dim = kl_ref.shape[1]
    cols = heads * dim
    scale = dim ** (-0.5)
    for row in range(0, out_ref.shape[0], ROW_BLOCK):
        rows, among = slice(row, row + ROW_BLOCK), slice(base + row, base + row + ROW_BLOCK)
        allowed = pos_ref[...] <= lim_ref[among, :]
        for head in range(heads):
            cut = slice(head * dim, (head + 1) * dim)
            scores = contract_cols(ql_ref[among, cut], kl_ref[...]) * scale
            scores = jnp.where(allowed, scores, MASKED_SCORE)
            top = jnp.max(scores, axis=1, keepdims=True)
            powers = jnp.exp(scores - top)
            total = jnp.sum(powers, axis=1, keepdims=True)
            lse_ref[head, rows, :] = top + jnp.log(total)
            probs = (powers * (1.0 / total)).astype(BF16)
            out_ref[rows, cut] = dot(probs, vl_ref[...]).astype(BF16)
        for spot, w_ref in spots(at_ref, w_refs):
            part_ref[rows, spot] = contract_cols(
                out_ref[rows, :], w_ref[:, cols + 2 * dim :]
            ).astype(BF16)


def attend(at, place, weights, position, limit, query, key, value):
    rows, dim = key.shape
    cols = query.shape[1]
    half, width = rows // 2, sum(w.shape[0] for w in weights)
    heads = cols // dim
    return call(
        functools.partial(attend_kernel, heads, place * half, len(weights)),
        6.5,
        in_specs=[smem_spec()] + [whole_spec()] * (5 + len(weights)),
        out_specs=[whole_spec()] * 3,
        out_shape=[
            jax.ShapeDtypeStruct((half, cols), BF16),
            jax.ShapeDtypeStruct((heads, half, 1), F32),
            jax.ShapeDtypeStruct((half, width), BF16),
        ],
    )(at, position, limit, query, key, value, *weights)


def attend_back_kernel(
    heads,
    parts,
    at_ref,
    bm_ref,
    bo_ref,
    cos_ref,
    sin_ref,
    qg_ref,
    kg_ref,
    pos_ref,
    lim_ref,
    raw_ref,
    ql_ref,
    kl_ref,
    vl_ref,
    lm_ref,
    lo_ref,
    *refs,
):
    w_refs, (rm_ref, ro_ref, gains_ref, pm_ref, po_ref, dk_ref, dv_ref) = refs[:parts], refs[parts:]
    dim = qg_ref.shape[1]
    cols = heads * dim
    scale = dim ** (-0.5)
    q_part = jnp.zeros((1, dim), F32)
    k_part = jnp.zeros((1, dim), F32)

    def norm_back(grad, rows, raw, gain):
        inverse = inverse_norm(raw)
        unit = raw * inverse
        grad = grad * cos_ref[rows, :] - turned(grad) * sin_ref[rows, :]
        part = jnp.sum(grad * unit, axis=0, keepdims=True)
        grad = grad * gain
        return inverse * (grad - unit * jnp.mean(grad * unit, axis=1, keepdims=True)), part

    first = True
    for (ref, start, row), lse_ref, rg_ref in zip(
        row_blocks(bm_ref, bo_ref), (lm_ref, lm_ref, lo_ref, lo_ref), (rm_ref, rm_ref, ro_ref, ro_ref)
    ):
        rows, here = slice(row, row + ROW_BLOCK), slice(start, start + ROW_BLOCK)
        grads = sum(
            dot(ref[here, spot], w_ref[:, cols + 2 * dim :]) for spot, w_ref in spots(at_ref, w_refs)
        ).astype(BF16)
        allowed = pos_ref[...] <= lim_ref[rows, :]
        for head in range(heads):
            cut = slice(head * dim, (head + 1) * dim)
            query, value_grad = ql_ref[rows, cut], grads[:, cut]
            scores = contract_cols(query, kl_ref[...]) * scale
            probs = jnp.exp(jnp.where(allowed, scores - lse_ref[head, here, :], MASKED_SCORE))
            prob_grad = contract_cols(value_grad, vl_ref[...])
            weighed = probs * prob_grad
            delta = jnp.sum(weighed, axis=1, keepdims=True)
            score_grad = (weighed - probs * delta).astype(BF16)
            q_grad = dot(score_grad, kl_ref[...]) * scale
            k_more = contract_rows(query, score_grad)
            v_more = contract_rows(value_grad, probs.astype(BF16))
            if first:
                dk_ref[...] = k_more
                dv_ref[...] = v_more
                first = False
            else:
                dk_ref[...] += k_more
                dv_ref[...] += v_more
            q_raw_grad, part = norm_back(q_grad, rows, raw_ref[rows, cut], qg_ref[...])
            q_part = q_part + part
            rg_ref[here, cut] = q_raw_grad.astype(BF16)
    for (_, start, row), rg_ref, ref in zip(
        row_blocks(bm_ref, bo_ref),
        (rm_ref, rm_ref, ro_ref, ro_ref),
        (pm_ref, pm_ref, po_ref, po_ref),
    ):
        rows, here = slice(row, row + ROW_BLOCK), slice(start, start + ROW_BLOCK)
        k_grad = dk_ref[:, rows].T * scale
        k_raw_grad, part = norm_back(k_grad, rows, raw_ref[rows, cols : cols + dim], kg_ref[...])
        k_part = k_part + part
        rg_ref[here, cols : cols + dim] = k_raw_grad.astype(BF16)
        rg_ref[here, cols + dim :] = dv_ref[:, rows].T.astype(BF16)
        for spot, w_ref in spots(at_ref, w_refs):
            part = contract_cols(rg_ref[here, :], w_ref[:, : cols + 2 * dim]).astype(BF16)
            ref[here, spot] = part
    gains_ref[0:1, :] = q_part
    gains_ref[1:2, :] = k_part


def attend_back(at, branch, weights, cosine, sine, q_gain, k_gain, position, limit, saved):
    half = branch[0].shape[0]
    dim = q_gain.shape[1]
    width = sum(w.shape[0] for w in weights)
    cols = saved[1].shape[1]
    raw_half = jax.ShapeDtypeStruct((half, cols + 2 * dim), BF16)
    return call(
        functools.partial(attend_back_kernel, cols // dim, len(weights)),
        18.5,
        in_specs=[smem_spec()] + [whole_spec()] * (14 + len(weights)),
        out_specs=[whole_spec()] * 5,
        out_shape=[
            raw_half,
            raw_half,
            jax.ShapeDtypeStruct((2, dim), F32),
            jax.ShapeDtypeStruct((half, width), BF16),
            jax.ShapeDtypeStruct((half, width), BF16),
        ],
        scratch_shapes=[VMEM((dim, 2 * half), F32), VMEM((dim, 2 * half), F32)],
    )(at, *branch, cosine, sine, q_gain, k_gain, position, limit, *saved, *weights)


def routed_gates(x_ref, g_ref, router_ref, picks):
    lane = lax.broadcasted_iota(jnp.int32, (1, LANES), 1).astype(F32)
    logits = dot(x_ref[...], router_ref[...])
    names = g_ref[:, x_ref.shape[1] :].astype(F32)
    chosen = jnp.zeros(logits.shape, F32)
    for k in range(picks):
        chosen = jnp.where(names[:, k : k + 1] == lane, 1.0, chosen)
    logits = jnp.where(chosen > 0.0, logits, MASKED_SCORE)
    powers = chosen * jnp.exp(logits - jnp.max(logits, axis=1, keepdims=True))
    return powers / jnp.sum(powers, axis=1, keepdims=True)


def expert_values(x, g, gates, name, gate_up, down):
    each = down.shape[0]
    lane = lax.broadcasted_iota(jnp.int32, (1, LANES), 1)
    both = dot(x, gate_up)
    gate_val, up_val = both[:, :each], both[:, each:]
    grad = contract_cols(g, down)
    gate = jnp.sum(jnp.where(lane == name, gates, 0.0), axis=1, keepdims=True)
    sigmoid_val = 0.5 * jnp.tanh(0.5 * gate_val) + 0.5
    silu_val = gate_val * sigmoid_val
    act = silu_val * up_val
    act_grad = gate * grad
    gate_low = (act_grad * up_val * (sigmoid_val + silu_val * (1.0 - sigmoid_val))).astype(BF16)
    up_low = (act_grad * silu_val).astype(BF16)
    return (gate * act).astype(BF16), gate_low, up_low, act * grad


def experts_kernel(
    picks,
    expert_count,
    first_ref,
    xm_ref,
    xo_ref,
    gm_ref,
    go_ref,
    wg_ref,
    wu_ref,
    wd_ref,
    router_ref,
    weighted_ref,
    hidden_ref,
    gates_ref,
    pm_ref,
    po_ref,
    both_ref,
    side_ref,
):
    expert = pl.program_id(0)
    wide, width = xm_ref.shape
    each = wg_ref.shape[2]
    lane = lax.broadcasted_iota(jnp.int32, (1, LANES), 1)
    halves = ((xm_ref, gm_ref, pm_ref, 0), (xo_ref, go_ref, po_ref, wide))

    @pl.when(expert == 0)
    def _():
        for x_ref, g_ref, _, row in halves:
            gates_ref[row : row + wide, :] = routed_gates(x_ref, g_ref, router_ref, picks)

    name = first_ref[0] + expert
    place = first_ref[1] + name
    at = pl.multiple_of(expert * 2 * each, 2 * each)
    both_ref[:, pl.ds(at, each)] = wg_ref[0]
    both_ref[:, pl.ds(at + each, each)] = wu_ref[0]
    for x_ref, g_ref, _, row in halves:
        rows = slice(row, row + wide)
        weighted, gate_low, up_low, products = expert_values(
            x_ref[...],
            g_ref[:, :width],
            gates_ref[rows, :],
            name,
            both_ref[:, pl.ds(at, 2 * each)],
            wd_ref[0],
        )
        weighted_ref[rows, :] = weighted
        hidden_ref[rows, pl.ds(at, each)] = gate_low
        hidden_ref[rows, pl.ds(at + each, each)] = up_low
        row_grad = jnp.sum(products, axis=1, keepdims=True)
        high = row_grad.astype(BF16).astype(F32)
        side = jnp.where(lane == place, high, 0.0)
        side = side + jnp.where(lane == place + 2 * expert_count, row_grad - high, 0.0)
        side_ref[rows, :] = jnp.where(expert == 0, side, side_ref[rows, :] + side)

    @pl.when(expert == pl.num_programs(0) - 1)
    def _():
        for _, _, ref, row in halves:
            rows = slice(row, row + wide)
            ref[:, :width] = contract_cols(hidden_ref[rows, :], both_ref[...]).astype(BF16)
            ref[:, width:] = side_ref[rows, :].astype(BF16)


def experts(first, x, g, gate_proj, up_proj, down_proj, router, picks, expert_count):
    half, width = x[0].shape
    rows = 2 * half
    count, _, each = gate_proj.shape
    resident = lambda shape: pl.BlockSpec(
        shape, lambda i, first: (0,) * len(shape), pipeline_mode=pl.Buffered(1)
    )
    payload = (half, width + LANES)
    return call(
        functools.partial(experts_kernel, picks, expert_count),
        41,
        grid_spec=pltpu.PrefetchScalarGridSpec(
            num_scalar_prefetch=1,
            grid=(count,),
            in_specs=[resident((half, width))] * 2
            + [resident(payload)] * 2
            + [pl.BlockSpec((1, width, each), lambda i, first: (i, 0, 0))] * 2
            + [
                pl.BlockSpec((1, each, width), lambda i, first: (i, 0, 0)),
                resident((width, LANES)),
            ],
            out_specs=[
                pl.BlockSpec((rows, each), lambda i, first: (0, i)),
                resident((rows, 2 * count * each)),
                resident((rows, LANES)),
                resident(payload),
                resident(payload),
            ],
            scratch_shapes=[VMEM((width, 2 * count * each), BF16), VMEM((rows, LANES), F32)],
        ),
        out_shape=[
            jax.ShapeDtypeStruct((rows, count * each), BF16),
            jax.ShapeDtypeStruct((rows, 2 * count * each), BF16),
            jax.ShapeDtypeStruct((rows, LANES), F32),
            jax.ShapeDtypeStruct(payload, BF16),
            jax.ShapeDtypeStruct(payload, BF16),
        ],
    )(first, x[0], x[1], g[0], g[1], gate_proj, up_proj, down_proj, router)


def transposed_product_kernel(side_ref, am_ref, ao_ref, bm_ref, bo_ref, out_ref):
    total = contract_rows(am_ref[...], bm_ref[...]) + contract_rows(ao_ref[...], bo_ref[...])
    out_ref[...] = total.astype(out_ref.dtype)


def transposed_product(lefts, rights, share, side, kind, cols=None, block=0):
    half = rights[0].shape[0]
    cols = cols or rights[0].shape[1]
    left = pl.BlockSpec((half, share), lambda i, side: (0, side[0]))
    return call(
        transposed_product_kernel,
        4,
        grid_spec=pltpu.PrefetchScalarGridSpec(
            num_scalar_prefetch=1,
            grid=(1,),
            in_specs=[left, left] + [pl.BlockSpec((half, cols), lambda i, side: (0, block))] * 2,
            out_specs=pl.BlockSpec((share, cols), lambda i, side: (0, 0)),
        ),
        out_shape=jax.ShapeDtypeStruct((share, cols), kind),
    )(side.reshape(1).astype(jnp.int32), *lefts, *rights)


def layer_kernel(w_ref, d_ref, out_ref):
    out_ref[...] = dot(w_ref[...], d_ref[...]).astype(BF16)


def layer_part(part, parts, weighted, down):
    rows, hidden = weighted.shape
    width = down.shape[1]
    return call(
        layer_kernel,
        4,
        grid=(1,),
        in_specs=[
            pl.BlockSpec((rows // parts, hidden), lambda i: (part, 0)),
            pl.BlockSpec((hidden, width), lambda i: (0, 0)),
        ],
        out_specs=pl.BlockSpec((rows // parts, width), lambda i: (0, 0)),
        out_shape=jax.ShapeDtypeStruct((rows // parts, width), BF16),
    )(weighted, down)


def other_experts_kernel(
    picks, first_ref, x_ref, g_ref, wg_ref, wu_ref, wd_ref, router_ref, w_ref, h_ref, gates_ref
):
    expert = pl.program_id(0)
    width = x_ref.shape[1]
    each = wg_ref.shape[2]

    @pl.when(expert == 0)
    def _():
        gates_ref[...] = routed_gates(x_ref, g_ref, router_ref, picks)

    w_ref[...], h_ref[:, :each], h_ref[:, each:], _ = expert_values(
        x_ref[...],
        g_ref[:, :width],
        gates_ref[...],
        first_ref[0] + expert,
        jnp.concatenate([wg_ref[0], wu_ref[0]], axis=1),
        wd_ref[0],
    )


def other_experts(first, x, g, gate_proj, up_proj, down_proj, router, picks):
    rows, width = x.shape
    count, _, each = gate_proj.shape
    resident = lambda shape: pl.BlockSpec(
        shape, lambda i, first: (0,) * len(shape), pipeline_mode=pl.Buffered(1)
    )
    return call(
        functools.partial(other_experts_kernel, picks),
        15,
        grid_spec=pltpu.PrefetchScalarGridSpec(
            num_scalar_prefetch=1,
            grid=(count,),
            in_specs=[resident(x.shape), resident(g.shape)]
            + [pl.BlockSpec((1, width, each), lambda i, first: (i, 0, 0))] * 2
            + [
                pl.BlockSpec((1, each, width), lambda i, first: (i, 0, 0)),
                resident(router.shape),
            ],
            out_specs=[
                pl.BlockSpec((rows, each), lambda i, first: (0, i)),
                pl.BlockSpec((rows, 2 * each), lambda i, first: (0, i)),
            ],
            scratch_shapes=[VMEM((rows, LANES), F32)],
        ),
        out_shape=[
            jax.ShapeDtypeStruct((rows, count * each), BF16),
            jax.ShapeDtypeStruct((rows, 2 * count * each), BF16),
        ],
    )(first, x, g, gate_proj, up_proj, down_proj, router)


def in_halves(values, block, index):
    if isinstance(values, (tuple, list)):
        places = (0, 0)
    else:
        values, places = (values, values), (0, 1)
    specs = [
        pl.BlockSpec(block, lambda i, place=place: (place, index), pipeline_mode=pl.Buffered(1))
        for place in places
    ]
    return list(values), specs


def sign(token_ref):
    token_ref[...] = jnp.zeros(token_ref.shape, token_ref.dtype)


TOKEN = (8, LANES)


def product_sum(lefts, rights):
    parts = [contract_rows(left[...], right[...]) for left, right in zip(lefts, rights)]
    return parts[0] + parts[1]


def gate_up_grad_kernel(x0, x1, x2, x3, d0, d1, d2, d3, *refs):
    gate_ref, up_ref, token_ref = refs[-3:]
    each = gate_ref.shape[2]
    total = product_sum((x0, x1), (d0, d1)) + product_sum((x2, x3), (d2, d3))
    gate_ref[0] = total[:, :each]
    up_ref[0] = total[:, each:]
    sign(token_ref)


def gate_up_grad(expert, count, totals, own, other, own_hidden, other_hidden):
    half, width = own[0].shape
    each = own_hidden.shape[1] // 2 // count
    wide = 2 * ROW_BLOCK
    part = pl.BlockSpec((1, wide, each), lambda i: (expert, i, 0))
    rights, specs = in_halves(own_hidden, (half, 2 * each), expert)
    single = pl.Buffered(1)
    return call(
        gate_up_grad_kernel,
        11.7,
        grid=(width // wide,),
        in_specs=[pl.BlockSpec((half, wide), lambda i: (0, i))] * 4
        + specs
        + [pl.BlockSpec((half, 2 * each), lambda i: (0, expert), pipeline_mode=single)] * 2
        + [pl.BlockSpec(memory_space=pl.ANY)] * len(totals),
        out_specs=[part] * 2 + [pl.BlockSpec(TOKEN, lambda i: (0, 0))],
        out_shape=[jax.ShapeDtypeStruct((count, width, each), F32)] * 2
        + [jax.ShapeDtypeStruct(TOKEN, F32)],
        input_output_aliases={8: 0, 9: 1} if totals else {},
    )(*own, *other, *rights, *other_hidden, *totals)


def down_grad_kernel(count, w0, w1, g0, g1, g2, g3, w2, w3, *refs):
    out_ref, token_ref = refs[-2:]
    each = out_ref.shape[1]
    total = product_sum((w0, w1), (g0, g1)) + product_sum((w2, w3), (g2, g3))
    for i in range(count):
        out_ref[i] = total[i * each : (i + 1) * each, :]
    sign(token_ref)


def down_grad(part, parts, count, totals, own_weighted, other_weighted, own, other):
    half, width = own[0].shape[0], own[0].shape[1] - LANES
    hidden = own_weighted.shape[1]
    each = hidden // count
    wide = 2 * ROW_BLOCK
    steps = width // wide // parts
    right = pl.BlockSpec((half, wide), lambda i: (0, part * steps + i))
    place = pl.BlockSpec((count, each, wide), lambda i: (0, 0, part * steps + i))
    lefts, specs = in_halves(own_weighted, (half, hidden), 0)
    single = pl.Buffered(1)
    return call(
        functools.partial(down_grad_kernel, count),
        9.7,
        grid=(steps,),
        in_specs=specs
        + [right] * 4
        + [pl.BlockSpec((half, hidden), lambda i: (0, 0), pipeline_mode=single)] * 2
        + [pl.BlockSpec(memory_space=pl.ANY)] * len(totals),
        out_specs=[place, pl.BlockSpec(TOKEN, lambda i: (0, 0))],
        out_shape=[
            jax.ShapeDtypeStruct((count, each, width), F32),
            jax.ShapeDtypeStruct(TOKEN, F32),
        ],
        input_output_aliases={8: 0} if totals else {},
    )(*lefts, *own, *other, *other_weighted, *totals)


def place_wide_kernel(owners_ref, *refs):
    blocks, (last_top, last_low), out_ref = refs[:-3], refs[-3:-1], refs[-1]
    cols = blocks[0].shape[1]

    def put(slot, ref):
        at = pl.multiple_of(owners_ref[slot] * cols, cols)
        out_ref[:, pl.ds(at, cols)] = ref[...].astype(F32)

    for slot, ref in enumerate(blocks):
        put(slot, ref)
    top = pl.program_id(0) < pl.num_programs(0) // 2

    @pl.when(top)
    def _():
        put(len(blocks), last_top)

    @pl.when(jnp.logical_not(top))
    def _():
        put(len(blocks), last_low)


def place_wide(owners_by_slot, blocks, width):
    share, cols = blocks[0].shape
    steps = share // ROW_BLOCK
    half = steps // 2
    return call(
        place_wide_kernel,
        4,
        grid=(steps,),
        in_specs=[smem_spec()]
        + [pl.BlockSpec((ROW_BLOCK, cols), lambda i: (i, 0))] * (len(blocks) - 2)
        + [
            pl.BlockSpec((ROW_BLOCK, cols), lambda i: (jnp.minimum(i, half - 1), 0)),
            pl.BlockSpec((ROW_BLOCK, cols), lambda i: (jnp.maximum(i - half, 0), 0)),
        ],
        out_specs=pl.BlockSpec((ROW_BLOCK, width), lambda i: (i, 0)),
        out_shape=jax.ShapeDtypeStruct((share, width), F32),
    )(owners_by_slot, *blocks)


def place_kernel(sharers, owners_ref, *refs):
    count = (len(refs) - 3) // 2
    blocks, lows, (q_ref, k_ref, v_ref) = refs[:count], refs[count:-3], refs[-3:]
    cols = blocks[0].shape[1]
    dim = cols // 2
    for i, ref in enumerate(blocks):
        at = pl.multiple_of(owners_ref[i] * cols, cols)
        q_ref[:, pl.ds(at, cols)] = ref[...].astype(F32)

    @pl.when(pl.program_id(0) == 0)
    def _():
        for i, ref in enumerate(lows):
            rows = ref.shape[0]
            down = pl.multiple_of(owners_ref[i] % sharers * rows, rows)
            right = pl.multiple_of(owners_ref[i] // sharers * dim, dim)
            k_ref[pl.ds(down, rows), pl.ds(right, dim)] = ref[:, :dim].astype(F32)
            v_ref[pl.ds(down, rows), pl.ds(right, dim)] = ref[:, dim:].astype(F32)


def place_blocks(owners_by_slot, blocks, shapes, sharers):
    share, width = shapes[0]
    cols = blocks[0].shape[1]
    rows = blocks[0].shape[0] - share
    return call(
        functools.partial(place_kernel, sharers),
        5,
        grid=(share // ROW_BLOCK,),
        in_specs=[smem_spec()]
        + [pl.BlockSpec((ROW_BLOCK, cols), lambda i: (i, 0))] * len(blocks)
        + [pl.BlockSpec((rows, cols), lambda i: (share // rows, 0))] * len(blocks),
        out_specs=[
            pl.BlockSpec((ROW_BLOCK, width), lambda i: (i, 0)),
            pl.BlockSpec(shapes[1], lambda i: (0, 0)),
            pl.BlockSpec(shapes[2], lambda i: (0, 0)),
        ],
        out_shape=[jax.ShapeDtypeStruct(shape, F32) for shape in shapes],
    )(owners_by_slot, *blocks, *blocks)


def place_last_kernel(share, owner_ref, top_in, low_in, q_any, k_any, v_any, q_ref, k_ref, v_ref):
    dim = k_ref.shape[1]
    cut = top_in.shape[0]
    q_ref[:cut, :] = top_in[...].astype(F32)
    q_ref[cut:, :] = low_in[: share - cut, :].astype(F32)
    k_ref[...] = low_in[share - cut :, :dim].astype(F32)
    v_ref[...] = low_in[share - cut :, dim:].astype(F32)


def place_last(owner, halves, totals, sharers):
    share = totals[0].shape[0]
    top, low = halves
    cols = top.shape[1]
    rows = top.shape[0] + low.shape[0] - share
    spots = pl.BlockSpec((rows, cols // 2), lambda i, o: (o[0] % sharers, o[0] // sharers))
    return call(
        functools.partial(place_last_kernel, share),
        3,
        grid_spec=pltpu.PrefetchScalarGridSpec(
            num_scalar_prefetch=1,
            grid=(1,),
            in_specs=[
                pl.BlockSpec(top.shape, lambda i, o: (0, 0)),
                pl.BlockSpec(low.shape, lambda i, o: (0, 0)),
            ]
            + [pl.BlockSpec(memory_space=pl.ANY)] * 3,
            out_specs=[pl.BlockSpec((share, cols), lambda i, o: (0, o[0])), spots, spots],
        ),
        out_shape=[jax.ShapeDtypeStruct(total.shape, F32) for total in totals],
        input_output_aliases={3: 0, 4: 1, 5: 2},
    )(owner.reshape(1), top, low, *totals)


def body(
    tokens,
    routes,
    places,
    piece_starts,
    attn_gain,
    query_proj,
    key_matrix,
    value_matrix,
    out_proj,
    query_gain,
    key_gain,
    ffn_gain,
    router,
    gate_proj,
    up_proj,
    down_proj,
    out_grad,
):
    ring = Ring()
    local_rows, width = tokens.shape
    head_dim = query_gain.shape[0]
    owners, groups = ring.owners, ring.groups
    heads_tp = query_proj.shape[1] // head_dim
    kv_tp = key_matrix.shape[1] // head_dim
    heads_here = heads_tp // owners
    heads_each_key = heads_tp // kv_tp
    sharers = heads_each_key // heads_here
    experts_here, _, each = gate_proj.shape
    expert_count = experts_here * owners
    picks = routes.shape[1]
    seq_len = local_rows * owners
    half_rows = local_rows // 2
    scale = head_dim ** (-0.5)
    e, f, t = ring.index, ring.group, ring.half
    key_head = (e * heads_here) // heads_each_key
    shared_index = e % sharers

    pair = groups == 2
    q_cols = heads_here * head_dim
    down = down_proj.reshape(experts_here * each, width)
    first = jnp.stack([e * experts_here, t * expert_count]).astype(jnp.int32)

    def attention_tables(places, piece_starts):
        group_places = lax.dynamic_slice_in_dim(places, f * seq_len, seq_len)
        by_slot = jnp.take(group_places.reshape(owners, 2, half_rows), ring.owners_by_slot, axis=0)
        order_places = jnp.concatenate(
            [
                lax.dynamic_index_in_dim(by_slot, t, 1, keepdims=False).reshape(-1),
                lax.dynamic_index_in_dim(by_slot, 1 - t, 1, keepdims=False).reshape(-1),
            ]
        )
        position = order_places % seq_len
        begins = lax.dynamic_slice_in_dim(piece_starts, f, 1)
        inside = (begins <= position[:, None]) & (position[:, None] < begins + PIECE)
        limit = jnp.maximum(
            position, jnp.max(jnp.where(inside, begins + (PIECE - 1), 0), axis=1)
        )
        half_dim = head_dim // 2
        freqs = jnp.exp(jnp.arange(half_dim, dtype=F32) * (-2.0 * LOG_THETA / head_dim))
        angles = position.astype(F32)[:, None] * freqs[None, :]
        cosine, sine = jnp.cos(angles), jnp.sin(angles)
        return (
            jnp.concatenate([cosine, cosine], axis=1),
            jnp.concatenate([-sine, sine], axis=1),
            query_gain[None, :],
            key_gain[None, :],
            position[None, :],
            limit[:, None],
        )

    grads_own = ring.own_rows(out_grad)
    payload = jnp.concatenate([grads_own, pad_lanes(ring.own_rows(routes).astype(BF16))], axis=1)
    stream = ring.own_rows(tokens).astype(F32)
    first_inverse = inverse_norm(stream)
    normed = stream * first_inverse
    made = {}

    def first_hook(step, walk):
        done = []
        if step == 0:
            made["cut"] = cut_weights(
                e, key_head, query_proj, key_matrix, value_matrix, out_proj, q_cols, head_dim
            )
            made["chunks"] = []
            if not pair:
                made["weights"] = (lax.all_gather(made["cut"], "fsdp", axis=0, tiled=True),)
        if pair:
            rows = made["cut"].shape[0] // ring.ahead
            chunk = made["cut"][step * rows : (step + 1) * rows]
            if step:
                chunk = after(chunk, walk.ahead)
            made["chunks"].append(ring.swap_groups(chunk))
            done.append(made["chunks"][-1])
        grads_walk.step(walk.ahead if step else None)
        done.append(grads_walk.ahead)
        if step == 1:
            made["tables"] = attention_tables(*after((places, piece_starts), walk.ahead))
            done += made["tables"][:4]
        if step == 2:
            done += made["tables"][4:]
        return tuple(done)

    grads_walk = ring.walk(payload)
    attn_in, _ = ring.gather((normed * attn_gain).astype(BF16), first_hook)
    if pair:
        made["weights"] = (made["cut"], jnp.concatenate(made["chunks"], axis=0))
    tables, weights = made["tables"], made["weights"]
    at = jnp.stack([f, 1 - f] if pair else [jnp.zeros_like(f)]).astype(jnp.int32)
    raw, query_low, key_low, value_low = project(at, attn_in, weights, heads_here, *tables[:4])
    low = (query_low, key_low, value_low)
    attn_other, lse_other, part_other = attend(at, 1, weights, *tables[4:], *low)
    attn_mine, lse_mine, part_mine = attend(at, 0, weights, *tables[4:], *low)
    grads_found = grads_walk.found
    grads_mine = jnp.concatenate(grads_found, axis=0)
    grads = (grads_mine, ring.swap_halves(grads_mine))
    their_rows = []

    def across(signal):
        if not pair:
            return []
        rows = ffn_in[0].shape[0] // ring.ahead
        start = len(their_rows) * rows
        their_rows.append(ring.swap_groups(after(ffn_in[0], signal)[start : start + rows]))
        return their_rows[-1:]

    def branch_hook(step, signal):
        if step != 1:
            return None
        made["router"] = ring.whole_rows(after(router, signal))
        made["lanes"] = pad_lanes(made["router"])
        return made["lanes"]

    residual = stream + ring.scatter(part_mine, part_other, branch_hook)
    whole_router, router_lanes = made["router"], made["lanes"]

    second_inverse = inverse_norm(residual)
    mid_normed = residual * second_inverse
    ffn_in, _ = ring.gather((mid_normed * ffn_gain).astype(BF16))
    if pair:
        their_grads = ring.swap_groups(grads_mine)
    weighted, hidden, gates, back_mine, back_other = experts(
        first, ffn_in, grads, gate_proj, up_proj, down_proj, router_lanes, picks, expert_count
    )

    if pair:
        made["grads"], back_mine = after((their_grads, back_mine), their_grads)
    layer_parts = []

    def back_hook(step, signal):
        layer_parts.append(layer_part(step, ring.ahead, after(weighted, signal), down))
        if step == 1 and pair:
            made["routed"] = (made["grads"], ring.swap_halves(made["grads"]))
        return tuple([layer_parts[-1]] + across(signal))

    back_sum = ring.scatter(back_mine, back_other, back_hook)

    gate_grad_rows = sum(
        back_sum[:, width + i * expert_count : width + (i + 1) * expert_count] for i in range(4)
    )
    own_gates = gates[:half_rows, :expert_count]
    picked_grad = own_gates * (
        gate_grad_rows - jnp.sum(own_gates * gate_grad_rows, axis=-1, keepdims=True)
    )
    logit_grad = picked_grad.astype(BF16)
    ffn_in_grad = back_sum[:, :width] + contract_cols(logit_grad, whole_router)
    ffn_gain_part = jnp.sum(ffn_in_grad * mid_normed, axis=0)
    second_normed_grad = ffn_in_grad * ffn_gain
    mid_grad = grads_own.astype(F32) + second_inverse * (
        second_normed_grad
        - mid_normed * jnp.mean(second_normed_grad * mid_normed, axis=-1, keepdims=True)
    )
    made["theirs"], made["other"] = [], []

    def other_hook(step, walk):
        done = []
        if step == 0:
            middle = len(layer_parts) // 2
            halves = [
                jnp.concatenate(part, axis=0) for part in (layer_parts[:middle], layer_parts[middle:])
            ]
            made["layer"] = Fold(ring, *after(halves, walk.ahead))
            made["layer"].step()
        else:
            made["layer"].step(walk.ahead)
        done.append(made["layer"].ahead)
        if pair and step == 0:
            rows = jnp.concatenate(after(their_rows, walk.ahead), axis=0)
            made["theirs"] = [rows, ring.swap_halves(rows)]
            done.append(rows)
        if pair and step % 2:
            x, g = after((made["theirs"][step // 2], made["routed"][step // 2]), walk.ahead)
            made["other"].append(
                other_experts(first, x, g, gate_proj, up_proj, down_proj, router_lanes, picks)
            )
            done += made["other"][-1]
        return tuple(done)

    branch, _ = ring.gather(
        jnp.concatenate([mid_grad.astype(BF16), pad_lanes(logit_grad)], axis=1), other_hook
    )
    layer_out = ring.join_halves((residual + made["layer"].result()).astype(BF16))

    attn_halves = (attn_mine, attn_other)
    out_theirs, out_arrived = ring.send_share(branch, attn_halves, width, BF16)
    raw_mine, raw_other, head_gains, in_mine, in_other = attend_back(
        at,
        branch if out_theirs is None else after(branch, out_theirs),
        weights,
        *tables,
        (raw, query_low, key_low, value_low, lse_mine, lse_other),
    )
    raw_halves = (raw_mine, raw_other)
    qkv_theirs, qkv_arrived = ring.send_share(attn_in, raw_halves, width, BF16)

    totals = {"gate_up": [], "down": []}

    def last_piece(n, signal):
        if n < experts_here:
            *totals["gate_up"], token = gate_up_grad(
                n,
                experts_here,
                totals["gate_up"],
                after(ffn_in, signal),
                made["theirs"],
                hidden,
                [part[1] for part in made["other"]],
            )
        else:
            *totals["down"], token = down_grad(
                n - experts_here,
                2,
                experts_here,
                totals["down"],
                after(weighted, signal),
                [part[0] for part in made["other"]],
                grads,
                made["routed"],
            )
        return [token]

    def in_hook(step, signal):
        done = []
        if step == 0:
            share = ring.add_share(out_arrived, after(branch, signal), attn_halves, width)
            made["out_walk"] = ring.walk(share.astype(BF16), True)
        else:
            made["out_walk"].step(signal)
        done.append(made["out_walk"].found[-1])
        if step == 1:
            made["qkv"] = ring.add_share(qkv_arrived, after(attn_in, signal), raw_halves, width)
            done.append(made["qkv"])
        if pair and step < 3:
            done += last_piece(step, signal)
        return tuple(done)

    if qkv_theirs is not None:
        in_mine = after(in_mine, qkv_theirs)
    attn_in_grad = ring.scatter(in_mine, in_other, in_hook)
    qkv_share = made["qkv"]
    first_normed_grad = attn_in_grad * attn_gain
    tokens_grad = mid_grad + first_inverse * (
        first_normed_grad - normed * jnp.mean(first_normed_grad * normed, axis=-1, keepdims=True)
    )
    tokens_grad = ring.join_halves(tokens_grad)
    attn_gain_part = jnp.sum(attn_in_grad * normed, axis=0)
    gains = ring.sum_all(
        jnp.concatenate([attn_gain_part, ffn_gain_part, head_gains[0], head_gains[1]])
    )

    kv_share = qkv_share[:, q_cols:]
    step = sharers // 2
    while step:
        rows = kv_share.shape[0] // 2
        bit = (shared_index // step) % 2
        pairs = [(i, i ^ step) for i in range(owners)]
        sent = lax.dynamic_slice_in_dim(kv_share, (1 - bit) * rows, rows)
        kept = lax.dynamic_slice_in_dim(kv_share, bit * rows, rows)
        kv_share = kept + ring.send(sent.astype(BF16), pairs).astype(F32)
        step //= 2
    own_share = jnp.concatenate([qkv_share[:, :q_cols], kv_share], axis=0).astype(BF16)

    last = ring.ahead - 1
    lanes_at = width // LANES

    share_rows = qkv_share.shape[0]
    shapes = [(share_rows, heads_tp * head_dim)] + [(share_rows, kv_tp * head_dim)] * 2

    def weight_hook(step, walk):
        signal = walk.ahead
        done = []
        if step == 0:
            made["out_walk"].step(signal)
            done += made["out_walk"].found[-1]
        if pair and step < 2:
            done += last_piece(step + 3, signal)
        if step == 1:
            _, arrived = ring.send_share(after(ffn_in, signal), branch, width, F32, LANES, lanes_at)
            made["router_arrived"] = arrived
            done += [] if arrived is None else [arrived]
        if step == 2:
            made["router_grad"] = ring.add_share(
                made["router_arrived"], after(ffn_in, signal), branch, width, LANES, lanes_at
            )
            done.append(made["router_grad"])
        if step == 2:
            found = made["out_walk"].found
            made["out_grad"] = place_wide(
                ring.owners_by_slot,
                [after(found[0], signal)] + found[1:-1] + list(found[-1]),
                heads_tp * head_dim,
            )
            done.append(made["out_grad"])
        if step == last:
            found = walk.found
            made["placed"] = place_blocks(
                ring.owners_by_slot, [after(found[0], signal)] + found[1:], shapes, sharers
            )
            done += made["placed"]
        return tuple(done)

    found = ring.blocks(own_share, weight_hook, True)
    out_grad_w = made["out_grad"]
    query_grad_w, key_grad_w, value_grad_w = place_last(
        ring.owners_by_slot[owners - 1], found[-1], made["placed"], sharers
    )
    router_grad = made["router_grad"][:, :expert_count]

    if pair:
        gate_total, up_total = totals["gate_up"]
        (down_total,) = totals["down"]
    else:
        all_rows, all_grads = ring.all_groups(ffn_in[0]), ring.all_groups(grads[0])

        def add_group(n, sums):
            gate_up, low = 0.0, 0.0
            for x, g in zip(all_rows, all_grads, strict=True):
                w, h = other_experts(
                    first, x[n], g[n], gate_proj, up_proj, down_proj, router_lanes, picks
                )
                gate_up = gate_up + contract_rows(x[n], h)
                low = low + contract_rows(w, g[n])[:, :width]
            gate_up = gate_up.reshape(width, experts_here, 2, each)
            return (
                sums[0] + jnp.swapaxes(gate_up[:, :, 0], 0, 1),
                sums[1] + jnp.swapaxes(gate_up[:, :, 1], 0, 1),
                sums[2] + low.reshape(experts_here, each, width),
            )

        gate_total, up_total, down_total = lax.fori_loop(
            0,
            groups,
            add_group,
            tuple(jnp.zeros(w.shape, F32) for w in (gate_proj, up_proj, down_proj)),
        )
    return (
        layer_out,
        tokens_grad,
        gains[:width],
        query_grad_w,
        key_grad_w,
        value_grad_w,
        out_grad_w,
        gains[2 * width : 2 * width + head_dim],
        gains[2 * width + head_dim :],
        gains[width : 2 * width],
        router_grad,
        gate_total,
        up_total,
        down_total,
    )


def solution(mesh):
    return jax.shard_map(
        body,
        mesh=mesh,
        in_specs=(
            P(("fsdp", "ep"), None),
            P(("fsdp", "ep"), None),
            P(),
            P(),
            P(),
            P("fsdp", "tp"),
            P("fsdp", "tp"),
            P("fsdp", "tp"),
            P("fsdp", "tp"),
            P(),
            P(),
            P(),
            P("fsdp", None),
            P("ep", None, "tp"),
            P("ep", None, "tp"),
            P("ep", "tp", None),
            P(("fsdp", "ep"), None),
        ),
        out_specs=(
            P(("fsdp", "ep"), None),
            P(("fsdp", "ep"), None),
            P(),
            P("fsdp", "tp"),
            P("fsdp", "tp"),
            P("fsdp", "tp"),
            P("fsdp", "tp"),
            P(),
            P(),
            P(),
            P("fsdp", None),
            P("ep", None, "tp"),
            P("ep", None, "tp"),
            P("ep", "tp", None),
        ),
        check_vma=False,
    )
```

```python
import functools
import math

import jax
import jax.numpy as jnp
import numpy as np
from jax import lax
from jax.experimental import pallas as pl
from jax.experimental.pallas import tpu as pltpu
from jax.sharding import PartitionSpec as P

PIECE = 256


EPSILON = 1e-06
LOG_THETA = math.log(1000000.0)
MASKED_SCORE = -1e30
LANES = 128
BF16 = jnp.bfloat16
F32 = jnp.float32


def inverse_norm(values):
    return lax.rsqrt(jnp.mean(values * values, axis=-1, keepdims=True) + EPSILON)


def dot(left, right):
    return jnp.dot(left, right, preferred_element_type=F32)


def contract_rows(left, right):
    return lax.dot_general(left, right, (((0,), (0,)), ((), ())), preferred_element_type=F32)


def contract_cols(left, right):
    return lax.dot_general(left, right, (((1,), (1,)), ((), ())), preferred_element_type=F32)


class Ring:
    def __init__(self):
        self.owners = lax.axis_size("ep")
        self.groups = lax.axis_size("fsdp")
        self.index = lax.axis_index("ep")
        self.group = lax.axis_index("fsdp")
        self.half = lax.axis_index("tp")
        n = self.owners
        if n == 8:
            order = [0, 2, 4, 6, 7, 5, 3, 1] if self.groups == 2 else [0, 1, 2, 3, 7, 6, 5, 4]
        else:
            order = list(range(n))
        self.forward = [(order[i], order[(i + 1) % n]) for i in range(n)]
        self.backward = [(dst, src) for src, dst in self.forward]
        self.ahead = n // 2
        self.behind = (n - 1) // 2
        offsets = [0]
        for step in range(1, self.ahead + 1):
            offsets.append(-step)
            if step <= self.behind:
                offsets.append(step)
        self.slot = {offset: place for place, offset in enumerate(offsets)}
        self.slot[self.ahead] = self.slot[-self.ahead] if n % 2 == 0 else self.slot[self.ahead]
        table = np.zeros((n, n), np.int32)
        for position, owner in enumerate(order):
            for place, offset in enumerate(offsets):
                table[owner, place] = order[(position + offset) % n]
        self.owners_by_slot = jnp.asarray(table)[self.index]

    def send(self, values, pairs, axis="ep"):
        return lax.ppermute(values, axis, pairs)

    def swap_halves(self, values):
        return self.send(values, [(0, 1), (1, 0)], "tp")

    def swap_groups(self, values):
        return self.send(values, [(0, 1), (1, 0)], "fsdp")

    def walk(self, own, even=False):
        return Walk(self, own, even)

    def blocks(self, own, hook=None, even=False):
        walk = Walk(self, own, even)
        for step in range(self.ahead):
            done = None if hook is None else hook(step, walk)
            walk.step()
            walk.hold(done)
        return walk.found

    def gather(self, own, hook=None):
        found = self.blocks(own, hook)
        mine = jnp.concatenate(found, axis=0)
        return (mine, self.swap_halves(mine)), found

    def scatter(self, mine, other, hook=None):
        fold = Fold(self, mine, other)
        for step in range(self.ahead):
            done = None if hook is None else hook(step, fold.ahead)
            fold.step(None, done)
        return fold.result()

    def own_rows(self, values):
        rows = values.shape[0] // 2
        return lax.dynamic_slice_in_dim(values, self.half * rows, rows)

    def join_halves(self, own):
        other = self.swap_halves(own)
        first = self.half == 0
        return jnp.concatenate([jnp.where(first, own, other), jnp.where(first, other, own)], axis=0)

    def whole_rows(self, own):
        if self.groups == 2:
            other = self.swap_groups(own)
            first = self.group == 0
            return jnp.concatenate(
                [jnp.where(first, own, other), jnp.where(first, other, own)], axis=0
            )
        return lax.all_gather(own, "fsdp", axis=0, tiled=True)

    def send_share(self, lefts, rights, width, kind, cols=None, block=0):
        if self.groups != 2:
            return None, None
        theirs = transposed_product(lefts, rights, width // 2, 1 - self.group, kind, cols, block)
        return theirs, self.swap_groups(theirs)

    def add_share(self, arrived, lefts, rights, width, cols=None, block=0):
        if self.groups == 2:
            ours = transposed_product(lefts, rights, width // 2, self.group, F32, cols, block)
            return ours + arrived.astype(F32)
        cols = cols or rights[0].shape[1]
        whole = contract_rows(
            jnp.concatenate(lefts, axis=0)[:, :width],
            jnp.concatenate(rights, axis=0)[:, block * cols : (block + 1) * cols],
        )
        return lax.psum_scatter(whole, "fsdp", scatter_dimension=0, tiled=True)

    def all_groups(self, mine):
        theirs = lax.all_gather(mine, "fsdp", axis=0)
        return theirs, self.swap_halves(theirs)

    def sum_all(self, values):
        for axis in ("ep", "fsdp", "tp"):
            step = 1
            while step < lax.axis_size(axis):
                pairs = [(i, i ^ step) for i in range(lax.axis_size(axis))]
                values = values + self.send(values, pairs, axis)
                step *= 2
        return values


def after(values, signal):
    return lax.optimization_barrier((values, signal))[0]


class Walk:
    def __init__(self, ring, own, even):
        self.ring, self.ahead, self.behind, self.even = ring, own, own, even
        self.found, self.count = [own], 0

    def hold(self, done):
        if done is not None:
            self.ahead, self.behind, self.found[-1] = after(
                (self.ahead, self.behind, self.found[-1]), done
            )

    def step(self, signal=None):
        ring = self.ring
        self.count += 1
        if signal is not None:
            self.ahead, self.behind = after((self.ahead, self.behind), signal)
        if self.count > ring.behind and self.even and ring.behind:
            cut = self.ahead.shape[0] // 2
            self.found.append(
                (
                    ring.send(self.ahead[:cut], ring.forward),
                    ring.send(self.behind[cut:], ring.backward),
                )
            )
            return
        self.ahead = ring.send(self.ahead, ring.forward)
        self.found.append(self.ahead)
        if self.count <= ring.behind:
            self.behind = ring.send(self.behind, ring.backward)
            self.found.append(self.behind)


class Fold:
    def __init__(self, ring, mine, other):
        mine = mine.astype(F32) + ring.swap_halves(other).astype(F32)
        self.ring = ring
        self.mine = mine.astype(BF16).reshape(ring.owners, -1, mine.shape[-1])
        self.ahead = self.mine[ring.slot[ring.ahead]]
        self.behind = self.mine[ring.slot[-ring.behind]] if ring.behind else None
        self.count = 0

    def block(self, offset):
        return self.mine[self.ring.slot[offset]].astype(F32)

    def step(self, signal=None, done=None):
        ring = self.ring
        self.count += 1
        if signal is not None:
            self.ahead = after(self.ahead, signal)
        offset = ring.ahead - self.count
        self.ahead = ring.send(self.ahead, ring.forward)
        if done is not None:
            self.ahead = after(self.ahead, done)
        if offset:
            self.ahead = (self.ahead.astype(F32) + self.block(offset)).astype(BF16)
        offset = ring.behind - self.count
        if offset >= 0:
            if signal is not None:
                self.behind = after(self.behind, signal)
            self.behind = ring.send(self.behind, ring.backward)
            if done is not None:
                self.behind = after(self.behind, done)
            if offset:
                self.behind = (self.behind.astype(F32) + self.block(-offset)).astype(BF16)

    def result(self):
        total = self.block(0) + self.ahead.astype(F32)
        return total if self.behind is None else total + self.behind.astype(F32)


def pad_lanes(values):
    return jnp.pad(values, ((0, 0), (0, LANES - values.shape[1])))


VMEM = pltpu.VMEM
SMEM = pltpu.SMEM
ROW_BLOCK = 256


def call(kernel, micros, **kwargs):
    return pl.pallas_call(
        kernel,
        compiler_params=pltpu.CompilerParams(vmem_limit_bytes=56 * 1024 * 1024),
        cost_estimate=pl.CostEstimate(
            flops=int(micros * 1.15e9), bytes_accessed=0, transcendentals=0
        ),
        **kwargs,
    )


def whole_spec():
    return pl.BlockSpec(memory_space=VMEM)


def turned(values):
    return pltpu.roll(values, values.shape[-1] // 2, 1)


def row_blocks(mine, other, step=ROW_BLOCK):
    half = mine.shape[0]
    for place, ref in enumerate((mine, other)):
        for start in range(0, half, step):
            yield ref, start, place * half + start


def cut_kernel(e_ref, q_ref, k_ref, v_ref, o_ref, out_ref):
    cols, dim = q_ref.shape[1], k_ref.shape[1]
    out_ref[:, :cols] = q_ref[...]
    out_ref[:, cols : cols + dim] = k_ref[...]
    out_ref[:, cols + dim : cols + 2 * dim] = v_ref[...]
    out_ref[:, cols + 2 * dim :] = o_ref[...]


def cut_weights(device, key_head, query_proj, key_matrix, value_matrix, out_proj, cols, dim):
    rows = query_proj.shape[0]
    heads = pl.BlockSpec((rows, cols), lambda i, e: (0, e[0]))
    key = pl.BlockSpec((rows, dim), lambda i, e: (0, e[1]))
    return call(
        cut_kernel,
        3,
        grid_spec=pltpu.PrefetchScalarGridSpec(
            num_scalar_prefetch=1,
            grid=(1,),
            in_specs=[heads, key, key, heads],
            out_specs=pl.BlockSpec((rows, 2 * cols + 2 * dim), lambda i, e: (0, 0)),
        ),
        out_shape=jax.ShapeDtypeStruct((rows, 2 * cols + 2 * dim), BF16),
    )(jnp.stack([device, key_head]).astype(jnp.int32), query_proj, key_matrix, value_matrix, out_proj)


def spots(at_ref, w_refs):
    rows = w_refs[0].shape[0]
    return [(pl.ds(pl.multiple_of(at_ref[i] * rows, rows), rows), ref) for i, ref in enumerate(w_refs)]


def project_kernel(
    heads, parts, at_ref, xm_ref, xo_ref, cos_ref, sin_ref, qg_ref, kg_ref, *refs
):
    w_refs, (raw_ref, ql_ref, kl_ref, vl_ref) = refs[:parts], refs[parts:]
    dim = qg_ref.shape[1]
    cols = heads * dim
    for ref, start, row in row_blocks(xm_ref, xo_ref):
        rows = slice(row, row + ROW_BLOCK)
        raw = sum(
            dot(ref[start : start + ROW_BLOCK, spot], w_ref[:, : cols + 2 * dim])
            for spot, w_ref in spots(at_ref, w_refs)
        )
        raw_ref[rows, :] = raw[:, : cols + dim]
        cosine, sine = cos_ref[rows, :], sin_ref[rows, :]
        for head in range(heads + 1):
            part = raw[:, head * dim : (head + 1) * dim]
            gain = qg_ref[...] if head < heads else kg_ref[...]
            part = part * inverse_norm(part) * gain
            part = (part * cosine + turned(part) * sine).astype(BF16)
            if head < heads:
                ql_ref[rows, head * dim : (head + 1) * dim] = part
            else:
                kl_ref[rows, :] = part
        vl_ref[rows, :] = raw[:, cols + dim :].astype(BF16)


def smem_spec():
    return pl.BlockSpec(memory_space=SMEM)


def project(at, x, weights, heads, cosine, sine, q_gain, k_gain):
    rows, dim = 2 * x[0].shape[0], q_gain.shape[1]
    cols = heads * dim
    return call(
        functools.partial(project_kernel, heads, len(weights)),
        7,
        in_specs=[smem_spec()] + [whole_spec()] * (6 + len(weights)),
        out_specs=[whole_spec()] * 4,
        out_shape=[
            jax.ShapeDtypeStruct((rows, cols + dim), F32),
            jax.ShapeDtypeStruct((rows, cols), BF16),
            jax.ShapeDtypeStruct((rows, dim), BF16),
            jax.ShapeDtypeStruct((rows, dim), BF16),
        ],
    )(at, *x, cosine, sine, q_gain, k_gain, *weights)


def attend_kernel(heads, base, parts, at_ref, pos_ref, lim_ref, ql_ref, kl_ref, vl_ref, *refs):
    w_refs, (out_ref, lse_ref, part_ref) = refs[:parts], refs[parts:]
    dim = kl_ref.shape[1]
    cols = heads * dim
    scale = dim ** (-0.5)
    for row in range(0, out_ref.shape[0], ROW_BLOCK):
        rows, among = slice(row, row + ROW_BLOCK), slice(base + row, base + row + ROW_BLOCK)
        allowed = pos_ref[...] <= lim_ref[among, :]
        for head in range(heads):
            cut = slice(head * dim, (head + 1) * dim)
            scores = contract_cols(ql_ref[among, cut], kl_ref[...]) * scale
            scores = jnp.where(allowed, scores, MASKED_SCORE)
            top = jnp.max(scores, axis=1, keepdims=True)
            powers = jnp.exp(scores - top)
            total = jnp.sum(powers, axis=1, keepdims=True)
            lse_ref[head, rows, :] = top + jnp.log(total)
            probs = (powers * (1.0 / total)).astype(BF16)
            out_ref[rows, cut] = dot(probs, vl_ref[...]).astype(BF16)
        for spot, w_ref in spots(at_ref, w_refs):
            part_ref[rows, spot] = contract_cols(
                out_ref[rows, :], w_ref[:, cols + 2 * dim :]
            ).astype(BF16)


def attend(at, place, weights, position, limit, query, key, value):
    rows, dim = key.shape
    cols = query.shape[1]
    half, width = rows // 2, sum(w.shape[0] for w in weights)
    heads = cols // dim
    return call(
        functools.partial(attend_kernel, heads, place * half, len(weights)),
        6.5,
        in_specs=[smem_spec()] + [whole_spec()] * (5 + len(weights)),
        out_specs=[whole_spec()] * 3,
        out_shape=[
            jax.ShapeDtypeStruct((half, cols), BF16),
            jax.ShapeDtypeStruct((heads, half, 1), F32),
            jax.ShapeDtypeStruct((half, width), BF16),
        ],
    )(at, position, limit, query, key, value, *weights)


def attend_back_kernel(
    heads,
    parts,
    at_ref,
    bm_ref,
    bo_ref,
    cos_ref,
    sin_ref,
    qg_ref,
    kg_ref,
    pos_ref,
    lim_ref,
    raw_ref,
    ql_ref,
    kl_ref,
    vl_ref,
    lm_ref,
    lo_ref,
    *refs,
):
    w_refs, (rm_ref, ro_ref, gains_ref, pm_ref, po_ref, dk_ref, dv_ref) = refs[:parts], refs[parts:]
    dim = qg_ref.shape[1]
    cols = heads * dim
    scale = dim ** (-0.5)
    q_part = jnp.zeros((1, dim), F32)
    k_part = jnp.zeros((1, dim), F32)

    def norm_back(grad, rows, raw, gain):
        inverse = inverse_norm(raw)
        unit = raw * inverse
        grad = grad * cos_ref[rows, :] - turned(grad) * sin_ref[rows, :]
        part = jnp.sum(grad * unit, axis=0, keepdims=True)
        grad = grad * gain
        return inverse * (grad - unit * jnp.mean(grad * unit, axis=1, keepdims=True)), part

    first = True
    for (ref, start, row), lse_ref, rg_ref in zip(
        row_blocks(bm_ref, bo_ref), (lm_ref, lm_ref, lo_ref, lo_ref), (rm_ref, rm_ref, ro_ref, ro_ref)
    ):
        rows, here = slice(row, row + ROW_BLOCK), slice(start, start + ROW_BLOCK)
        grads = sum(
            dot(ref[here, spot], w_ref[:, cols + 2 * dim :]) for spot, w_ref in spots(at_ref, w_refs)
        ).astype(BF16)
        allowed = pos_ref[...] <= lim_ref[rows, :]
        for head in range(heads):
            cut = slice(head * dim, (head + 1) * dim)
            query, value_grad = ql_ref[rows, cut], grads[:, cut]
            scores = contract_cols(query, kl_ref[...]) * scale
            probs = jnp.exp(jnp.where(allowed, scores - lse_ref[head, here, :], MASKED_SCORE))
            prob_grad = contract_cols(value_grad, vl_ref[...])
            weighed = probs * prob_grad
            delta = jnp.sum(weighed, axis=1, keepdims=True)
            score_grad = (weighed - probs * delta).astype(BF16)
            q_grad = dot(score_grad, kl_ref[...]) * scale
            k_more = contract_rows(query, score_grad)
            v_more = contract_rows(value_grad, probs.astype(BF16))
            if first:
                dk_ref[...] = k_more
                dv_ref[...] = v_more
                first = False
            else:
                dk_ref[...] += k_more
                dv_ref[...] += v_more
            q_raw_grad, part = norm_back(q_grad, rows, raw_ref[rows, cut], qg_ref[...])
            q_part = q_part + part
            rg_ref[here, cut] = q_raw_grad.astype(BF16)
    for (_, start, row), rg_ref, ref in zip(
        row_blocks(bm_ref, bo_ref),
        (rm_ref, rm_ref, ro_ref, ro_ref),
        (pm_ref, pm_ref, po_ref, po_ref),
    ):
        rows, here = slice(row, row + ROW_BLOCK), slice(start, start + ROW_BLOCK)
        k_grad = dk_ref[:, rows].T * scale
        k_raw_grad, part = norm_back(k_grad, rows, raw_ref[rows, cols : cols + dim], kg_ref[...])
        k_part = k_part + part
        rg_ref[here, cols : cols + dim] = k_raw_grad.astype(BF16)
        rg_ref[here, cols + dim :] = dv_ref[:, rows].T.astype(BF16)
        for spot, w_ref in spots(at_ref, w_refs):
            part = contract_cols(rg_ref[here, :], w_ref[:, : cols + 2 * dim]).astype(BF16)
            ref[here, spot] = part
    gains_ref[0:1, :] = q_part
    gains_ref[1:2, :] = k_part


def attend_back(at, branch, weights, cosine, sine, q_gain, k_gain, position, limit, saved):
    half = branch[0].shape[0]
    dim = q_gain.shape[1]
    width = sum(w.shape[0] for w in weights)
    cols = saved[1].shape[1]
    raw_half = jax.ShapeDtypeStruct((half, cols + 2 * dim), BF16)
    return call(
        functools.partial(attend_back_kernel, cols // dim, len(weights)),
        18.5,
        in_specs=[smem_spec()] + [whole_spec()] * (14 + len(weights)),
        out_specs=[whole_spec()] * 5,
        out_shape=[
            raw_half,
            raw_half,
            jax.ShapeDtypeStruct((2, dim), F32),
            jax.ShapeDtypeStruct((half, width), BF16),
            jax.ShapeDtypeStruct((half, width), BF16),
        ],
        scratch_shapes=[VMEM((dim, 2 * half), F32), VMEM((dim, 2 * half), F32)],
    )(at, *branch, cosine, sine, q_gain, k_gain, position, limit, *saved, *weights)


def routed_gates(x_ref, g_ref, router_ref, picks):
    lane = lax.broadcasted_iota(jnp.int32, (1, LANES), 1).astype(F32)
    logits = dot(x_ref[...], router_ref[...])
    names = g_ref[:, x_ref.shape[1] :].astype(F32)
    chosen = jnp.zeros(logits.shape, F32)
    for k in range(picks):
        chosen = jnp.where(names[:, k : k + 1] == lane, 1.0, chosen)
    logits = jnp.where(chosen > 0.0, logits, MASKED_SCORE)
    powers = chosen * jnp.exp(logits - jnp.max(logits, axis=1, keepdims=True))
    return powers / jnp.sum(powers, axis=1, keepdims=True)


def expert_values(x, g, gates, name, gate_up, down):
    each = down.shape[0]
    lane = lax.broadcasted_iota(jnp.int32, (1, LANES), 1)
    both = dot(x, gate_up)
    gate_val, up_val = both[:, :each], both[:, each:]
    grad = contract_cols(g, down)
    gate = jnp.sum(jnp.where(lane == name, gates, 0.0), axis=1, keepdims=True)
    sigmoid_val = 0.5 * jnp.tanh(0.5 * gate_val) + 0.5
    silu_val = gate_val * sigmoid_val
    act = silu_val * up_val
    act_grad = gate * grad
    gate_low = (act_grad * up_val * (sigmoid_val + silu_val * (1.0 - sigmoid_val))).astype(BF16)
    up_low = (act_grad * silu_val).astype(BF16)
    return (gate * act).astype(BF16), gate_low, up_low, act * grad


def experts_kernel(
    picks,
    expert_count,
    first_ref,
    xm_ref,
    xo_ref,
    gm_ref,
    go_ref,
    wg_ref,
    wu_ref,
    wd_ref,
    router_ref,
    weighted_ref,
    hidden_ref,
    gates_ref,
    pm_ref,
    po_ref,
    both_ref,
    side_ref,
):
    expert = pl.program_id(0)
    wide, width = xm_ref.shape
    each = wg_ref.shape[2]
    lane = lax.broadcasted_iota(jnp.int32, (1, LANES), 1)
    halves = ((xm_ref, gm_ref, pm_ref, 0), (xo_ref, go_ref, po_ref, wide))

    @pl.when(expert == 0)
    def _():
        for x_ref, g_ref, _, row in halves:
            gates_ref[row : row + wide, :] = routed_gates(x_ref, g_ref, router_ref, picks)

    name = first_ref[0] + expert
    place = first_ref[1] + name
    at = pl.multiple_of(expert * 2 * each, 2 * each)
    both_ref[:, pl.ds(at, each)] = wg_ref[0]
    both_ref[:, pl.ds(at + each, each)] = wu_ref[0]
    for x_ref, g_ref, _, row in halves:
        rows = slice(row, row + wide)
        weighted, gate_low, up_low, products = expert_values(
            x_ref[...],
            g_ref[:, :width],
            gates_ref[rows, :],
            name,
            both_ref[:, pl.ds(at, 2 * each)],
            wd_ref[0],
        )
        weighted_ref[rows, :] = weighted
        hidden_ref[rows, pl.ds(at, each)] = gate_low
        hidden_ref[rows, pl.ds(at + each, each)] = up_low
        row_grad = jnp.sum(products, axis=1, keepdims=True)
        high = row_grad.astype(BF16).astype(F32)
        side = jnp.where(lane == place, high, 0.0)
        side = side + jnp.where(lane == place + 2 * expert_count, row_grad - high, 0.0)
        side_ref[rows, :] = jnp.where(expert == 0, side, side_ref[rows, :] + side)

    @pl.when(expert == pl.num_programs(0) - 1)
    def _():
        for _, _, ref, row in halves:
            rows = slice(row, row + wide)
            ref[:, :width] = contract_cols(hidden_ref[rows, :], both_ref[...]).astype(BF16)
            ref[:, width:] = side_ref[rows, :].astype(BF16)


def experts(first, x, g, gate_proj, up_proj, down_proj, router, picks, expert_count):
    half, width = x[0].shape
    rows = 2 * half
    count, _, each = gate_proj.shape
    resident = lambda shape: pl.BlockSpec(
        shape, lambda i, first: (0,) * len(shape), pipeline_mode=pl.Buffered(1)
    )
    payload = (half, width + LANES)
    return call(
        functools.partial(experts_kernel, picks, expert_count),
        41,
        grid_spec=pltpu.PrefetchScalarGridSpec(
            num_scalar_prefetch=1,
            grid=(count,),
            in_specs=[resident((half, width))] * 2
            + [resident(payload)] * 2
            + [pl.BlockSpec((1, width, each), lambda i, first: (i, 0, 0))] * 2
            + [
                pl.BlockSpec((1, each, width), lambda i, first: (i, 0, 0)),
                resident((width, LANES)),
            ],
            out_specs=[
                pl.BlockSpec((rows, each), lambda i, first: (0, i)),
                resident((rows, 2 * count * each)),
                resident((rows, LANES)),
                resident(payload),
                resident(payload),
            ],
            scratch_shapes=[VMEM((width, 2 * count * each), BF16), VMEM((rows, LANES), F32)],
        ),
        out_shape=[
            jax.ShapeDtypeStruct((rows, count * each), BF16),
            jax.ShapeDtypeStruct((rows, 2 * count * each), BF16),
            jax.ShapeDtypeStruct((rows, LANES), F32),
            jax.ShapeDtypeStruct(payload, BF16),
            jax.ShapeDtypeStruct(payload, BF16),
        ],
    )(first, x[0], x[1], g[0], g[1], gate_proj, up_proj, down_proj, router)


def transposed_product_kernel(side_ref, am_ref, ao_ref, bm_ref, bo_ref, out_ref):
    total = contract_rows(am_ref[...], bm_ref[...]) + contract_rows(ao_ref[...], bo_ref[...])
    out_ref[...] = total.astype(out_ref.dtype)


def transposed_product(lefts, rights, share, side, kind, cols=None, block=0):
    half = rights[0].shape[0]
    cols = cols or rights[0].shape[1]
    left = pl.BlockSpec((half, share), lambda i, side: (0, side[0]))
    return call(
        transposed_product_kernel,
        4,
        grid_spec=pltpu.PrefetchScalarGridSpec(
            num_scalar_prefetch=1,
            grid=(1,),
            in_specs=[left, left] + [pl.BlockSpec((half, cols), lambda i, side: (0, block))] * 2,
            out_specs=pl.BlockSpec((share, cols), lambda i, side: (0, 0)),
        ),
        out_shape=jax.ShapeDtypeStruct((share, cols), kind),
    )(side.reshape(1).astype(jnp.int32), *lefts, *rights)


def layer_kernel(w_ref, d_ref, out_ref):
    out_ref[...] = dot(w_ref[...], d_ref[...]).astype(BF16)


def layer_part(part, parts, weighted, down):
    rows, hidden = weighted.shape
    width = down.shape[1]
    return call(
        layer_kernel,
        4,
        grid=(1,),
        in_specs=[
            pl.BlockSpec((rows // parts, hidden), lambda i: (part, 0)),
            pl.BlockSpec((hidden, width), lambda i: (0, 0)),
        ],
        out_specs=pl.BlockSpec((rows // parts, width), lambda i: (0, 0)),
        out_shape=jax.ShapeDtypeStruct((rows // parts, width), BF16),
    )(weighted, down)


def other_experts_kernel(
    picks, first_ref, x_ref, g_ref, wg_ref, wu_ref, wd_ref, router_ref, w_ref, h_ref, gates_ref
):
    expert = pl.program_id(0)
    width = x_ref.shape[1]
    each = wg_ref.shape[2]

    @pl.when(expert == 0)
    def _():
        gates_ref[...] = routed_gates(x_ref, g_ref, router_ref, picks)

    w_ref[...], h_ref[:, :each], h_ref[:, each:], _ = expert_values(
        x_ref[...],
        g_ref[:, :width],
        gates_ref[...],
        first_ref[0] + expert,
        jnp.concatenate([wg_ref[0], wu_ref[0]], axis=1),
        wd_ref[0],
    )


def other_experts(first, x, g, gate_proj, up_proj, down_proj, router, picks):
    rows, width = x.shape
    count, _, each = gate_proj.shape
    resident = lambda shape: pl.BlockSpec(
        shape, lambda i, first: (0,) * len(shape), pipeline_mode=pl.Buffered(1)
    )
    return call(
        functools.partial(other_experts_kernel, picks),
        15,
        grid_spec=pltpu.PrefetchScalarGridSpec(
            num_scalar_prefetch=1,
            grid=(count,),
            in_specs=[resident(x.shape), resident(g.shape)]
            + [pl.BlockSpec((1, width, each), lambda i, first: (i, 0, 0))] * 2
            + [
                pl.BlockSpec((1, each, width), lambda i, first: (i, 0, 0)),
                resident(router.shape),
            ],
            out_specs=[
                pl.BlockSpec((rows, each), lambda i, first: (0, i)),
                pl.BlockSpec((rows, 2 * each), lambda i, first: (0, i)),
            ],
            scratch_shapes=[VMEM((rows, LANES), F32)],
        ),
        out_shape=[
            jax.ShapeDtypeStruct((rows, count * each), BF16),
            jax.ShapeDtypeStruct((rows, 2 * count * each), BF16),
        ],
    )(first, x, g, gate_proj, up_proj, down_proj, router)


def in_halves(values, block, index):
    if isinstance(values, (tuple, list)):
        places = (0, 0)
    else:
        values, places = (values, values), (0, 1)
    specs = [
        pl.BlockSpec(block, lambda i, place=place: (place, index), pipeline_mode=pl.Buffered(1))
        for place in places
    ]
    return list(values), specs


def sign(token_ref):
    token_ref[...] = jnp.zeros(token_ref.shape, token_ref.dtype)


TOKEN = (8, LANES)


def product_sum(lefts, rights):
    parts = [contract_rows(left[...], right[...]) for left, right in zip(lefts, rights)]
    return parts[0] + parts[1]


def gate_up_grad_kernel(x0, x1, x2, x3, d0, d1, d2, d3, *refs):
    gate_ref, up_ref, token_ref = refs[-3:]
    each = gate_ref.shape[2]
    total = product_sum((x0, x1), (d0, d1)) + product_sum((x2, x3), (d2, d3))
    gate_ref[0] = total[:, :each]
    up_ref[0] = total[:, each:]
    sign(token_ref)


def gate_up_grad(expert, count, totals, own, other, own_hidden, other_hidden):
    half, width = own[0].shape
    each = own_hidden.shape[1] // 2 // count
    wide = 2 * ROW_BLOCK
    part = pl.BlockSpec((1, wide, each), lambda i: (expert, i, 0))
    rights, specs = in_halves(own_hidden, (half, 2 * each), expert)
    single = pl.Buffered(1)
    return call(
        gate_up_grad_kernel,
        11.7,
        grid=(width // wide,),
        in_specs=[pl.BlockSpec((half, wide), lambda i: (0, i))] * 4
        + specs
        + [pl.BlockSpec((half, 2 * each), lambda i: (0, expert), pipeline_mode=single)] * 2
        + [pl.BlockSpec(memory_space=pl.ANY)] * len(totals),
        out_specs=[part] * 2 + [pl.BlockSpec(TOKEN, lambda i: (0, 0))],
        out_shape=[jax.ShapeDtypeStruct((count, width, each), F32)] * 2
        + [jax.ShapeDtypeStruct(TOKEN, F32)],
        input_output_aliases={8: 0, 9: 1} if totals else {},
    )(*own, *other, *rights, *other_hidden, *totals)


def down_grad_kernel(count, w0, w1, g0, g1, g2, g3, w2, w3, *refs):
    out_ref, token_ref = refs[-2:]
    each = out_ref.shape[1]
    total = product_sum((w0, w1), (g0, g1)) + product_sum((w2, w3), (g2, g3))
    for i in range(count):
        out_ref[i] = total[i * each : (i + 1) * each, :]
    sign(token_ref)


def down_grad(part, parts, count, totals, own_weighted, other_weighted, own, other):
    half, width = own[0].shape[0], own[0].shape[1] - LANES
    hidden = own_weighted.shape[1]
    each = hidden // count
    wide = 2 * ROW_BLOCK
    steps = width // wide // parts
    right = pl.BlockSpec((half, wide), lambda i: (0, part * steps + i))
    place = pl.BlockSpec((count, each, wide), lambda i: (0, 0, part * steps + i))
    lefts, specs = in_halves(own_weighted, (half, hidden), 0)
    single = pl.Buffered(1)
    return call(
        functools.partial(down_grad_kernel, count),
        9.7,
        grid=(steps,),
        in_specs=specs
        + [right] * 4
        + [pl.BlockSpec((half, hidden), lambda i: (0, 0), pipeline_mode=single)] * 2
        + [pl.BlockSpec(memory_space=pl.ANY)] * len(totals),
        out_specs=[place, pl.BlockSpec(TOKEN, lambda i: (0, 0))],
        out_shape=[
            jax.ShapeDtypeStruct((count, each, width), F32),
            jax.ShapeDtypeStruct(TOKEN, F32),
        ],
        input_output_aliases={8: 0} if totals else {},
    )(*lefts, *own, *other, *other_weighted, *totals)


def place_wide_kernel(owners_ref, *refs):
    blocks, (last_top, last_low), out_ref = refs[:-3], refs[-3:-1], refs[-1]
    cols = blocks[0].shape[1]

    def put(slot, ref):
        at = pl.multiple_of(owners_ref[slot] * cols, cols)
        out_ref[:, pl.ds(at, cols)] = ref[...].astype(F32)

    for slot, ref in enumerate(blocks):
        put(slot, ref)
    top = pl.program_id(0) < pl.num_programs(0) // 2

    @pl.when(top)
    def _():
        put(len(blocks), last_top)

    @pl.when(jnp.logical_not(top))
    def _():
        put(len(blocks), last_low)


def place_wide(owners_by_slot, blocks, width):
    share, cols = blocks[0].shape
    steps = share // ROW_BLOCK
    half = steps // 2
    return call(
        place_wide_kernel,
        4,
        grid=(steps,),
        in_specs=[smem_spec()]
        + [pl.BlockSpec((ROW_BLOCK, cols), lambda i: (i, 0))] * (len(blocks) - 2)
        + [
            pl.BlockSpec((ROW_BLOCK, cols), lambda i: (jnp.minimum(i, half - 1), 0)),
            pl.BlockSpec((ROW_BLOCK, cols), lambda i: (jnp.maximum(i - half, 0), 0)),
        ],
        out_specs=pl.BlockSpec((ROW_BLOCK, width), lambda i: (i, 0)),
        out_shape=jax.ShapeDtypeStruct((share, width), F32),
    )(owners_by_slot, *blocks)


def place_kernel(sharers, owners_ref, *refs):
    count = (len(refs) - 3) // 2
    blocks, lows, (q_ref, k_ref, v_ref) = refs[:count], refs[count:-3], refs[-3:]
    cols = blocks[0].shape[1]
    dim = cols // 2
    for i, ref in enumerate(blocks):
        at = pl.multiple_of(owners_ref[i] * cols, cols)
        q_ref[:, pl.ds(at, cols)] = ref[...].astype(F32)

    @pl.when(pl.program_id(0) == 0)
    def _():
        for i, ref in enumerate(lows):
            rows = ref.shape[0]
            down = pl.multiple_of(owners_ref[i] % sharers * rows, rows)
            right = pl.multiple_of(owners_ref[i] // sharers * dim, dim)
            k_ref[pl.ds(down, rows), pl.ds(right, dim)] = ref[:, :dim].astype(F32)
            v_ref[pl.ds(down, rows), pl.ds(right, dim)] = ref[:, dim:].astype(F32)


def place_blocks(owners_by_slot, blocks, shapes, sharers):
    share, width = shapes[0]
    cols = blocks[0].shape[1]
    rows = blocks[0].shape[0] - share
    return call(
        functools.partial(place_kernel, sharers),
        5,
        grid=(share // ROW_BLOCK,),
        in_specs=[smem_spec()]
        + [pl.BlockSpec((ROW_BLOCK, cols), lambda i: (i, 0))] * len(blocks)
        + [pl.BlockSpec((rows, cols), lambda i: (share // rows, 0))] * len(blocks),
        out_specs=[
            pl.BlockSpec((ROW_BLOCK, width), lambda i: (i, 0)),
            pl.BlockSpec(shapes[1], lambda i: (0, 0)),
            pl.BlockSpec(shapes[2], lambda i: (0, 0)),
        ],
        out_shape=[jax.ShapeDtypeStruct(shape, F32) for shape in shapes],
    )(owners_by_slot, *blocks, *blocks)


def place_last_kernel(share, owner_ref, top_in, low_in, q_any, k_any, v_any, q_ref, k_ref, v_ref):
    dim = k_ref.shape[1]
    cut = top_in.shape[0]
    q_ref[:cut, :] = top_in[...].astype(F32)
    q_ref[cut:, :] = low_in[: share - cut, :].astype(F32)
    k_ref[...] = low_in[share - cut :, :dim].astype(F32)
    v_ref[...] = low_in[share - cut :, dim:].astype(F32)


def place_last(owner, halves, totals, sharers):
    share = totals[0].shape[0]
    top, low = halves
    cols = top.shape[1]
    rows = top.shape[0] + low.shape[0] - share
    spots = pl.BlockSpec((rows, cols // 2), lambda i, o: (o[0] % sharers, o[0] // sharers))
    return call(
        functools.partial(place_last_kernel, share),
        3,
        grid_spec=pltpu.PrefetchScalarGridSpec(
            num_scalar_prefetch=1,
            grid=(1,),
            in_specs=[
                pl.BlockSpec(top.shape, lambda i, o: (0, 0)),
                pl.BlockSpec(low.shape, lambda i, o: (0, 0)),
            ]
            + [pl.BlockSpec(memory_space=pl.ANY)] * 3,
            out_specs=[pl.BlockSpec((share, cols), lambda i, o: (0, o[0])), spots, spots],
        ),
        out_shape=[jax.ShapeDtypeStruct(total.shape, F32) for total in totals],
        input_output_aliases={3: 0, 4: 1, 5: 2},
    )(owner.reshape(1), top, low, *totals)


def body(
    tokens,
    routes,
    places,
    piece_starts,
    attn_gain,
    query_proj,
    key_matrix,
    value_matrix,
    out_proj,
    query_gain,
    key_gain,
    ffn_gain,
    router,
    gate_proj,
    up_proj,
    down_proj,
    out_grad,
):
    ring = Ring()
    local_rows, width = tokens.shape
    head_dim = query_gain.shape[0]
    owners, groups = ring.owners, ring.groups
    heads_tp = query_proj.shape[1] // head_dim
    kv_tp = key_matrix.shape[1] // head_dim
    heads_here = heads_tp // owners
    heads_each_key = heads_tp // kv_tp
    sharers = heads_each_key // heads_here
    experts_here, _, each = gate_proj.shape
    expert_count = experts_here * owners
    picks = routes.shape[1]
    seq_len = local_rows * owners
    half_rows = local_rows // 2
    scale = head_dim ** (-0.5)
    e, f, t = ring.index, ring.group, ring.half
    key_head = (e * heads_here) // heads_each_key
    shared_index = e % sharers

    pair = groups == 2
    q_cols = heads_here * head_dim
    down = down_proj.reshape(experts_here * each, width)
    first = jnp.stack([e * experts_here, t * expert_count]).astype(jnp.int32)

    def attention_tables(places, piece_starts):
        group_places = lax.dynamic_slice_in_dim(places, f * seq_len, seq_len)
        by_slot = jnp.take(group_places.reshape(owners, 2, half_rows), ring.owners_by_slot, axis=0)
        order_places = jnp.concatenate(
            [
                lax.dynamic_index_in_dim(by_slot, t, 1, keepdims=False).reshape(-1),
                lax.dynamic_index_in_dim(by_slot, 1 - t, 1, keepdims=False).reshape(-1),
            ]
        )
        position = order_places % seq_len
        begins = lax.dynamic_slice_in_dim(piece_starts, f, 1)
        inside = (begins <= position[:, None]) & (position[:, None] < begins + PIECE)
        limit = jnp.maximum(
            position, jnp.max(jnp.where(inside, begins + (PIECE - 1), 0), axis=1)
        )
        half_dim = head_dim // 2
        freqs = jnp.exp(jnp.arange(half_dim, dtype=F32) * (-2.0 * LOG_THETA / head_dim))
        angles = position.astype(F32)[:, None] * freqs[None, :]
        cosine, sine = jnp.cos(angles), jnp.sin(angles)
        return (
            jnp.concatenate([cosine, cosine], axis=1),
            jnp.concatenate([-sine, sine], axis=1),
            query_gain[None, :],
            key_gain[None, :],
            position[None, :],
            limit[:, None],
        )

    grads_own = ring.own_rows(out_grad)
    payload = jnp.concatenate([grads_own, pad_lanes(ring.own_rows(routes).astype(BF16))], axis=1)
    stream = ring.own_rows(tokens).astype(F32)
    first_inverse = inverse_norm(stream)
    normed = stream * first_inverse
    made = {}

    def first_hook(step, walk):
        done = []
        if step == 0:
            made["cut"] = cut_weights(
                e, key_head, query_proj, key_matrix, value_matrix, out_proj, q_cols, head_dim
            )
            made["chunks"] = []
            if not pair:
                made["weights"] = (lax.all_gather(made["cut"], "fsdp", axis=0, tiled=True),)
        if pair:
            rows = made["cut"].shape[0] // ring.ahead
            chunk = made["cut"][step * rows : (step + 1) * rows]
            if step:
                chunk = after(chunk, walk.ahead)
            made["chunks"].append(ring.swap_groups(chunk))
            done.append(made["chunks"][-1])
        grads_walk.step(walk.ahead if step else None)
        done.append(grads_walk.ahead)
        if step == 1:
            made["tables"] = attention_tables(*after((places, piece_starts), walk.ahead))
            done += made["tables"][:4]
        if step == 2:
            done += made["tables"][4:]
        return tuple(done)

    grads_walk = ring.walk(payload)
    attn_in, _ = ring.gather((normed * attn_gain).astype(BF16), first_hook)
    if pair:
        made["weights"] = (made["cut"], jnp.concatenate(made["chunks"], axis=0))
    tables, weights = made["tables"], made["weights"]
    at = jnp.stack([f, 1 - f] if pair else [jnp.zeros_like(f)]).astype(jnp.int32)
    raw, query_low, key_low, value_low = project(at, attn_in, weights, heads_here, *tables[:4])
    low = (query_low, key_low, value_low)
    attn_other, lse_other, part_other = attend(at, 1, weights, *tables[4:], *low)
    attn_mine, lse_mine, part_mine = attend(at, 0, weights, *tables[4:], *low)
    grads_found = grads_walk.found
    grads_mine = jnp.concatenate(grads_found, axis=0)
    grads = (grads_mine, ring.swap_halves(grads_mine))
    their_rows = []

    def across(signal):
        if not pair:
            return []
        rows = ffn_in[0].shape[0] // ring.ahead
        start = len(their_rows) * rows
        their_rows.append(ring.swap_groups(after(ffn_in[0], signal)[start : start + rows]))
        return their_rows[-1:]

    def branch_hook(step, signal):
        if step != 1:
            return None
        made["router"] = ring.whole_rows(after(router, signal))
        made["lanes"] = pad_lanes(made["router"])
        return made["lanes"]

    residual = stream + ring.scatter(part_mine, part_other, branch_hook)
    whole_router, router_lanes = made["router"], made["lanes"]

    second_inverse = inverse_norm(residual)
    mid_normed = residual * second_inverse
    ffn_in, _ = ring.gather((mid_normed * ffn_gain).astype(BF16))
    if pair:
        their_grads = ring.swap_groups(grads_mine)
    weighted, hidden, gates, back_mine, back_other = experts(
        first, ffn_in, grads, gate_proj, up_proj, down_proj, router_lanes, picks, expert_count
    )

    if pair:
        made["grads"], back_mine = after((their_grads, back_mine), their_grads)
    layer_parts = []

    def back_hook(step, signal):
        layer_parts.append(layer_part(step, ring.ahead, after(weighted, signal), down))
        if step == 1 and pair:
            made["routed"] = (made["grads"], ring.swap_halves(made["grads"]))
        earlier = their_rows[-1:]
        across(signal)
        return tuple([layer_parts[-1]] + earlier)

    back_sum = ring.scatter(back_mine, back_other, back_hook)

    gate_grad_rows = sum(
        back_sum[:, width + i * expert_count : width + (i + 1) * expert_count] for i in range(4)
    )
    own_gates = gates[:half_rows, :expert_count]
    picked_grad = own_gates * (
        gate_grad_rows - jnp.sum(own_gates * gate_grad_rows, axis=-1, keepdims=True)
    )
    logit_grad = picked_grad.astype(BF16)
    ffn_in_grad = back_sum[:, :width] + contract_cols(logit_grad, whole_router)
    ffn_gain_part = jnp.sum(ffn_in_grad * mid_normed, axis=0)
    second_normed_grad = ffn_in_grad * ffn_gain
    mid_grad = grads_own.astype(F32) + second_inverse * (
        second_normed_grad
        - mid_normed * jnp.mean(second_normed_grad * mid_normed, axis=-1, keepdims=True)
    )
    made["theirs"], made["other"] = [], []

    def other_hook(step, walk):
        done = []
        if step == 0:
            middle = len(layer_parts) // 2
            halves = [
                jnp.concatenate(part, axis=0) for part in (layer_parts[:middle], layer_parts[middle:])
            ]
            made["layer"] = Fold(ring, *after(halves, walk.ahead))
        else:
            made["layer"].step(walk.ahead)
        done.append(made["layer"].ahead)
        if pair and step == 1:
            rows = jnp.concatenate(after(their_rows, walk.ahead), axis=0)
            made["theirs"] = [rows, ring.swap_halves(rows)]
            done += made["theirs"]
        if pair and step >= ring.ahead - 2:
            half = step - (ring.ahead - 2)
            x, g = after((made["theirs"][half], made["routed"][half]), walk.ahead)
            made["other"].append(
                other_experts(first, x, g, gate_proj, up_proj, down_proj, router_lanes, picks)
            )
            done += made["other"][-1]
        return tuple(done)

    branch, _ = ring.gather(
        jnp.concatenate([mid_grad.astype(BF16), pad_lanes(logit_grad)], axis=1), other_hook
    )

    attn_halves = (attn_mine, attn_other)
    out_theirs, out_arrived = ring.send_share(branch, attn_halves, width, BF16)
    raw_mine, raw_other, head_gains, in_mine, in_other = attend_back(
        at,
        branch if out_theirs is None else after(branch, out_theirs),
        weights,
        *tables,
        (raw, query_low, key_low, value_low, lse_mine, lse_other),
    )
    raw_halves = (raw_mine, raw_other)
    qkv_theirs, qkv_arrived = ring.send_share(attn_in, raw_halves, width, BF16)

    totals = {"gate_up": [], "down": []}

    def last_piece(n, signal):
        if n < experts_here:
            *totals["gate_up"], token = gate_up_grad(
                n,
                experts_here,
                totals["gate_up"],
                after(ffn_in, signal),
                made["theirs"],
                hidden,
                [part[1] for part in made["other"]],
            )
        else:
            *totals["down"], token = down_grad(
                n - experts_here,
                2,
                experts_here,
                totals["down"],
                after(weighted, signal),
                [part[0] for part in made["other"]],
                grads,
                made["routed"],
            )
        return [token]

    def in_hook(step, signal):
        done = []
        if step == 0:
            made["layer"].step(signal)
            done.append(made["layer"].ahead)
            share = ring.add_share(out_arrived, after(branch, signal), attn_halves, width)
            made["out_walk"] = ring.walk(share.astype(BF16), True)
        else:
            made["out_walk"].step(signal)
        done.append(made["out_walk"].found[-1])
        if step == 1:
            made["qkv"] = ring.add_share(qkv_arrived, after(attn_in, signal), raw_halves, width)
            done.append(made["qkv"])
        if pair and step < 3:
            done += last_piece(step, signal)
        return tuple(done)

    if qkv_theirs is not None:
        in_mine = after(in_mine, qkv_theirs)
    attn_in_grad = ring.scatter(in_mine, in_other, in_hook)
    layer_out = ring.join_halves((residual + made["layer"].result()).astype(BF16))
    qkv_share = made["qkv"]
    first_normed_grad = attn_in_grad * attn_gain
    tokens_grad = mid_grad + first_inverse * (
        first_normed_grad - normed * jnp.mean(first_normed_grad * normed, axis=-1, keepdims=True)
    )
    tokens_grad = ring.join_halves(tokens_grad)
    attn_gain_part = jnp.sum(attn_in_grad * normed, axis=0)
    gains = ring.sum_all(
        jnp.concatenate([attn_gain_part, ffn_gain_part, head_gains[0], head_gains[1]])
    )

    kv_share = qkv_share[:, q_cols:]
    step = sharers // 2
    while step:
        rows = kv_share.shape[0] // 2
        bit = (shared_index // step) % 2
        pairs = [(i, i ^ step) for i in range(owners)]
        sent = lax.dynamic_slice_in_dim(kv_share, (1 - bit) * rows, rows)
        kept = lax.dynamic_slice_in_dim(kv_share, bit * rows, rows)
        kv_share = kept + ring.send(sent.astype(BF16), pairs).astype(F32)
        step //= 2
    own_share = jnp.concatenate([qkv_share[:, :q_cols], kv_share], axis=0).astype(BF16)

    last = ring.ahead - 1
    lanes_at = width // LANES

    share_rows = qkv_share.shape[0]
    shapes = [(share_rows, heads_tp * head_dim)] + [(share_rows, kv_tp * head_dim)] * 2

    def weight_hook(step, walk):
        signal = walk.ahead
        done = []
        if step == 0:
            made["out_walk"].step(signal)
            done += made["out_walk"].found[-1]
        if pair and step < 2:
            done += last_piece(step + 3, signal)
        if step == 1:
            _, arrived = ring.send_share(after(ffn_in, signal), branch, width, F32, LANES, lanes_at)
            made["router_arrived"] = arrived
            done += [] if arrived is None else [arrived]
        if step == 2:
            made["router_grad"] = ring.add_share(
                made["router_arrived"], after(ffn_in, signal), branch, width, LANES, lanes_at
            )
            done.append(made["router_grad"])
        if step == 2:
            found = made["out_walk"].found
            made["out_grad"] = place_wide(
                ring.owners_by_slot,
                [after(found[0], signal)] + found[1:-1] + list(found[-1]),
                heads_tp * head_dim,
            )
            done.append(made["out_grad"])
        if step == last:
            found = walk.found
            made["placed"] = place_blocks(
                ring.owners_by_slot, [after(found[0], signal)] + found[1:], shapes, sharers
            )
            done += made["placed"]
        return tuple(done)

    found = ring.blocks(own_share, weight_hook, True)
    out_grad_w = made["out_grad"]
    query_grad_w, key_grad_w, value_grad_w = place_last(
        ring.owners_by_slot[owners - 1], found[-1], made["placed"], sharers
    )
    router_grad = made["router_grad"][:, :expert_count]

    if pair:
        gate_total, up_total = totals["gate_up"]
        (down_total,) = totals["down"]
    else:
        all_rows, all_grads = ring.all_groups(ffn_in[0]), ring.all_groups(grads[0])

        def add_group(n, sums):
            gate_up, low = 0.0, 0.0
            for x, g in zip(all_rows, all_grads, strict=True):
                w, h = other_experts(
                    first, x[n], g[n], gate_proj, up_proj, down_proj, router_lanes, picks
                )
                gate_up = gate_up + contract_rows(x[n], h)
                low = low + contract_rows(w, g[n])[:, :width]
            gate_up = gate_up.reshape(width, experts_here, 2, each)
            return (
                sums[0] + jnp.swapaxes(gate_up[:, :, 0], 0, 1),
                sums[1] + jnp.swapaxes(gate_up[:, :, 1], 0, 1),
                sums[2] + low.reshape(experts_here, each, width),
            )

        gate_total, up_total, down_total = lax.fori_loop(
            0,
            groups,
            add_group,
            tuple(jnp.zeros(w.shape, F32) for w in (gate_proj, up_proj, down_proj)),
        )
    return (
        layer_out,
        tokens_grad,
        gains[:width],
        query_grad_w,
        key_grad_w,
        value_grad_w,
        out_grad_w,
        gains[2 * width : 2 * width + head_dim],
        gains[2 * width + head_dim :],
        gains[width : 2 * width],
        router_grad,
        gate_total,
        up_total,
        down_total,
    )


def solution(mesh):
    return jax.shard_map(
        body,
        mesh=mesh,
        in_specs=(
            P(("fsdp", "ep"), None),
            P(("fsdp", "ep"), None),
            P(),
            P(),
            P(),
            P("fsdp", "tp"),
            P("fsdp", "tp"),
            P("fsdp", "tp"),
            P("fsdp", "tp"),
            P(),
            P(),
            P(),
            P("fsdp", None),
            P("ep", None, "tp"),
            P("ep", None, "tp"),
            P("ep", "tp", None),
            P(("fsdp", "ep"), None),
        ),
        out_specs=(
            P(("fsdp", "ep"), None),
            P(("fsdp", "ep"), None),
            P(),
            P("fsdp", "tp"),
            P("fsdp", "tp"),
            P("fsdp", "tp"),
            P("fsdp", "tp"),
            P(),
            P(),
            P(),
            P("fsdp", None),
            P("ep", None, "tp"),
            P("ep", None, "tp"),
            P("ep", "tp", None),
        ),
        check_vma=False,
    )
```

```python
import functools
import math

import jax
import jax.numpy as jnp
import numpy as np
from jax import lax
from jax.experimental import pallas as pl
from jax.experimental.pallas import tpu as pltpu
from jax.sharding import PartitionSpec as P

PIECE = 256


EPSILON = 1e-06
LOG_THETA = math.log(1000000.0)
MASKED_SCORE = -1e30
LANES = 128
BF16 = jnp.bfloat16
F32 = jnp.float32


def inverse_norm(values):
    return lax.rsqrt(jnp.mean(values * values, axis=-1, keepdims=True) + EPSILON)


def dot(left, right):
    return jnp.dot(left, right, preferred_element_type=F32)


def contract_rows(left, right):
    return lax.dot_general(left, right, (((0,), (0,)), ((), ())), preferred_element_type=F32)


def contract_cols(left, right):
    return lax.dot_general(left, right, (((1,), (1,)), ((), ())), preferred_element_type=F32)


class Ring:
    def __init__(self):
        self.owners = lax.axis_size("ep")
        self.groups = lax.axis_size("fsdp")
        self.index = lax.axis_index("ep")
        self.group = lax.axis_index("fsdp")
        self.half = lax.axis_index("tp")
        n = self.owners
        if n == 8:
            order = [0, 2, 4, 6, 7, 5, 3, 1] if self.groups == 2 else [0, 1, 2, 3, 7, 6, 5, 4]
        else:
            order = list(range(n))
        self.forward = [(order[i], order[(i + 1) % n]) for i in range(n)]
        self.backward = [(dst, src) for src, dst in self.forward]
        self.ahead = n // 2
        self.behind = (n - 1) // 2
        offsets = [0]
        for step in range(1, self.ahead + 1):
            offsets.append(-step)
            if step <= self.behind:
                offsets.append(step)
        self.slot = {offset: place for place, offset in enumerate(offsets)}
        self.slot[self.ahead] = self.slot[-self.ahead] if n % 2 == 0 else self.slot[self.ahead]
        table = np.zeros((n, n), np.int32)
        for position, owner in enumerate(order):
            for place, offset in enumerate(offsets):
                table[owner, place] = order[(position + offset) % n]
        self.owners_by_slot = jnp.asarray(table)[self.index]

    def send(self, values, pairs, axis="ep"):
        return lax.ppermute(values, axis, pairs)

    def swap_halves(self, values):
        return self.send(values, [(0, 1), (1, 0)], "tp")

    def swap_groups(self, values):
        return self.send(values, [(0, 1), (1, 0)], "fsdp")

    def walk(self, own, even=False):
        return Walk(self, own, even)

    def blocks(self, own, hook=None, even=False):
        walk = Walk(self, own, even)
        for step in range(self.ahead):
            done = None if hook is None else hook(step, walk)
            walk.step()
            walk.hold(done)
        return walk.found

    def gather(self, own, hook=None):
        found = self.blocks(own, hook)
        mine = jnp.concatenate(found, axis=0)
        return (mine, self.swap_halves(mine)), found

    def scatter(self, mine, other, hook=None):
        fold = Fold(self, mine, other)
        for step in range(self.ahead):
            done = None if hook is None else hook(step, fold.ahead)
            fold.step(None, done)
        return fold.result()

    def own_rows(self, values):
        rows = values.shape[0] // 2
        return lax.dynamic_slice_in_dim(values, self.half * rows, rows)

    def join_halves(self, own):
        other = self.swap_halves(own)
        first = self.half == 0
        return jnp.concatenate([jnp.where(first, own, other), jnp.where(first, other, own)], axis=0)

    def whole_rows(self, own):
        if self.groups == 2:
            other = self.swap_groups(own)
            first = self.group == 0
            return jnp.concatenate(
                [jnp.where(first, own, other), jnp.where(first, other, own)], axis=0
            )
        return lax.all_gather(own, "fsdp", axis=0, tiled=True)

    def send_share(self, lefts, rights, width, kind, cols=None, block=0):
        if self.groups != 2:
            return None, None
        theirs = transposed_product(lefts, rights, width // 2, 1 - self.group, kind, cols, block)
        return theirs, self.swap_groups(theirs)

    def add_share(self, arrived, lefts, rights, width, cols=None, block=0):
        if self.groups == 2:
            ours = transposed_product(lefts, rights, width // 2, self.group, F32, cols, block)
            return ours + arrived.astype(F32)
        cols = cols or rights[0].shape[1]
        whole = contract_rows(
            jnp.concatenate(lefts, axis=0)[:, :width],
            jnp.concatenate(rights, axis=0)[:, block * cols : (block + 1) * cols],
        )
        return lax.psum_scatter(whole, "fsdp", scatter_dimension=0, tiled=True)

    def all_groups(self, mine):
        theirs = lax.all_gather(mine, "fsdp", axis=0)
        return theirs, self.swap_halves(theirs)

    def sum_all(self, values):
        for axis in ("tp", "fsdp", "ep"):
            step = 1
            while step < lax.axis_size(axis):
                pairs = [(i, i ^ step) for i in range(lax.axis_size(axis))]
                values = values + self.send(values, pairs, axis)
                step *= 2
        return values


def after(values, signal):
    return lax.optimization_barrier((values, signal))[0]


class Walk:
    def __init__(self, ring, own, even):
        self.ring, self.ahead, self.behind, self.even = ring, own, own, even
        self.found, self.count = [own], 0

    def hold(self, done):
        if done is not None:
            self.ahead, self.behind, self.found[-1] = after(
                (self.ahead, self.behind, self.found[-1]), done
            )

    def step(self, signal=None):
        ring = self.ring
        self.count += 1
        if signal is not None:
            self.ahead, self.behind = after((self.ahead, self.behind), signal)
        if self.count > ring.behind and self.even and ring.behind:
            cut = self.ahead.shape[0] // 2
            self.found.append(
                (
                    ring.send(self.ahead[:cut], ring.forward),
                    ring.send(self.behind[cut:], ring.backward),
                )
            )
            return
        self.ahead = ring.send(self.ahead, ring.forward)
        self.found.append(self.ahead)
        if self.count <= ring.behind:
            self.behind = ring.send(self.behind, ring.backward)
            self.found.append(self.behind)


class Fold:
    def __init__(self, ring, mine, other):
        mine = mine.astype(F32) + ring.swap_halves(other).astype(F32)
        self.ring = ring
        self.mine = mine.astype(BF16).reshape(ring.owners, -1, mine.shape[-1])
        self.ahead = self.mine[ring.slot[ring.ahead]]
        self.behind = self.mine[ring.slot[-ring.behind]] if ring.behind else None
        self.count = 0

    def block(self, offset):
        return self.mine[self.ring.slot[offset]].astype(F32)

    def step(self, signal=None, done=None):
        ring = self.ring
        self.count += 1
        if signal is not None:
            self.ahead = after(self.ahead, signal)
        offset = ring.ahead - self.count
        self.ahead = ring.send(self.ahead, ring.forward)
        if done is not None:
            self.ahead = after(self.ahead, done)
        if offset:
            self.ahead = (self.ahead.astype(F32) + self.block(offset)).astype(BF16)
        offset = ring.behind - self.count
        if offset >= 0:
            if signal is not None:
                self.behind = after(self.behind, signal)
            self.behind = ring.send(self.behind, ring.backward)
            if done is not None:
                self.behind = after(self.behind, done)
            if offset:
                self.behind = (self.behind.astype(F32) + self.block(-offset)).astype(BF16)

    def result(self):
        total = self.block(0) + self.ahead.astype(F32)
        return total if self.behind is None else total + self.behind.astype(F32)


def pad_lanes(values):
    return jnp.pad(values, ((0, 0), (0, LANES - values.shape[1])))


VMEM = pltpu.VMEM
SMEM = pltpu.SMEM
ROW_BLOCK = 256


def call(kernel, micros, **kwargs):
    return pl.pallas_call(
        kernel,
        compiler_params=pltpu.CompilerParams(vmem_limit_bytes=56 * 1024 * 1024),
        cost_estimate=pl.CostEstimate(
            flops=int(micros * 1.15e9), bytes_accessed=0, transcendentals=0
        ),
        **kwargs,
    )


def whole_spec():
    return pl.BlockSpec(memory_space=VMEM)


def turned(values):
    return pltpu.roll(values, values.shape[-1] // 2, 1)


def row_blocks(mine, other, step=ROW_BLOCK):
    half = mine.shape[0]
    for place, ref in enumerate((mine, other)):
        for start in range(0, half, step):
            yield ref, start, place * half + start


def cut_kernel(e_ref, q_ref, k_ref, v_ref, o_ref, out_ref):
    cols, dim = q_ref.shape[1], k_ref.shape[1]
    out_ref[:, :cols] = q_ref[...]
    out_ref[:, cols : cols + dim] = k_ref[...]
    out_ref[:, cols + dim : cols + 2 * dim] = v_ref[...]
    out_ref[:, cols + 2 * dim :] = o_ref[...]


def cut_weights(device, key_head, query_proj, key_matrix, value_matrix, out_proj, cols, dim):
    rows = query_proj.shape[0]
    heads = pl.BlockSpec((rows, cols), lambda i, e: (0, e[0]))
    key = pl.BlockSpec((rows, dim), lambda i, e: (0, e[1]))
    return call(
        cut_kernel,
        3,
        grid_spec=pltpu.PrefetchScalarGridSpec(
            num_scalar_prefetch=1,
            grid=(1,),
            in_specs=[heads, key, key, heads],
            out_specs=pl.BlockSpec((rows, 2 * cols + 2 * dim), lambda i, e: (0, 0)),
        ),
        out_shape=jax.ShapeDtypeStruct((rows, 2 * cols + 2 * dim), BF16),
    )(jnp.stack([device, key_head]).astype(jnp.int32), query_proj, key_matrix, value_matrix, out_proj)


def spots(at_ref, w_refs):
    rows = w_refs[0].shape[0]
    return [(pl.ds(pl.multiple_of(at_ref[i] * rows, rows), rows), ref) for i, ref in enumerate(w_refs)]


def project_kernel(
    heads, parts, at_ref, xm_ref, xo_ref, cos_ref, sin_ref, qg_ref, kg_ref, *refs
):
    w_refs, (raw_ref, ql_ref, kl_ref, vl_ref) = refs[:parts], refs[parts:]
    dim = qg_ref.shape[1]
    cols = heads * dim
    for ref, start, row in row_blocks(xm_ref, xo_ref):
        rows = slice(row, row + ROW_BLOCK)
        raw = sum(
            dot(ref[start : start + ROW_BLOCK, spot], w_ref[:, : cols + 2 * dim])
            for spot, w_ref in spots(at_ref, w_refs)
        )
        raw_ref[rows, :] = raw[:, : cols + dim]
        cosine, sine = cos_ref[rows, :], sin_ref[rows, :]
        for head in range(heads + 1):
            part = raw[:, head * dim : (head + 1) * dim]
            gain = qg_ref[...] if head < heads else kg_ref[...]
            part = part * inverse_norm(part) * gain
            part = (part * cosine + turned(part) * sine).astype(BF16)
            if head < heads:
                ql_ref[rows, head * dim : (head + 1) * dim] = part
            else:
                kl_ref[rows, :] = part
        vl_ref[rows, :] = raw[:, cols + dim :].astype(BF16)


def smem_spec():
    return pl.BlockSpec(memory_space=SMEM)


def project(at, x, weights, heads, cosine, sine, q_gain, k_gain):
    rows, dim = 2 * x[0].shape[0], q_gain.shape[1]
    cols = heads * dim
    return call(
        functools.partial(project_kernel, heads, len(weights)),
        7,
        in_specs=[smem_spec()] + [whole_spec()] * (6 + len(weights)),
        out_specs=[whole_spec()] * 4,
        out_shape=[
            jax.ShapeDtypeStruct((rows, cols + dim), F32),
            jax.ShapeDtypeStruct((rows, cols), BF16),
            jax.ShapeDtypeStruct((rows, dim), BF16),
            jax.ShapeDtypeStruct((rows, dim), BF16),
        ],
    )(at, *x, cosine, sine, q_gain, k_gain, *weights)


def attend_kernel(heads, base, parts, at_ref, pos_ref, lim_ref, ql_ref, kl_ref, vl_ref, *refs):
    w_refs, (out_ref, lse_ref, part_ref) = refs[:parts], refs[parts:]
    dim = kl_ref.shape[1]
    cols = heads * dim
    scale = dim ** (-0.5)
    for row in range(0, out_ref.shape[0], ROW_BLOCK):
        rows, among = slice(row, row + ROW_BLOCK), slice(base + row, base + row + ROW_BLOCK)
        allowed = pos_ref[...] <= lim_ref[among, :]
        for head in range(heads):
            cut = slice(head * dim, (head + 1) * dim)
            scores = contract_cols(ql_ref[among, cut], kl_ref[...]) * scale
            scores = jnp.where(allowed, scores, MASKED_SCORE)
            top = jnp.max(scores, axis=1, keepdims=True)
            powers = jnp.exp(scores - top)
            total = jnp.sum(powers, axis=1, keepdims=True)
            lse_ref[head, rows, :] = top + jnp.log(total)
            probs = (powers * (1.0 / total)).astype(BF16)
            out_ref[rows, cut] = dot(probs, vl_ref[...]).astype(BF16)
        for spot, w_ref in spots(at_ref, w_refs):
            part_ref[rows, spot] = contract_cols(
                out_ref[rows, :], w_ref[:, cols + 2 * dim :]
            ).astype(BF16)


def attend(at, place, weights, position, limit, query, key, value):
    rows, dim = key.shape
    cols = query.shape[1]
    half, width = rows // 2, sum(w.shape[0] for w in weights)
    heads = cols // dim
    return call(
        functools.partial(attend_kernel, heads, place * half, len(weights)),
        6.5,
        in_specs=[smem_spec()] + [whole_spec()] * (5 + len(weights)),
        out_specs=[whole_spec()] * 3,
        out_shape=[
            jax.ShapeDtypeStruct((half, cols), BF16),
            jax.ShapeDtypeStruct((heads, half, 1), F32),
            jax.ShapeDtypeStruct((half, width), BF16),
        ],
    )(at, position, limit, query, key, value, *weights)


def attend_back_kernel(
    heads,
    parts,
    at_ref,
    bm_ref,
    bo_ref,
    cos_ref,
    sin_ref,
    qg_ref,
    kg_ref,
    pos_ref,
    lim_ref,
    raw_ref,
    ql_ref,
    kl_ref,
    vl_ref,
    lm_ref,
    lo_ref,
    *refs,
):
    w_refs, (rm_ref, ro_ref, gains_ref, pm_ref, po_ref, dk_ref, dv_ref) = refs[:parts], refs[parts:]
    dim = qg_ref.shape[1]
    cols = heads * dim
    scale = dim ** (-0.5)
    q_part = jnp.zeros((1, dim), F32)
    k_part = jnp.zeros((1, dim), F32)

    def norm_back(grad, rows, raw, gain):
        inverse = inverse_norm(raw)
        unit = raw * inverse
        grad = grad * cos_ref[rows, :] - turned(grad) * sin_ref[rows, :]
        part = jnp.sum(grad * unit, axis=0, keepdims=True)
        grad = grad * gain
        return inverse * (grad - unit * jnp.mean(grad * unit, axis=1, keepdims=True)), part

    first = True
    for (ref, start, row), lse_ref, rg_ref in zip(
        row_blocks(bm_ref, bo_ref), (lm_ref, lm_ref, lo_ref, lo_ref), (rm_ref, rm_ref, ro_ref, ro_ref)
    ):
        rows, here = slice(row, row + ROW_BLOCK), slice(start, start + ROW_BLOCK)
        grads = sum(
            dot(ref[here, spot], w_ref[:, cols + 2 * dim :]) for spot, w_ref in spots(at_ref, w_refs)
        ).astype(BF16)
        allowed = pos_ref[...] <= lim_ref[rows, :]
        for head in range(heads):
            cut = slice(head * dim, (head + 1) * dim)
            query, value_grad = ql_ref[rows, cut], grads[:, cut]
            scores = contract_cols(query, kl_ref[...]) * scale
            probs = jnp.exp(jnp.where(allowed, scores - lse_ref[head, here, :], MASKED_SCORE))
            prob_grad = contract_cols(value_grad, vl_ref[...])
            weighed = probs * prob_grad
            delta = jnp.sum(weighed, axis=1, keepdims=True)
            score_grad = (weighed - probs * delta).astype(BF16)
            q_grad = dot(score_grad, kl_ref[...]) * scale
            k_more = contract_rows(query, score_grad)
            v_more = contract_rows(value_grad, probs.astype(BF16))
            if first:
                dk_ref[...] = k_more
                dv_ref[...] = v_more
                first = False
            else:
                dk_ref[...] += k_more
                dv_ref[...] += v_more
            q_raw_grad, part = norm_back(q_grad, rows, raw_ref[rows, cut], qg_ref[...])
            q_part = q_part + part
            rg_ref[here, cut] = q_raw_grad.astype(BF16)
    for (_, start, row), rg_ref, ref in zip(
        row_blocks(bm_ref, bo_ref),
        (rm_ref, rm_ref, ro_ref, ro_ref),
        (pm_ref, pm_ref, po_ref, po_ref),
    ):
        rows, here = slice(row, row + ROW_BLOCK), slice(start, start + ROW_BLOCK)
        k_grad = dk_ref[:, rows].T * scale
        k_raw_grad, part = norm_back(k_grad, rows, raw_ref[rows, cols : cols + dim], kg_ref[...])
        k_part = k_part + part
        rg_ref[here, cols : cols + dim] = k_raw_grad.astype(BF16)
        rg_ref[here, cols + dim :] = dv_ref[:, rows].T.astype(BF16)
        for spot, w_ref in spots(at_ref, w_refs):
            part = contract_cols(rg_ref[here, :], w_ref[:, : cols + 2 * dim]).astype(BF16)
            ref[here, spot] = part
    gains_ref[0:1, :] = q_part
    gains_ref[1:2, :] = k_part


def attend_back(at, branch, weights, cosine, sine, q_gain, k_gain, position, limit, saved):
    half = branch[0].shape[0]
    dim = q_gain.shape[1]
    width = sum(w.shape[0] for w in weights)
    cols = saved[1].shape[1]
    raw_half = jax.ShapeDtypeStruct((half, cols + 2 * dim), BF16)
    return call(
        functools.partial(attend_back_kernel, cols // dim, len(weights)),
        18.5,
        in_specs=[smem_spec()] + [whole_spec()] * (14 + len(weights)),
        out_specs=[whole_spec()] * 5,
        out_shape=[
            raw_half,
            raw_half,
            jax.ShapeDtypeStruct((2, dim), F32),
            jax.ShapeDtypeStruct((half, width), BF16),
            jax.ShapeDtypeStruct((half, width), BF16),
        ],
        scratch_shapes=[VMEM((dim, 2 * half), F32), VMEM((dim, 2 * half), F32)],
    )(at, *branch, cosine, sine, q_gain, k_gain, position, limit, *saved, *weights)


def routed_gates(x_ref, g_ref, router_ref, picks):
    lane = lax.broadcasted_iota(jnp.int32, (1, LANES), 1).astype(F32)
    logits = dot(x_ref[...], router_ref[...])
    names = g_ref[:, x_ref.shape[1] :].astype(F32)
    chosen = jnp.zeros(logits.shape, F32)
    for k in range(picks):
        chosen = jnp.where(names[:, k : k + 1] == lane, 1.0, chosen)
    logits = jnp.where(chosen > 0.0, logits, MASKED_SCORE)
    powers = chosen * jnp.exp(logits - jnp.max(logits, axis=1, keepdims=True))
    return powers / jnp.sum(powers, axis=1, keepdims=True)


def expert_values(x, g, gates, name, gate_up, down):
    each = down.shape[0]
    lane = lax.broadcasted_iota(jnp.int32, (1, LANES), 1)
    both = dot(x, gate_up)
    gate_val, up_val = both[:, :each], both[:, each:]
    grad = contract_cols(g, down)
    gate = jnp.sum(jnp.where(lane == name, gates, 0.0), axis=1, keepdims=True)
    sigmoid_val = 0.5 * jnp.tanh(0.5 * gate_val) + 0.5
    silu_val = gate_val * sigmoid_val
    act = silu_val * up_val
    act_grad = gate * grad
    gate_low = (act_grad * up_val * (sigmoid_val + silu_val * (1.0 - sigmoid_val))).astype(BF16)
    up_low = (act_grad * silu_val).astype(BF16)
    return (gate * act).astype(BF16), gate_low, up_low, act * grad


def experts_kernel(
    picks,
    expert_count,
    first_ref,
    xm_ref,
    xo_ref,
    gm_ref,
    go_ref,
    wg_ref,
    wu_ref,
    wd_ref,
    router_ref,
    weighted_ref,
    hidden_ref,
    gates_ref,
    pm_ref,
    po_ref,
    both_ref,
    side_ref,
):
    expert = pl.program_id(0)
    wide, width = xm_ref.shape
    each = wg_ref.shape[2]
    lane = lax.broadcasted_iota(jnp.int32, (1, LANES), 1)
    halves = ((xm_ref, gm_ref, pm_ref, 0), (xo_ref, go_ref, po_ref, wide))

    @pl.when(expert == 0)
    def _():
        for x_ref, g_ref, _, row in halves:
            gates_ref[row : row + wide, :] = routed_gates(x_ref, g_ref, router_ref, picks)

    name = first_ref[0] + expert
    place = first_ref[1] + name
    at = pl.multiple_of(expert * 2 * each, 2 * each)
    both_ref[:, pl.ds(at, each)] = wg_ref[0]
    both_ref[:, pl.ds(at + each, each)] = wu_ref[0]
    for x_ref, g_ref, _, row in halves:
        rows = slice(row, row + wide)
        weighted, gate_low, up_low, products = expert_values(
            x_ref[...],
            g_ref[:, :width],
            gates_ref[rows, :],
            name,
            both_ref[:, pl.ds(at, 2 * each)],
            wd_ref[0],
        )
        weighted_ref[rows, :] = weighted
        hidden_ref[rows, pl.ds(at, each)] = gate_low
        hidden_ref[rows, pl.ds(at + each, each)] = up_low
        row_grad = jnp.sum(products, axis=1, keepdims=True)
        high = row_grad.astype(BF16).astype(F32)
        side = jnp.where(lane == place, high, 0.0)
        side = side + jnp.where(lane == place + 2 * expert_count, row_grad - high, 0.0)
        side_ref[rows, :] = jnp.where(expert == 0, side, side_ref[rows, :] + side)

    @pl.when(expert == pl.num_programs(0) - 1)
    def _():
        for _, _, ref, row in halves:
            rows = slice(row, row + wide)
            ref[:, :width] = contract_cols(hidden_ref[rows, :], both_ref[...]).astype(BF16)
            ref[:, width:] = side_ref[rows, :].astype(BF16)


def experts(first, x, g, gate_proj, up_proj, down_proj, router, picks, expert_count):
    half, width = x[0].shape
    rows = 2 * half
    count, _, each = gate_proj.shape
    resident = lambda shape: pl.BlockSpec(
        shape, lambda i, first: (0,) * len(shape), pipeline_mode=pl.Buffered(1)
    )
    payload = (half, width + LANES)
    return call(
        functools.partial(experts_kernel, picks, expert_count),
        41,
        grid_spec=pltpu.PrefetchScalarGridSpec(
            num_scalar_prefetch=1,
            grid=(count,),
            in_specs=[resident((half, width))] * 2
            + [resident(payload)] * 2
            + [pl.BlockSpec((1, width, each), lambda i, first: (i, 0, 0))] * 2
            + [
                pl.BlockSpec((1, each, width), lambda i, first: (i, 0, 0)),
                resident((width, LANES)),
            ],
            out_specs=[
                pl.BlockSpec((rows, each), lambda i, first: (0, i)),
                resident((rows, 2 * count * each)),
                resident((rows, LANES)),
                resident(payload),
                resident(payload),
            ],
            scratch_shapes=[VMEM((width, 2 * count * each), BF16), VMEM((rows, LANES), F32)],
        ),
        out_shape=[
            jax.ShapeDtypeStruct((rows, count * each), BF16),
            jax.ShapeDtypeStruct((rows, 2 * count * each), BF16),
            jax.ShapeDtypeStruct((rows, LANES), F32),
            jax.ShapeDtypeStruct(payload, BF16),
            jax.ShapeDtypeStruct(payload, BF16),
        ],
    )(first, x[0], x[1], g[0], g[1], gate_proj, up_proj, down_proj, router)


def transposed_product_kernel(side_ref, am_ref, ao_ref, bm_ref, bo_ref, out_ref):
    total = contract_rows(am_ref[...], bm_ref[...]) + contract_rows(ao_ref[...], bo_ref[...])
    out_ref[...] = total.astype(out_ref.dtype)


def transposed_product(lefts, rights, share, side, kind, cols=None, block=0):
    half = rights[0].shape[0]
    cols = cols or rights[0].shape[1]
    left = pl.BlockSpec((half, share), lambda i, side: (0, side[0]))
    return call(
        transposed_product_kernel,
        4,
        grid_spec=pltpu.PrefetchScalarGridSpec(
            num_scalar_prefetch=1,
            grid=(1,),
            in_specs=[left, left] + [pl.BlockSpec((half, cols), lambda i, side: (0, block))] * 2,
            out_specs=pl.BlockSpec((share, cols), lambda i, side: (0, 0)),
        ),
        out_shape=jax.ShapeDtypeStruct((share, cols), kind),
    )(side.reshape(1).astype(jnp.int32), *lefts, *rights)


def layer_kernel(w_ref, d_ref, out_ref):
    out_ref[...] = dot(w_ref[...], d_ref[...]).astype(BF16)


def layer_part(part, parts, weighted, down):
    rows, hidden = weighted.shape
    width = down.shape[1]
    return call(
        layer_kernel,
        4,
        grid=(1,),
        in_specs=[
            pl.BlockSpec((rows // parts, hidden), lambda i: (part, 0)),
            pl.BlockSpec((hidden, width), lambda i: (0, 0)),
        ],
        out_specs=pl.BlockSpec((rows // parts, width), lambda i: (0, 0)),
        out_shape=jax.ShapeDtypeStruct((rows // parts, width), BF16),
    )(weighted, down)


def other_experts_kernel(
    picks, first_ref, x_ref, g_ref, wg_ref, wu_ref, wd_ref, router_ref, w_ref, h_ref, gates_ref
):
    expert = pl.program_id(0)
    width = x_ref.shape[1]
    each = wg_ref.shape[2]

    @pl.when(expert == 0)
    def _():
        gates_ref[...] = routed_gates(x_ref, g_ref, router_ref, picks)

    w_ref[...], h_ref[:, :each], h_ref[:, each:], _ = expert_values(
        x_ref[...],
        g_ref[:, :width],
        gates_ref[...],
        first_ref[0] + expert,
        jnp.concatenate([wg_ref[0], wu_ref[0]], axis=1),
        wd_ref[0],
    )


def other_experts(first, x, g, gate_proj, up_proj, down_proj, router, picks):
    rows, width = x.shape
    count, _, each = gate_proj.shape
    resident = lambda shape: pl.BlockSpec(
        shape, lambda i, first: (0,) * len(shape), pipeline_mode=pl.Buffered(1)
    )
    return call(
        functools.partial(other_experts_kernel, picks),
        15,
        grid_spec=pltpu.PrefetchScalarGridSpec(
            num_scalar_prefetch=1,
            grid=(count,),
            in_specs=[resident(x.shape), resident(g.shape)]
            + [pl.BlockSpec((1, width, each), lambda i, first: (i, 0, 0))] * 2
            + [
                pl.BlockSpec((1, each, width), lambda i, first: (i, 0, 0)),
                resident(router.shape),
            ],
            out_specs=[
                pl.BlockSpec((rows, each), lambda i, first: (0, i)),
                pl.BlockSpec((rows, 2 * each), lambda i, first: (0, i)),
            ],
            scratch_shapes=[VMEM((rows, LANES), F32)],
        ),
        out_shape=[
            jax.ShapeDtypeStruct((rows, count * each), BF16),
            jax.ShapeDtypeStruct((rows, 2 * count * each), BF16),
        ],
    )(first, x, g, gate_proj, up_proj, down_proj, router)


def in_halves(values, block, index):
    if isinstance(values, (tuple, list)):
        places = (0, 0)
    else:
        values, places = (values, values), (0, 1)
    specs = [
        pl.BlockSpec(block, lambda i, place=place: (place, index), pipeline_mode=pl.Buffered(1))
        for place in places
    ]
    return list(values), specs


def sign(token_ref):
    token_ref[...] = jnp.zeros(token_ref.shape, token_ref.dtype)


TOKEN = (8, LANES)


def product_sum(lefts, rights):
    parts = [contract_rows(left[...], right[...]) for left, right in zip(lefts, rights)]
    return parts[0] + parts[1]


def gate_up_grad_kernel(x0, x1, x2, x3, d0, d1, d2, d3, *refs):
    gate_ref, up_ref, token_ref = refs[-3:]
    each = gate_ref.shape[2]
    total = product_sum((x0, x1), (d0, d1)) + product_sum((x2, x3), (d2, d3))
    gate_ref[0] = total[:, :each]
    up_ref[0] = total[:, each:]
    sign(token_ref)


def gate_up_grad(expert, count, totals, own, other, own_hidden, other_hidden):
    half, width = own[0].shape
    each = own_hidden.shape[1] // 2 // count
    wide = 2 * ROW_BLOCK
    part = pl.BlockSpec((1, wide, each), lambda i: (expert, i, 0))
    rights, specs = in_halves(own_hidden, (half, 2 * each), expert)
    single = pl.Buffered(1)
    return call(
        gate_up_grad_kernel,
        11.7,
        grid=(width // wide,),
        in_specs=[pl.BlockSpec((half, wide), lambda i: (0, i))] * 4
        + specs
        + [pl.BlockSpec((half, 2 * each), lambda i: (0, expert), pipeline_mode=single)] * 2
        + [pl.BlockSpec(memory_space=pl.ANY)] * len(totals),
        out_specs=[part] * 2 + [pl.BlockSpec(TOKEN, lambda i: (0, 0))],
        out_shape=[jax.ShapeDtypeStruct((count, width, each), F32)] * 2
        + [jax.ShapeDtypeStruct(TOKEN, F32)],
        input_output_aliases={8: 0, 9: 1} if totals else {},
    )(*own, *other, *rights, *other_hidden, *totals)


def down_grad_kernel(count, w0, w1, g0, g1, g2, g3, w2, w3, *refs):
    out_ref, token_ref = refs[-2:]
    each = out_ref.shape[1]
    total = product_sum((w0, w1), (g0, g1)) + product_sum((w2, w3), (g2, g3))
    for i in range(count):
        out_ref[i] = total[i * each : (i + 1) * each, :]
    sign(token_ref)


def down_grad(part, parts, count, totals, own_weighted, other_weighted, own, other):
    half, width = own[0].shape[0], own[0].shape[1] - LANES
    hidden = own_weighted.shape[1]
    each = hidden // count
    wide = 2 * ROW_BLOCK
    steps = width // wide // parts
    right = pl.BlockSpec((half, wide), lambda i: (0, part * steps + i))
    place = pl.BlockSpec((count, each, wide), lambda i: (0, 0, part * steps + i))
    lefts, specs = in_halves(own_weighted, (half, hidden), 0)
    single = pl.Buffered(1)
    return call(
        functools.partial(down_grad_kernel, count),
        9.7,
        grid=(steps,),
        in_specs=specs
        + [right] * 4
        + [pl.BlockSpec((half, hidden), lambda i: (0, 0), pipeline_mode=single)] * 2
        + [pl.BlockSpec(memory_space=pl.ANY)] * len(totals),
        out_specs=[place, pl.BlockSpec(TOKEN, lambda i: (0, 0))],
        out_shape=[
            jax.ShapeDtypeStruct((count, each, width), F32),
            jax.ShapeDtypeStruct(TOKEN, F32),
        ],
        input_output_aliases={8: 0} if totals else {},
    )(*lefts, *own, *other, *other_weighted, *totals)


def place_wide_kernel(owners_ref, *refs):
    blocks, (last_top, last_low), out_ref = refs[:-3], refs[-3:-1], refs[-1]
    cols = blocks[0].shape[1]

    def put(slot, ref):
        at = pl.multiple_of(owners_ref[slot] * cols, cols)
        out_ref[:, pl.ds(at, cols)] = ref[...].astype(F32)

    for slot, ref in enumerate(blocks):
        put(slot, ref)
    top = pl.program_id(0) < pl.num_programs(0) // 2

    @pl.when(top)
    def _():
        put(len(blocks), last_top)

    @pl.when(jnp.logical_not(top))
    def _():
        put(len(blocks), last_low)


def place_wide(owners_by_slot, blocks, width):
    share, cols = blocks[0].shape
    steps = share // ROW_BLOCK
    half = steps // 2
    return call(
        place_wide_kernel,
        4,
        grid=(steps,),
        in_specs=[smem_spec()]
        + [pl.BlockSpec((ROW_BLOCK, cols), lambda i: (i, 0))] * (len(blocks) - 2)
        + [
            pl.BlockSpec((ROW_BLOCK, cols), lambda i: (jnp.minimum(i, half - 1), 0)),
            pl.BlockSpec((ROW_BLOCK, cols), lambda i: (jnp.maximum(i - half, 0), 0)),
        ],
        out_specs=pl.BlockSpec((ROW_BLOCK, width), lambda i: (i, 0)),
        out_shape=jax.ShapeDtypeStruct((share, width), F32),
    )(owners_by_slot, *blocks)


def place_kernel(sharers, owners_ref, *refs):
    count = (len(refs) - 3) // 2
    blocks, lows, (q_ref, k_ref, v_ref) = refs[:count], refs[count:-3], refs[-3:]
    cols = blocks[0].shape[1]
    dim = cols // 2
    for i, ref in enumerate(blocks):
        at = pl.multiple_of(owners_ref[i] * cols, cols)
        q_ref[:, pl.ds(at, cols)] = ref[...].astype(F32)

    @pl.when(pl.program_id(0) == 0)
    def _():
        for i, ref in enumerate(lows):
            rows = ref.shape[0]
            down = pl.multiple_of(owners_ref[i] % sharers * rows, rows)
            right = pl.multiple_of(owners_ref[i] // sharers * dim, dim)
            k_ref[pl.ds(down, rows), pl.ds(right, dim)] = ref[:, :dim].astype(F32)
            v_ref[pl.ds(down, rows), pl.ds(right, dim)] = ref[:, dim:].astype(F32)


def place_blocks(owners_by_slot, blocks, shapes, sharers):
    share, width = shapes[0]
    cols = blocks[0].shape[1]
    rows = blocks[0].shape[0] - share
    return call(
        functools.partial(place_kernel, sharers),
        5,
        grid=(share // ROW_BLOCK,),
        in_specs=[smem_spec()]
        + [pl.BlockSpec((ROW_BLOCK, cols), lambda i: (i, 0))] * len(blocks)
        + [pl.BlockSpec((rows, cols), lambda i: (share // rows, 0))] * len(blocks),
        out_specs=[
            pl.BlockSpec((ROW_BLOCK, width), lambda i: (i, 0)),
            pl.BlockSpec(shapes[1], lambda i: (0, 0)),
            pl.BlockSpec(shapes[2], lambda i: (0, 0)),
        ],
        out_shape=[jax.ShapeDtypeStruct(shape, F32) for shape in shapes],
    )(owners_by_slot, *blocks, *blocks)


def place_last_kernel(share, owner_ref, top_in, low_in, q_any, k_any, v_any, q_ref, k_ref, v_ref):
    dim = k_ref.shape[1]
    cut = top_in.shape[0]
    q_ref[:cut, :] = top_in[...].astype(F32)
    q_ref[cut:, :] = low_in[: share - cut, :].astype(F32)
    k_ref[...] = low_in[share - cut :, :dim].astype(F32)
    v_ref[...] = low_in[share - cut :, dim:].astype(F32)


def place_last(owner, halves, totals, sharers):
    share = totals[0].shape[0]
    top, low = halves
    cols = top.shape[1]
    rows = top.shape[0] + low.shape[0] - share
    spots = pl.BlockSpec((rows, cols // 2), lambda i, o: (o[0] % sharers, o[0] // sharers))
    return call(
        functools.partial(place_last_kernel, share),
        3,
        grid_spec=pltpu.PrefetchScalarGridSpec(
            num_scalar_prefetch=1,
            grid=(1,),
            in_specs=[
                pl.BlockSpec(top.shape, lambda i, o: (0, 0)),
                pl.BlockSpec(low.shape, lambda i, o: (0, 0)),
            ]
            + [pl.BlockSpec(memory_space=pl.ANY)] * 3,
            out_specs=[pl.BlockSpec((share, cols), lambda i, o: (0, o[0])), spots, spots],
        ),
        out_shape=[jax.ShapeDtypeStruct(total.shape, F32) for total in totals],
        input_output_aliases={3: 0, 4: 1, 5: 2},
    )(owner.reshape(1), top, low, *totals)


def body(
    tokens,
    routes,
    places,
    piece_starts,
    attn_gain,
    query_proj,
    key_matrix,
    value_matrix,
    out_proj,
    query_gain,
    key_gain,
    ffn_gain,
    router,
    gate_proj,
    up_proj,
    down_proj,
    out_grad,
):
    ring = Ring()
    local_rows, width = tokens.shape
    head_dim = query_gain.shape[0]
    owners, groups = ring.owners, ring.groups
    heads_tp = query_proj.shape[1] // head_dim
    kv_tp = key_matrix.shape[1] // head_dim
    heads_here = heads_tp // owners
    heads_each_key = heads_tp // kv_tp
    sharers = heads_each_key // heads_here
    experts_here, _, each = gate_proj.shape
    expert_count = experts_here * owners
    picks = routes.shape[1]
    seq_len = local_rows * owners
    half_rows = local_rows // 2
    scale = head_dim ** (-0.5)
    e, f, t = ring.index, ring.group, ring.half
    key_head = (e * heads_here) // heads_each_key
    shared_index = e % sharers

    pair = groups == 2
    q_cols = heads_here * head_dim
    down = down_proj.reshape(experts_here * each, width)
    first = jnp.stack([e * experts_here, t * expert_count]).astype(jnp.int32)

    def attention_tables(places, piece_starts):
        group_places = lax.dynamic_slice_in_dim(places, f * seq_len, seq_len)
        by_slot = jnp.take(group_places.reshape(owners, 2, half_rows), ring.owners_by_slot, axis=0)
        order_places = jnp.concatenate(
            [
                lax.dynamic_index_in_dim(by_slot, t, 1, keepdims=False).reshape(-1),
                lax.dynamic_index_in_dim(by_slot, 1 - t, 1, keepdims=False).reshape(-1),
            ]
        )
        position = order_places % seq_len
        begins = lax.dynamic_slice_in_dim(piece_starts, f, 1)
        inside = (begins <= position[:, None]) & (position[:, None] < begins + PIECE)
        limit = jnp.maximum(
            position, jnp.max(jnp.where(inside, begins + (PIECE - 1), 0), axis=1)
        )
        half_dim = head_dim // 2
        freqs = jnp.exp(jnp.arange(half_dim, dtype=F32) * (-2.0 * LOG_THETA / head_dim))
        angles = position.astype(F32)[:, None] * freqs[None, :]
        cosine, sine = jnp.cos(angles), jnp.sin(angles)
        return (
            jnp.concatenate([cosine, cosine], axis=1),
            jnp.concatenate([-sine, sine], axis=1),
            query_gain[None, :],
            key_gain[None, :],
            position[None, :],
            limit[:, None],
        )

    grads_own = ring.own_rows(out_grad)
    payload = jnp.concatenate([grads_own, pad_lanes(ring.own_rows(routes).astype(BF16))], axis=1)
    stream = ring.own_rows(tokens).astype(F32)
    first_inverse = inverse_norm(stream)
    normed = stream * first_inverse
    made = {}

    def first_hook(step, walk):
        done = []
        if step == 0:
            made["cut"] = cut_weights(
                e, key_head, query_proj, key_matrix, value_matrix, out_proj, q_cols, head_dim
            )
            made["chunks"] = []
            if not pair:
                made["weights"] = (lax.all_gather(made["cut"], "fsdp", axis=0, tiled=True),)
        if pair:
            rows = made["cut"].shape[0] // ring.ahead
            chunk = made["cut"][step * rows : (step + 1) * rows]
            if step:
                chunk = after(chunk, walk.ahead)
            made["chunks"].append(ring.swap_groups(chunk))
            done.append(made["chunks"][-1])
        grads_walk.step(walk.ahead if step else None)
        done.append(grads_walk.ahead)
        if step == 1:
            made["tables"] = attention_tables(*after((places, piece_starts), walk.ahead))
            done += made["tables"][:4]
        if step == 2:
            done += made["tables"][4:]
        return tuple(done)

    grads_walk = ring.walk(payload)
    attn_in, _ = ring.gather((normed * attn_gain).astype(BF16), first_hook)
    if pair:
        made["weights"] = (made["cut"], jnp.concatenate(made["chunks"], axis=0))
    tables, weights = made["tables"], made["weights"]
    at = jnp.stack([f, 1 - f] if pair else [jnp.zeros_like(f)]).astype(jnp.int32)
    raw, query_low, key_low, value_low = project(at, attn_in, weights, heads_here, *tables[:4])
    low = (query_low, key_low, value_low)
    attn_other, lse_other, part_other = attend(at, 1, weights, *tables[4:], *low)
    attn_mine, lse_mine, part_mine = attend(at, 0, weights, *tables[4:], *low)
    grads_found = grads_walk.found
    grads_mine = jnp.concatenate(grads_found, axis=0)
    grads = (grads_mine, ring.swap_halves(grads_mine))
    their_rows = []

    def across(signal):
        if not pair:
            return []
        rows = ffn_in[0].shape[0] // ring.ahead
        start = len(their_rows) * rows
        their_rows.append(ring.swap_groups(after(ffn_in[0], signal)[start : start + rows]))
        return their_rows[-1:]

    def branch_hook(step, signal):
        if step != 1:
            return None
        made["router"] = ring.whole_rows(after(router, signal))
        made["lanes"] = pad_lanes(made["router"])
        return made["lanes"]

    residual = stream + ring.scatter(part_mine, part_other, branch_hook)
    whole_router, router_lanes = made["router"], made["lanes"]

    second_inverse = inverse_norm(residual)
    mid_normed = residual * second_inverse
    ffn_in, _ = ring.gather((mid_normed * ffn_gain).astype(BF16))
    if pair:
        their_grads = ring.swap_groups(grads_mine)
    weighted, hidden, gates, back_mine, back_other = experts(
        first, ffn_in, grads, gate_proj, up_proj, down_proj, router_lanes, picks, expert_count
    )

    if pair:
        made["grads"], back_mine = after((their_grads, back_mine), their_grads)
    layer_parts = []

    def back_hook(step, signal):
        layer_parts.append(layer_part(step, ring.ahead, after(weighted, signal), down))
        if step == 1 and pair:
            made["routed"] = (made["grads"], ring.swap_halves(made["grads"]))
        earlier = their_rows[-1:]
        across(signal)
        return tuple([layer_parts[-1]] + earlier)

    back_sum = ring.scatter(back_mine, back_other, back_hook)

    gate_grad_rows = sum(
        back_sum[:, width + i * expert_count : width + (i + 1) * expert_count] for i in range(4)
    )
    own_gates = gates[:half_rows, :expert_count]
    picked_grad = own_gates * (
        gate_grad_rows - jnp.sum(own_gates * gate_grad_rows, axis=-1, keepdims=True)
    )
    logit_grad = picked_grad.astype(BF16)
    ffn_in_grad = back_sum[:, :width] + contract_cols(logit_grad, whole_router)
    ffn_gain_part = jnp.sum(ffn_in_grad * mid_normed, axis=0)
    second_normed_grad = ffn_in_grad * ffn_gain
    mid_grad = grads_own.astype(F32) + second_inverse * (
        second_normed_grad
        - mid_normed * jnp.mean(second_normed_grad * mid_normed, axis=-1, keepdims=True)
    )
    made["theirs"], made["other"] = [], []

    def other_hook(step, walk):
        done = []
        if step == 0:
            middle = len(layer_parts) // 2
            halves = [
                jnp.concatenate(part, axis=0) for part in (layer_parts[:middle], layer_parts[middle:])
            ]
            made["layer"] = Fold(ring, *after(halves, walk.ahead))
        else:
            made["layer"].step(walk.ahead)
        done.append(made["layer"].ahead)
        if pair and step == 1:
            rows = jnp.concatenate(after(their_rows, walk.ahead), axis=0)
            made["theirs"] = [rows, ring.swap_halves(rows)]
            done += made["theirs"]
        if pair and step >= ring.ahead - 2:
            half = step - (ring.ahead - 2)
            x, g = after((made["theirs"][half], made["routed"][half]), walk.ahead)
            made["other"].append(
                other_experts(first, x, g, gate_proj, up_proj, down_proj, router_lanes, picks)
            )
            done += made["other"][-1]
        return tuple(done)

    branch, _ = ring.gather(
        jnp.concatenate([mid_grad.astype(BF16), pad_lanes(logit_grad)], axis=1), other_hook
    )

    attn_halves = (attn_mine, attn_other)
    out_theirs, out_arrived = ring.send_share(branch, attn_halves, width, BF16)
    raw_mine, raw_other, head_gains, in_mine, in_other = attend_back(
        at,
        branch if out_theirs is None else after(branch, out_theirs),
        weights,
        *tables,
        (raw, query_low, key_low, value_low, lse_mine, lse_other),
    )
    raw_halves = (raw_mine, raw_other)
    qkv_theirs, qkv_arrived = ring.send_share(attn_in, raw_halves, width, BF16)

    totals = {"gate_up": [], "down": []}

    def last_piece(n, signal):
        if n < experts_here:
            *totals["gate_up"], token = gate_up_grad(
                n,
                experts_here,
                totals["gate_up"],
                after(ffn_in, signal),
                made["theirs"],
                hidden,
                [part[1] for part in made["other"]],
            )
        else:
            *totals["down"], token = down_grad(
                n - experts_here,
                2,
                experts_here,
                totals["down"],
                after(weighted, signal),
                [part[0] for part in made["other"]],
                grads,
                made["routed"],
            )
        return [token]

    def in_hook(step, signal):
        done = []
        if step == 0:
            made["layer"].step(signal)
            done.append(made["layer"].ahead)
            share = ring.add_share(out_arrived, after(branch, signal), attn_halves, width)
            made["out_walk"] = ring.walk(share.astype(BF16), True)
        else:
            made["out_walk"].step(signal)
        done.append(made["out_walk"].found[-1])
        if step == 1:
            made["qkv"] = ring.add_share(qkv_arrived, after(attn_in, signal), raw_halves, width)
            done.append(made["qkv"])
        if pair and step < 3:
            done += last_piece(step, signal)
        return tuple(done)

    if qkv_theirs is not None:
        in_mine = after(in_mine, qkv_theirs)
    attn_in_grad = ring.scatter(in_mine, in_other, in_hook)
    layer_out = ring.join_halves((residual + made["layer"].result()).astype(BF16))
    qkv_share = made["qkv"]
    first_normed_grad = attn_in_grad * attn_gain
    tokens_grad = mid_grad + first_inverse * (
        first_normed_grad - normed * jnp.mean(first_normed_grad * normed, axis=-1, keepdims=True)
    )
    tokens_grad = ring.join_halves(tokens_grad)
    attn_gain_part = jnp.sum(attn_in_grad * normed, axis=0)
    gains = ring.sum_all(
        jnp.concatenate([attn_gain_part, ffn_gain_part, head_gains[0], head_gains[1]])
    )

    kv_share = qkv_share[:, q_cols:]
    step = sharers // 2
    while step:
        rows = kv_share.shape[0] // 2
        bit = (shared_index // step) % 2
        pairs = [(i, i ^ step) for i in range(owners)]
        sent = lax.dynamic_slice_in_dim(kv_share, (1 - bit) * rows, rows)
        kept = lax.dynamic_slice_in_dim(kv_share, bit * rows, rows)
        kv_share = kept + ring.send(sent.astype(BF16), pairs).astype(F32)
        step //= 2
    own_share = jnp.concatenate([qkv_share[:, :q_cols], kv_share], axis=0).astype(BF16)
    own_share = after(own_share, made["out_walk"].found[-1])

    last = ring.ahead - 1
    lanes_at = width // LANES

    share_rows = qkv_share.shape[0]
    shapes = [(share_rows, heads_tp * head_dim)] + [(share_rows, kv_tp * head_dim)] * 2

    def weight_hook(step, walk):
        signal = walk.ahead
        done = []
        if step == 0:
            made["out_walk"].step(signal)
            done += made["out_walk"].found[-1]
        if pair and step < 2:
            done += last_piece(step + 3, signal)
        if step == 1:
            _, arrived = ring.send_share(after(ffn_in, signal), branch, width, F32, LANES, lanes_at)
            made["router_arrived"] = arrived
            done += [] if arrived is None else [arrived]
        if step == 2:
            made["router_grad"] = ring.add_share(
                made["router_arrived"], after(ffn_in, signal), branch, width, LANES, lanes_at
            )
            done.append(made["router_grad"])
        if step == 2:
            found = made["out_walk"].found
            made["out_grad"] = place_wide(
                ring.owners_by_slot,
                [after(found[0], signal)] + found[1:-1] + list(found[-1]),
                heads_tp * head_dim,
            )
            done.append(made["out_grad"])
        if step == last:
            found = walk.found
            made["placed"] = place_blocks(
                ring.owners_by_slot, [after(found[0], signal)] + found[1:], shapes, sharers
            )
            done += made["placed"]
        return tuple(done)

    found = ring.blocks(own_share, weight_hook, True)
    out_grad_w = made["out_grad"]
    query_grad_w, key_grad_w, value_grad_w = place_last(
        ring.owners_by_slot[owners - 1], found[-1], made["placed"], sharers
    )
    router_grad = made["router_grad"][:, :expert_count]

    if pair:
        gate_total, up_total = totals["gate_up"]
        (down_total,) = totals["down"]
    else:
        all_rows, all_grads = ring.all_groups(ffn_in[0]), ring.all_groups(grads[0])

        def add_group(n, sums):
            gate_up, low = 0.0, 0.0
            for x, g in zip(all_rows, all_grads, strict=True):
                w, h = other_experts(
                    first, x[n], g[n], gate_proj, up_proj, down_proj, router_lanes, picks
                )
                gate_up = gate_up + contract_rows(x[n], h)
                low = low + contract_rows(w, g[n])[:, :width]
            gate_up = gate_up.reshape(width, experts_here, 2, each)
            return (
                sums[0] + jnp.swapaxes(gate_up[:, :, 0], 0, 1),
                sums[1] + jnp.swapaxes(gate_up[:, :, 1], 0, 1),
                sums[2] + low.reshape(experts_here, each, width),
            )

        gate_total, up_total, down_total = lax.fori_loop(
            0,
            groups,
            add_group,
            tuple(jnp.zeros(w.shape, F32) for w in (gate_proj, up_proj, down_proj)),
        )
    return (
        layer_out,
        tokens_grad,
        gains[:width],
        query_grad_w,
        key_grad_w,
        value_grad_w,
        out_grad_w,
        gains[2 * width : 2 * width + head_dim],
        gains[2 * width + head_dim :],
        gains[width : 2 * width],
        router_grad,
        gate_total,
        up_total,
        down_total,
    )


def solution(mesh):
    return jax.shard_map(
        body,
        mesh=mesh,
        in_specs=(
            P(("fsdp", "ep"), None),
            P(("fsdp", "ep"), None),
            P(),
            P(),
            P(),
            P("fsdp", "tp"),
            P("fsdp", "tp"),
            P("fsdp", "tp"),
            P("fsdp", "tp"),
            P(),
            P(),
            P(),
            P("fsdp", None),
            P("ep", None, "tp"),
            P("ep", None, "tp"),
            P("ep", "tp", None),
            P(("fsdp", "ep"), None),
        ),
        out_specs=(
            P(("fsdp", "ep"), None),
            P(("fsdp", "ep"), None),
            P(),
            P("fsdp", "tp"),
            P("fsdp", "tp"),
            P("fsdp", "tp"),
            P("fsdp", "tp"),
            P(),
            P(),
            P(),
            P("fsdp", None),
            P("ep", None, "tp"),
            P("ep", None, "tp"),
            P("ep", "tp", None),
        ),
        check_vma=False,
    )
```
